256 devices in a mesh: visit: 8 (over z), prow: 4 (over y), pcol: 8 (over x, core).
Axes of the slice: x: 4, y: 4, z: 8, core: 2. Of those that a mesh axis runs over, the one named last changes fastest.
Arguments:
- stamps: float32 [2048, 36864], P(('visit', 'prow', 'pcol')), may hold values from -8 to 8
- variance: float32 [2048, 128, 128], P(('visit', 'prow', 'pcol')), may hold values from 0.5 to 8
- coefficients: float32 [2048, 9], P(('visit', 'prow', 'pcol')), may hold values from -2 to 2
- band_offsets: int32 [2048, 2], P(('visit', 'prow', 'pcol')), may hold values from 2 to 31
- shifts: float32 [2048, 2], P(('visit', 'prow', 'pcol')), may hold values from 0 to 1
- destination: int32 [2048], P(('visit', 'prow', 'pcol')), may hold values from 0 to 31, as said below
- position: int32 [2048], P(('visit', 'prow', 'pcol')), may hold values from 0 to 15
- psf_taps: float32 [17], replicated, may hold values from 0.1 to 1
Outputs:
- coadd: float32 [2048, 4096], P('prow', 'pcol')
- detection: float32 [2048, 4096], P('prow', 'pcol')
The draws below stay inside these ranges and needn't reach their ends.
Inputs may be any that keep to these rules, and one draw needn't show every extreme that they name: `destination`: each device's blocks name patches 0 .. 31; no device sends more than 2 of its blocks to one patch, and in every visit group one patch receives exactly 2 blocks from every device of that group.
All inputs are finite; a program needn't handle non-finite values.
Results may differ from the reference program's by a relative error of at most 0.0003.
Values sent between devices are 32-bit elements; how exact they have to be, the bound alone decides.
A program may use at most 64 MiB of HBM per device.

```python
import math
import jax
import jax.numpy as jnp
from jax import lax

NB = 8
S = 192
B = 128
KR = 15
NBASIS = 9
PB = 4
RF = 8
MATCHED = 162
PCOLS = 8
PROWS = 4
OWNERS = 32
CAP = 2
GROUPS = 8
BLOCKS = 2048
TROWS = 2048
TCOLS = 4096


def draw_destination(key, part):
    devices = BLOCKS // NB
    others = (OWNERS - 1) * CAP

    def one_device(device):
        group_index = device // OWNERS
        hot_owner = jax.random.randint(jax.random.fold_in(jax.random.fold_in(key, 101), group_index), (), 0, OWNERS)
        device_key = jax.random.fold_in(jax.random.fold_in(key, 202), device)
        ordering = jax.random.permutation(device_key, others)
        spread = ordering[:NB - CAP] // CAP
        spread = spread + (spread >= hot_owner).astype(jnp.int32)
        chosen = jnp.concatenate([jnp.full((CAP,), hot_owner, dtype=jnp.int32), spread.astype(jnp.int32)])
        shuffle = jax.random.permutation(jax.random.fold_in(device_key, 303), NB)
        return chosen[shuffle]
    return jax.vmap(one_device)(jnp.arange(devices, dtype=jnp.int32)).reshape(BLOCKS)


def plant(values, own_key, least, top_value):
    spot = [jax.random.randint(jax.random.fold_in(own_key, axis), (), 0, length) for axis, length in enumerate(values.shape)]
    main_axis = values.shape.index(max(values.shape))
    neighbour = spot[:main_axis] + [(spot[main_axis] + 1) % values.shape[main_axis]] + spot[main_axis + 1:]
    return values.at[tuple(spot)].set(least).at[tuple(neighbour)].set(top_value)


def block_scale(own_key, shape, cuts, smallest, top_value):
    def one(dim, blocks):
        draws = jax.random.uniform(jax.random.fold_in(jax.random.fold_in(own_key, 6), dim), (blocks,), jnp.float32, smallest / len(cuts), top_value / len(cuts))
        return jnp.repeat(jnp.exp(draws), shape[dim] // blocks).reshape((-1,) + (1,) * (len(shape) - dim - 1))

    loudness = one(*cuts[0])
    for cut in cuts[1:]:
        loudness = loudness * one(*cut)
    return loudness


def bell_draw(key, extent, deviation, most, cuts=(), kind=jnp.bfloat16):
    gain = block_scale(key, extent, cuts, -0.22, 0.18) if cuts else 1.0
    values = jax.random.normal(key, extent, jnp.float32) * deviation * gain
    return jnp.minimum(jnp.maximum(values, -most), most).astype(kind)


def setup_inputs(seed: int = 0) -> dict:
    keys = jax.random.split(jax.random.key(seed), 9)
    return {
        "stamps": bell_draw(keys[0], (BLOCKS, S * S), 1.0, 8.0, ((0, 256),), jnp.float32),
        "variance": jnp.clip(jnp.exp(math.log(8.0) - 2.7725887 * jax.random.uniform(keys[1], (BLOCKS, B, B), jnp.float32) ** block_scale(keys[1], (BLOCKS, B, B), ((0, 256),), -0.2, 0.2)), 0.5, 8.0),
        "coefficients": bell_draw(keys[2], (BLOCKS, NBASIS), 0.4, 2.0, ((0, 256),), jnp.float32),
        "band_offsets": plant(jax.random.randint(keys[3], (BLOCKS, 2), 2, MATCHED - B - 2), jax.random.fold_in(keys[3], 1), 2, (MATCHED - B - 2) - 1).astype(jnp.int32),
        "shifts": jnp.clip(1.0 * jax.random.uniform(keys[4], (BLOCKS, 2), jnp.float32) ** block_scale(keys[4], (BLOCKS, 2), ((0, 256),), -0.2, 0.2), 0.0, 1.0),
        "destination": draw_destination(jax.random.fold_in(keys[8], 71), 0),
        "position": plant(jax.random.randint(keys[6], (BLOCKS,), 0, PB * PB), jax.random.fold_in(keys[6], 1), 0, (PB * PB) - 1).astype(jnp.int32),
        "psf_taps": jnp.clip(jnp.exp(jax.random.uniform(keys[7], (2 * RF + 1,), jnp.float32, math.log(0.1), math.log(1.0))), 0.1, 1.0),
    }


basis_widths = (1.0, 2.0, 4.0)

def factor_tables(span, radius):
    matched_len = span - 2 * radius
    row_index = jnp.arange(matched_len, dtype=jnp.int32)[:, None]
    col_index = jnp.arange(span, dtype=jnp.int32)[None, :]
    lag_index = col_index - row_index - radius
    inside = (jnp.abs(lag_index) <= radius).astype(jnp.float32)
    lagged = lag_index.astype(jnp.float32)
    offsets = jnp.arange(-radius, radius + 1, dtype=jnp.int32).astype(jnp.float32)
    result = []
    for width in basis_widths:
        scaled = offsets / width
        gauss_norm = jnp.sqrt(jnp.sum(jnp.exp(-scaled * scaled)))
        quad_norm = jnp.sqrt(jnp.sum(scaled ** 4 * jnp.exp(-scaled * scaled)))
        ratio = lagged / width
        bell = jnp.exp(-0.5 * ratio * ratio) * inside
        result.append(jnp.stack([bell / gauss_norm, ratio * ratio * bell / quad_norm]))
    return jnp.stack(result)

def lanczos_bands(offsets, fractions, out_len, in_len):
    row_index = jnp.arange(out_len, dtype=jnp.int32)[None, :, None]
    col_index = jnp.arange(in_len, dtype=jnp.int32)[None, None, :]
    start = offsets.astype(jnp.int32)[:, None, None]
    distance = (col_index - row_index - start).astype(jnp.float32) - fractions[:, None, None]
    return jnp.where(jnp.abs(distance) < 3.0, jnp.sinc(distance) * jnp.sinc(distance / 3.0), 0.0)

def warp_blocks(stamps, coefficients, band_offsets, shifts, tables, side):
    highest = lax.Precision.HIGHEST
    count = stamps.shape[0]
    matched_len = tables.shape[2]
    matched = jnp.zeros((count, matched_len, matched_len), jnp.float32)
    for width_index in range(len(basis_widths)):
        bell = tables[width_index, 0]
        quad = tables[width_index, 1]
        rows_bell = jnp.einsum('ms,bst->bmt', bell, stamps, precision=highest, preferred_element_type=jnp.float32)
        rows_quad = jnp.einsum('ms,bst->bmt', quad, stamps, precision=highest, preferred_element_type=jnp.float32)
        first = coefficients[:, 3 * width_index][:, None, None]
        second = coefficients[:, 3 * width_index + 1][:, None, None]
        third = coefficients[:, 3 * width_index + 2][:, None, None]
        left = first * rows_bell + second * rows_quad
        matched = matched + jnp.einsum('bmt,nt->bmn', left, bell, precision=highest, preferred_element_type=jnp.float32)
        matched = matched + third * jnp.einsum('bmt,nt->bmn', rows_bell, quad, precision=highest, preferred_element_type=jnp.float32)
    band_rows = lanczos_bands(band_offsets[:, 0], shifts[:, 0], side, matched_len)
    band_cols = lanczos_bands(band_offsets[:, 1], shifts[:, 1], side, matched_len)
    halfway = jnp.einsum('bim,bmn->bin', band_rows, matched, precision=highest, preferred_element_type=jnp.float32)
    return jnp.einsum('bin,bjn->bij', halfway, band_cols, precision=highest, preferred_element_type=jnp.float32)

def filter_band(taps, length, radius):
    row_index = jnp.arange(length, dtype=jnp.int32)[:, None]
    col_index = jnp.arange(length + 2 * radius, dtype=jnp.int32)[None, :]
    lag_index = col_index - row_index
    band = jnp.zeros((length, length + 2 * radius), jnp.float32)
    for tap_index in range(2 * radius + 1):
        band = band + jnp.where(lag_index == tap_index, taps[tap_index], 0.0)
    return band

def reference(stamps, variance, coefficients, band_offsets, shifts, destination, position, psf_taps):
    highest = lax.Precision.HIGHEST
    per_group = NB * OWNERS
    tables = factor_tables(S, KR)
    pieces = (stamps.reshape(GROUPS, per_group, S, S), variance.reshape(GROUPS, per_group, B, B), coefficients.reshape(GROUPS, per_group, NBASIS), band_offsets.reshape(GROUPS, per_group, 2), shifts.reshape(GROUPS, per_group, 2), destination.reshape(GROUPS, per_group), position.reshape(GROUPS, per_group))

    def one_group(carry, group_pieces):
        group_stamps, group_var, group_coef, group_off, group_shift, group_dest, group_pos = group_pieces
        warped = warp_blocks(group_stamps, group_coef, group_off, group_shift, tables, B)
        weight = 1.0 / group_var
        terms = jnp.stack([weight * warped, weight], axis=1)
        tile_index = (group_dest * (PB * PB) + group_pos).astype(jnp.int32)
        summed = jax.ops.segment_sum(terms, tile_index, num_segments=OWNERS * PB * PB)
        return (carry + summed, None)
    start = jnp.zeros((OWNERS * PB * PB, 2, B, B), jnp.float32)
    tile_sums, _ = lax.scan(one_group, start, pieces)
    grid = tile_sums.reshape(PROWS, PCOLS, PB, PB, 2, B, B).transpose(4, 0, 2, 5, 1, 3, 6).reshape(2, TROWS, TCOLS)
    coadd = grid[0] / (1.0 + grid[1])
    padded = jnp.pad(coadd, RF)
    row_band = filter_band(psf_taps, TROWS, RF)
    col_band = filter_band(psf_taps, TCOLS, RF)
    across = jnp.dot(row_band, padded, precision=highest, preferred_element_type=jnp.float32)
    detection = jnp.dot(across, col_band.T, precision=highest, preferred_element_type=jnp.float32)
    return (coadd, detection)
```

```python
import math

import jax
import jax.numpy as jnp
from jax import lax
from jax.experimental import pallas as pl
from jax.experimental.pallas import tpu as pltpu
from jax.sharding import PartitionSpec as P

MESH = pl.DeviceIdType.MESH
NB = 8
S = 192
B = 128
KR = 15
RF = 8
NZ = 8
NY = 4
NP = 8
NPLANE = NY * NP
TILES = 512
LANES = 128
WIDTHS = (1.0, 2.0, 4.0)
TAPS = (-2, -1, 0, 1, 2, 3)
CHUNK = 264
FIRST = 128
BF = jnp.bfloat16
F32 = jnp.float32


def norms(width):
    lags = range(-KR, KR + 1)
    bell = math.sqrt(sum(math.exp(-((t / width) ** 2)) for t in lags))
    quad = math.sqrt(sum((t / width) ** 4 * math.exp(-((t / width) ** 2)) for t in lags))
    return bell, quad


def split(x):
    hi = x.astype(BF)
    return hi, (x - hi.astype(F32)).astype(BF)


def mm(a, b):
    return jnp.dot(a, b, preferred_element_type=F32)


def sinc(x):
    scaled = math.pi * x
    return jnp.where(x == 0.0, 1.0, jnp.sin(scaled) / jnp.where(x == 0.0, 1.0, scaled))


def lanczos_weights(shift):
    lane = lax.broadcasted_iota(jnp.int32, (NB, LANES), 1).astype(F32)
    x = lane + float(TAPS[0]) - shift
    return jnp.where(jnp.abs(x) < 3.0, sinc(x) * sinc(x / 3.0), 0.0)


def factor_rows(place, weights):
    bells = [jnp.zeros((NB, LANES), F32) for _ in WIDTHS]
    quads = [jnp.zeros((NB, LANES), F32) for _ in WIDTHS]
    for index, tap in enumerate(TAPS):
        lag = place - float(tap + KR)
        weight = jnp.where(jnp.abs(lag) <= float(KR), weights[:, index : index + 1], 0.0)
        for w, width in enumerate(WIDTHS):
            bell_norm, quad_norm = norms(width)
            ratio = lag * (1.0 / width)
            term = weight * jnp.exp(-0.5 * ratio * ratio)
            bells[w] = bells[w] + term * (1.0 / bell_norm)
            quads[w] = quads[w] + ratio * ratio * term * (1.0 / quad_norm)
    return bells, quads


def make_bases(coef_ref, off_ref, shift_ref, base_ref):
    offsets = off_ref[...].astype(F32)
    shifts = shift_ref[...]
    coef = coef_ref[...]
    lane_int = lax.broadcasted_iota(jnp.int32, (NB, LANES), 1)
    lane = lane_int.astype(F32)
    col_weights = lanczos_weights(shifts[:, 1:2])
    row_weights = lanczos_weights(shifts[:, 0:1])
    place = jnp.where(lane_int == 0, 0.0, float(LANES) - lane)
    bells, quads = factor_rows(place - offsets[:, 1:2], col_weights)
    for w in range(3):
        base_ref[2 * w] = bells[w]
        base_ref[2 * w + 1] = quads[w]
    for d, delta in enumerate((0.0, -1.0, 1.0)):
        bells, quads = factor_rows(2.0 * lane + delta - offsets[:, 0:1], row_weights)
        for w in range(3):
            first = coef[:, 3 * w : 3 * w + 1]
            second = coef[:, 3 * w + 1 : 3 * w + 2]
            third = coef[:, 3 * w + 2 : 3 * w + 3]
            base_ref[6 + 6 * d + 2 * w] = first * bells[w] + second * quads[w]
            base_ref[6 + 6 * d + 2 * w + 1] = third * bells[w]


def skew(row, count):
    return pltpu.roll(jnp.broadcast_to(row, (count, LANES)), 0, 1, stride=1, stride_axis=0)


def warp_block(k, stamps_ref, base_ref, mh, ml, lh, ll, zb, flux_ref):
    r_iota = lax.broadcasted_iota(jnp.int32, (LANES, LANES), 0)
    c_iota = lax.broadcasted_iota(jnp.int32, (LANES, LANES), 1)
    lower = r_iota >= c_iota
    for j in range(6):
        cols = slice(j * LANES, (j + 1) * LANES)
        full = skew(base_ref[j, pl.ds(k, 1), :], LANES)
        hi, lo = split(jnp.where(lower, full, 0.0))
        mh[64:192, cols] = hi
        ml[64:192, cols] = lo
        hi, lo = split(jnp.where(lower[0:64], 0.0, full[0:64]))
        mh[192:256, cols] = hi
        ml[192:256, cols] = lo
        for d, spots in enumerate((((0, 0), (1, 1)), ((1, 0),), ((0, 1),))):
            hi, lo = split(skew(base_ref[6 + 6 * d + j, pl.ds(k, 1), :], 64))
            for e, f in spots:
                at = (f * 6 + j) * LANES
                lh[e * 64 : (e + 1) * 64, at : at + LANES] = hi
                ll[e * 64 : (e + 1) * 64, at : at + LANES] = lo
    rows_a = stamps_ref[pl.ds(k, 96, 24), :]
    rows_b = stamps_ref[pl.ds(8 + k, 96, 24), :]
    rows_c = stamps_ref[pl.ds(16 + k, 96, 24), :]
    for f, (left, right, start) in enumerate(((rows_a, rows_b, 64), (rows_b, rows_c, 0))):
        xh, xl = split(jnp.concatenate([left, right], axis=1))
        z = mm(xh, mh[start : start + 256, :]) + mm(xl, mh[start : start + 256, :])
        z = z + mm(xh, ml[start : start + 256, :])
        zh, zl = split(z)
        for j in range(6):
            at = (f * 6 + j) * LANES
            zb[at : at + 96, 0:LANES] = zh[:, j * LANES : (j + 1) * LANES]
            zb[at : at + 96, LANES : 2 * LANES] = zl[:, j * LANES : (j + 1) * LANES]
    both = mm(lh[...], zb[...])
    out = both[:, 0:LANES] + both[:, LANES:] + mm(ll[...], zb[:, 0:LANES])
    flux_ref[k, 0] = out[0:64]
    flux_ref[k, 1] = out[64:128]


def filter_blocks(taps_ref, transposed):
    r_iota = lax.broadcasted_iota(jnp.int32, (LANES, LANES), 0)
    c_iota = lax.broadcasted_iota(jnp.int32, (LANES, LANES), 1)
    lag = c_iota - r_iota if transposed else r_iota - c_iota
    result = []
    for shift in (-LANES, 0, LANES):
        band = jnp.zeros((LANES, LANES), F32)
        for tap in range(2 * RF + 1):
            band = jnp.where(lag + shift == tap - RF, taps_ref[tap], band)
        result.append(band)
    return result


def kernel(
    stamps_hbm, var_ref, coef_ref, off_ref, shift_ref, dest_ref, pos_ref, taps_ref,
    coadd_ref, det_ref,
    stamps_ref, base_ref, mh, ml, lh, ll, zb, flux_ref,
    ids_z, zw, zf, ids_row, ids_in, send_w, send_f, landed, onehot, data,
    sums, mate, half_ref, msg, ret, chunks, xbuf, ybuf, halo_out, halo_in,
    local_sem, zw_send, zw_recv, zi_send, zi_recv, zf_send, zf_recv,
    id_send, id_recv, in_send, in_recv, mate_send, mate_recv, ret_send, ret_recv,
    ring_send, ring_recv, halo_send, halo_recv,
):
    z = lax.axis_index("visit")
    y = lax.axis_index("prow")
    p = lax.axis_index("pcol")
    j = y * NP + p
    r = j // 2
    core = lax.rem(p, 2)
    fetch = pltpu.make_async_copy(stamps_hbm, stamps_ref, local_sem.at[0])
    fetch.start()

    barrier = pltpu.get_barrier_semaphore()

    @pl.loop(1, NZ)
    def _(d):
        pl.semaphore_signal(barrier, inc=1, device_id=(lax.rem(z + d, NZ), y, p), device_id_type=MESH)

    @pl.loop(1, NPLANE)
    def _(d):
        other = lax.rem(j + d, NPLANE)
        pl.semaphore_signal(barrier, inc=1, device_id=(z, other // NP, lax.rem(other, NP)), device_id_type=MESH)

    row_iota = lax.broadcasted_iota(jnp.int32, (NB, LANES), 0)
    ids = jnp.zeros((NB, LANES), F32)
    for b in range(NB):
        ids = jnp.where(row_iota == b, (dest_ref[b] * 16 + pos_ref[b]).astype(F32), ids)
    ids_z[z] = ids
    pl.semaphore_wait(barrier, NZ - 1 + NPLANE - 1)

    def z_ids(d):
        return pltpu.make_async_remote_copy(
            src_ref=ids_z.at[z], dst_ref=ids_z.at[z], send_sem=zi_send.at[d], recv_sem=zi_recv.at[z],
            device_id=(lax.rem(z + d, NZ), y, p), device_id_type=MESH)

    def z_var(d):
        to = lax.rem(z + d, NZ)
        return pltpu.make_async_remote_copy(
            src_ref=var_ref.at[:, pl.ds(pl.multiple_of(to * 16, 16), 16), :], dst_ref=zw.at[z],
            send_sem=zw_send.at[d], recv_sem=zw_recv.at[z], device_id=(to, y, p), device_id_type=MESH)

    def z_flux(e, d):
        to = lax.rem(z + d, NZ)
        return pltpu.make_async_remote_copy(
            src_ref=flux_ref.at[:, e, pl.ds(pl.multiple_of(to * 8, 8), 8), :], dst_ref=zf.at[e, z],
            send_sem=zf_send.at[e, d], recv_sem=zf_recv.at[e, z], device_id=(to, y, p), device_id_type=MESH)

    def wait_z(recv, dst):
        for d in range(1, NZ):
            source = lax.rem(z + d, NZ)
            pltpu.make_async_copy(dst.at[source], dst.at[source], recv.at[source]).wait()

    @pl.loop(1, NZ)
    def _(d):
        z_ids(d).start()

    @pl.loop(1, NZ)
    def _(d):
        z_var(d).start()

    own_var = pltpu.make_async_copy(
        var_ref.at[:, pl.ds(pl.multiple_of(z * 16, 16), 16), :], zw.at[z], local_sem.at[1])
    own_var.start()

    make_bases(coef_ref, off_ref, shift_ref, base_ref)
    mh[0:64, :] = jnp.zeros((64, 6 * LANES), BF)
    ml[0:64, :] = jnp.zeros((64, 6 * LANES), BF)
    mh[256:320, :] = jnp.zeros((64, 6 * LANES), BF)
    ml[256:320, :] = jnp.zeros((64, 6 * LANES), BF)
    zb[...] = jnp.zeros(zb.shape, BF)
    fetch.wait()

    @pl.loop(0, NB)
    def _(k):
        warp_block(k, stamps_ref, base_ref, mh, ml, lh, ll, zb, flux_ref)

    for e in range(2):

        @pl.loop(1, NZ)
        def _(d):
            z_flux(e, d).start()

    wait_z(zi_recv, ids_z)
    lane64 = lax.rem(lax.broadcasted_iota(jnp.int32, (64, LANES), 1), 64)
    row64 = lax.broadcasted_iota(jnp.int32, (64, LANES), 0)
    picked = jnp.where(lane64 == row64, ids_z[...].reshape(64, LANES), 0.0)
    ids_in[j] = jnp.broadcast_to(jnp.sum(picked, axis=0, keepdims=True), (8, LANES))

    def in_ids(d):
        other = lax.rem(j + d, NPLANE)
        return pltpu.make_async_remote_copy(
            src_ref=ids_in.at[j], dst_ref=ids_in.at[j], send_sem=id_send.at[d], recv_sem=id_recv.at[j],
            device_id=(z, other // NP, lax.rem(other, NP)), device_id_type=MESH)

    @pl.loop(1, NPLANE)
    def _(d):
        in_ids(d).start()

    def in_copy(buf, kind, row):
        other = 2 * row + kind
        return pltpu.make_async_remote_copy(
            src_ref=buf.at[row], dst_ref=landed.at[j], send_sem=in_send.at[other], recv_sem=in_recv.at[j],
            device_id=(z, other // NP, lax.rem(other, NP)), device_id_type=MESH)

    def own_copy(buf):
        return pltpu.make_async_copy(buf.at[r], landed.at[j], in_recv.at[j])

    def send_rows(buf, kind, first, step):
        @pl.loop(0, 16 // step)
        def _(d):
            row = lax.rem(r // step + d, 16 // step) * step + first
            here = 2 * row + kind == j

            @pl.when(here)
            def _():
                own_copy(buf).start()

            @pl.when(jnp.logical_not(here))
            def _():
                in_copy(buf, kind, row).start()

    wait_z(zw_recv, zw)
    own_var.wait()
    for source in range(NZ):
        weight = 1.0 / jnp.swapaxes(zw[source], 0, 1)
        send_w[:, source * NB : (source + 1) * NB, :] = weight
    send_rows(send_w, 1, 0, 1)

    @pl.loop(1, NPLANE)
    def _(d):
        other = lax.rem(j + d, NPLANE)
        pltpu.make_async_copy(ids_in.at[other], ids_in.at[other], id_recv.at[other]).wait()

    @pl.loop(0, 16)
    def _(pair):
        lane = lax.broadcasted_iota(jnp.int32, (8, LANES), 1)
        mixed = jnp.where(lane < 64, ids_in[2 * pair], ids_in[2 * pair + 1])
        tile = lax.broadcasted_iota(jnp.int32, (TILES, LANES), 0).astype(F32)
        onehot[:, pl.ds(pl.multiple_of(pair * LANES, LANES), LANES)] = jnp.where(
            tile == mixed[0:1], 1.0, 0.0).astype(BF)

    col_blocks = jnp.concatenate(filter_blocks(taps_ref, False), axis=0)
    row_blocks = filter_blocks(taps_ref, True)
    col_hi, col_lo = split(col_blocks)
    row_band = jnp.concatenate(
        [row_blocks[0][:, LANES - RF :], row_blocks[1], row_blocks[2][:, 0:RF]], axis=1)
    row_hi, row_lo = split(row_band)

    for e in range(2):
        wait_z(zf_recv.at[e], zf.at[e])
        zf[e, z] = flux_ref[:, e, pl.ds(pl.multiple_of(z * 8, 8), 8), :]
        for source in range(NZ):
            cells = jnp.swapaxes(zf[e, source], 0, 1)
            for q in range(8):
                at = slice(source * NB, (source + 1) * NB)
                send_f[2 * q + e, at, :] = cells[q] * send_w[2 * q + e, at, :]
        send_rows(send_f, 0, e, 2)

    @pl.loop(0, NPLANE)
    def _(d):
        other = lax.rem(j + d, NPLANE)
        pltpu.make_async_copy(landed.at[other], landed.at[other], in_recv.at[other]).wait()

    hi, lo = split(landed[...].reshape(NPLANE * 64, LANES))
    data[:, 0:LANES] = hi
    data[:, LANES:] = lo
    total = mm(onehot[...], data[...])
    sums[...] = total[:, 0:LANES] + total[:, LANES:]

    trade = pltpu.make_async_remote_copy(
        src_ref=sums.at[pl.ds(pl.multiple_of((1 - core) * 256, 256), 256), :], dst_ref=mate,
        send_sem=mate_send, recv_sem=mate_recv, device_id=(z, y, p + 1 - 2 * core), device_id_type=MESH)
    trade.start()
    half_ref[0:16, :] = jnp.zeros((16, LANES), F32)
    half_ref[272:288, :] = jnp.zeros((16, LANES), F32)
    own = sums[pl.ds(pl.multiple_of(core * 256, 256), 256), :]
    trade.wait_recv()
    theirs = mate[...]
    half_ref[16:272, :] = jnp.where(core == 0, own, theirs) / (1.0 + jnp.where(core == 0, theirs, own))

    patch = lax.rem(lax.broadcasted_iota(jnp.int32, (64, LANES), 0) // 4, NP)
    lane = lax.broadcasted_iota(jnp.int32, (64, LANES), 1)
    right = half_ref[pl.ds(32, 64, 4), :]
    left = half_ref[pl.ds(3, 64, 4), :]
    beside = jnp.where((lane < RF) & (patch < NP - 1), right, 0.0)
    beside = jnp.where((lane >= LANES - RF) & (patch > 0), left, beside)
    for m in range(16):
        msg[m, 0:16, :] = half_ref[16 + 16 * m : 32 + 16 * m, :]
        msg[m, 16:20, :] = beside[4 * m : 4 * m + 4]
        msg[m, 20:24, :] = jnp.zeros((4, LANES), F32)

    def ret_copy(m):
        return pltpu.make_async_remote_copy(
            src_ref=msg.at[m], dst_ref=ret.at[r], send_sem=ret_send.at[m], recv_sem=ret_recv.at[r],
            device_id=(z, 2 * core + m // 8, lax.rem(m, 8)), device_id_type=MESH)

    def each_owner(far, near):
        @pl.loop(0, 16)
        def _(d):
            m = lax.rem(r + d, 16)
            here = jnp.logical_and(2 * core + m // 8 == y, lax.rem(m, 8) == p)

            @pl.when(here)
            def _():
                near(m)

            @pl.when(jnp.logical_not(here))
            def _():
                far(m)

    each_owner(
        lambda m: ret_copy(m).start(),
        lambda m: pltpu.make_async_copy(msg.at[m], ret.at[r], ret_recv.at[r]).start())

    @pl.loop(0, 16)
    def _(s):
        pltpu.make_async_copy(ret.at[s], ret.at[s], ret_recv.at[s]).wait()

    got = jnp.swapaxes(ret[...], 0, 1)
    mine = chunks.at[z]
    for t in range(16):
        mine[16 * t : 16 * t + 16, :] = got[t]
    packed = jnp.zeros((8, LANES), F32)
    for g in range(8):
        packed = packed + pltpu.roll(got[16 + g // 2, 8 * (g % 2) : 8 * (g % 2) + 8, :], (8 + 16 * g) % LANES, 1)
    mine[256:264, :] = packed

    parts = ((0, FIRST), (FIRST, CHUNK - FIRST))

    def ring(way, step, part):
        which = lax.rem(z - step + NZ, NZ) if way == 0 else lax.rem(z + step, NZ)
        to = lax.rem(z + 1, NZ) if way == 0 else lax.rem(z + NZ - 1, NZ)
        at, size = parts[part]
        ref = chunks.at[which, pl.ds(at, size), :]
        return pltpu.make_async_remote_copy(
            src_ref=ref, dst_ref=ref, send_sem=ring_send.at[way, step, part],
            recv_sem=ring_recv.at[way, step, part], device_id=(to, y, p), device_id_type=MESH)

    def came(way, step, part):
        which = lax.rem(z - step - 1 + NZ, NZ) if way == 0 else lax.rem(z + step + 1, NZ)
        at, size = parts[part]
        ref = chunks.at[which, pl.ds(at, size), :]
        pltpu.make_async_copy(ref, ref, ring_recv.at[way, step, part]).wait()

    def filter_chunk(which):
        chunk = chunks[which]
        lane8 = lax.broadcasted_iota(jnp.int32, (8, LANES), 1)
        for pr in range(4):
            beside = []
            for h in range(2):
                rolled = pltpu.roll(chunk[256:264], (LANES - 8 - 16 * (2 * pr + h)) % LANES, 1)
                beside.append(jnp.where((lane8 < RF) | (lane8 >= LANES - RF), rolled, 0.0))
            beside = jnp.concatenate(beside, axis=0)
            tiles = [chunk[(4 * pr + pc) * 16 : (4 * pr + pc) * 16 + 16] for pc in range(4)]
            at = pl.ds(pl.multiple_of(pr * 128 + which * 16, 16), 16)
            for pc in range(4):
                coadd_ref[at, pc * LANES : (pc + 1) * LANES] = tiles[pc]
            around = [beside, *tiles, beside]
            for pc in range(4):
                hi, lo = split(jnp.concatenate(around[pc : pc + 3], axis=1))
                xbuf[pc * 64 + pr * 16 : pc * 64 + pr * 16 + 16, :] = hi
                xbuf[256 + pc * 64 + pr * 16 : 256 + pc * 64 + pr * 16 + 16, :] = lo
        got = mm(xbuf[...], col_hi)
        got = got[0:256] + got[256:512] + mm(xbuf[0:256, :], col_lo)
        for pc in range(4):
            for pr in range(4):
                at = pl.ds(pl.multiple_of(RF + pr * 128 + which * 16, 8), 16)
                ybuf[at, pc * LANES : (pc + 1) * LANES] = got[pc * 64 + pr * 16 : pc * 64 + pr * 16 + 16]

    for part in range(2):
        ring(0, 0, part).start()
        ring(1, 0, part).start()
    filter_chunk(z)
    for step in range(1, 4):
        for part in range(2):
            for way in range(2):
                came(way, step - 1, part)
                if step < 3 or part == way:
                    ring(way, step, part).start()
                elif step == 3:
                    pass
        filter_chunk(lax.rem(z - step + NZ, NZ))
        filter_chunk(lax.rem(z + step, NZ))
    came(0, 3, 0)
    came(1, 3, 1)
    filter_chunk(lax.rem(z + 4, NZ))

    halo_out[0] = ybuf[RF : 2 * RF, :]
    halo_out[1] = ybuf[512 : 512 + RF, :]

    def halo(side):
        return pltpu.make_async_remote_copy(
            src_ref=halo_out.at[side], dst_ref=halo_in.at[1 - side], send_sem=halo_send.at[side],
            recv_sem=halo_recv.at[1 - side], device_id=(z, y - 1 + 2 * side, p), device_id_type=MESH)

    for side in range(2):
        there = y > 0 if side == 0 else y < NY - 1

        @pl.when(there)
        def _():
            halo(side).start()

    for side in range(2):
        there = y > 0 if side == 0 else y < NY - 1
        rows = slice(0, RF) if side == 0 else slice(512 + RF, 512 + 2 * RF)

        @pl.when(there)
        def _():
            halo(1 - side).wait_recv()
            ybuf[rows, :] = halo_in[side]

        @pl.when(jnp.logical_not(there))
        def _():
            ybuf[rows, :] = jnp.zeros((RF, 512), F32)

    for t in range(4):
        yh, yl = split(ybuf[t * 128 : t * 128 + 128 + 2 * RF, :])
        det_ref[t * 128 : (t + 1) * 128, :] = mm(row_hi, yh) + mm(row_hi, yl) + mm(row_lo, yh)

    for side in range(2):
        there = y > 0 if side == 0 else y < NY - 1

        @pl.when(there)
        def _():
            halo(side).wait_send()

    for way in range(2):
        for step in range(4):
            for part in range(2):
                if step < 3 or part == way:
                    ring(way, step, part).wait_send()
    each_owner(lambda m: ret_copy(m).wait_send(), lambda m: None)
    trade.wait_send()

    @pl.loop(0, 16)
    def _(row):
        for kind, buf in ((0, send_f), (1, send_w)):

            @pl.when(2 * row + kind != j)
            def _():
                in_copy(buf, kind, row).wait_send()

    @pl.loop(1, NPLANE)
    def _(d):
        in_ids(d).wait_send()

    @pl.loop(1, NZ)
    def _(d):
        z_ids(d).wait_send()
        z_var(d).wait_send()
        for e in range(2):
            z_flux(e, d).wait_send()


def body(stamps, variance, coefficients, band_offsets, shifts, destination, position, psf_taps):
    cells = stamps.reshape(NB, S * S // LANES, LANES).transpose(1, 0, 2).reshape(NB * S * S // LANES, LANES)
    vmem = pl.BlockSpec(memory_space=pltpu.VMEM)
    smem = pl.BlockSpec(memory_space=pltpu.SMEM)
    hbm = pl.BlockSpec(memory_space=pl.ANY)
    dma = pltpu.SemaphoreType.DMA
    scratch = [
        pltpu.VMEM((NB * S * S // LANES, LANES), F32),
        pltpu.VMEM((24, NB, LANES), F32),
        pltpu.VMEM((320, 768), BF),
        pltpu.VMEM((320, 768), BF),
        pltpu.VMEM((LANES, 12 * LANES), BF),
        pltpu.VMEM((LANES, 12 * LANES), BF),
        pltpu.VMEM((12 * LANES, 2 * LANES), BF),
        pltpu.VMEM((NB, 2, 64, LANES), F32),
        pltpu.VMEM((NZ, NB, LANES), F32),
        pltpu.VMEM((NZ, NB, 16, LANES), F32),
        pltpu.VMEM((2, NZ, NB, 8, LANES), F32),
        pltpu.VMEM((8, LANES), F32),
        pltpu.VMEM((NPLANE, 8, LANES), F32),
        pltpu.VMEM((16, 64, LANES), F32),
        pltpu.VMEM((16, 64, LANES), F32),
        pltpu.VMEM((NPLANE, 64, LANES), F32),
        pltpu.VMEM((TILES, NPLANE * 64), BF),
        pltpu.VMEM((NPLANE * 64, 2 * LANES), BF),
        pltpu.VMEM((TILES, LANES), F32),
        pltpu.VMEM((TILES // 2, LANES), F32),
        pltpu.VMEM((288, LANES), F32),
        pltpu.VMEM((16, 24, LANES), F32),
        pltpu.VMEM((16, 24, LANES), F32),
        pltpu.VMEM((NZ, CHUNK, LANES), F32),
        pltpu.VMEM((512, 3 * LANES), BF),
        pltpu.VMEM((512 + 2 * RF, 512), F32),
        pltpu.VMEM((2, RF, 512), F32),
        pltpu.VMEM((2, RF, 512), F32),
        dma((2,)),
        dma((NZ,)), dma((NZ,)), dma((NZ,)), dma((NZ,)), dma((2, NZ)), dma((2, NZ)),
        dma((NPLANE,)), dma((NPLANE,)), dma((NPLANE,)), dma((NPLANE,)), dma, dma, dma((16,)), dma((16,)),
        dma((2, 4, 2)), dma((2, 4, 2)), dma((2,)), dma((2,)),
    ]
    return pl.pallas_call(
        kernel,
        out_shape=(jax.ShapeDtypeStruct((512, 512), F32), jax.ShapeDtypeStruct((512, 512), F32)),
        in_specs=[hbm, hbm, vmem, vmem, vmem, smem, smem, smem],
        out_specs=(vmem, vmem),
        scratch_shapes=scratch,
        compiler_params=pltpu.CompilerParams(
            collective_id=0, has_side_effects=True, vmem_limit_bytes=40 * 1024 * 1024),
    )(cells, variance, coefficients, band_offsets, shifts, destination, position, psf_taps)


def solution(mesh):
    placed = (
        P(("visit", "prow", "pcol"), None),
        P(("visit", "prow", "pcol"), None, None),
        P(("visit", "prow", "pcol"), None),
        P(("visit", "prow", "pcol"), None),
        P(("visit", "prow", "pcol"), None),
        P(("visit", "prow", "pcol")),
        P(("visit", "prow", "pcol")),
        P(),
    )
    return jax.shard_map(
        body,
        mesh=mesh,
        in_specs=placed,
        out_specs=(P("prow", "pcol"), P("prow", "pcol")),
        check_vma=False,
    )
```

```python
import math

import jax
import jax.numpy as jnp
from jax import lax
from jax.experimental import pallas as pl
from jax.experimental.pallas import tpu as pltpu
from jax.sharding import PartitionSpec as P

MESH = pl.DeviceIdType.MESH
NB = 8
S = 192
B = 128
KR = 15
RF = 8
NZ = 8
NY = 4
NP = 8
NPLANE = NY * NP
TILES = 512
LANES = 128
WIDTHS = (1.0, 2.0, 4.0)
TAPS = (-2, -1, 0, 1, 2, 3)
CHUNK = 264
PARTS = ((0, 64), (64, 64), (128, 64), (192, 72))
BF = jnp.bfloat16
F32 = jnp.float32


def norms(width):
    lags = range(-KR, KR + 1)
    bell = math.sqrt(sum(math.exp(-((t / width) ** 2)) for t in lags))
    quad = math.sqrt(sum((t / width) ** 4 * math.exp(-((t / width) ** 2)) for t in lags))
    return bell, quad


def split(x):
    hi = x.astype(BF)
    return hi, (x - hi.astype(F32)).astype(BF)


def mm(a, b):
    return jnp.dot(a, b, preferred_element_type=F32)


def sinc(x):
    scaled = math.pi * x
    return jnp.where(x == 0.0, 1.0, jnp.sin(scaled) / jnp.where(x == 0.0, 1.0, scaled))


def lanczos_weights(shift):
    lane = lax.broadcasted_iota(jnp.int32, (NB, LANES), 1).astype(F32)
    x = lane + float(TAPS[0]) - shift
    return jnp.where(jnp.abs(x) < 3.0, sinc(x) * sinc(x / 3.0), 0.0)


def factor_rows(place, weights):
    bells = [jnp.zeros((NB, LANES), F32) for _ in WIDTHS]
    quads = [jnp.zeros((NB, LANES), F32) for _ in WIDTHS]
    for index, tap in enumerate(TAPS):
        lag = place - float(tap + KR)
        weight = jnp.where(jnp.abs(lag) <= float(KR), weights[:, index : index + 1], 0.0)
        for w, width in enumerate(WIDTHS):
            bell_norm, quad_norm = norms(width)
            ratio = lag * (1.0 / width)
            term = weight * jnp.exp(-0.5 * ratio * ratio)
            bells[w] = bells[w] + term * (1.0 / bell_norm)
            quads[w] = quads[w] + ratio * ratio * term * (1.0 / quad_norm)
    return bells, quads


def make_bases(coef_ref, off_ref, shift_ref, base_ref):
    row = lax.broadcasted_iota(jnp.int32, (NB, LANES), 0)

    def column(read):
        result = jnp.zeros((NB, LANES), F32)
        for b in range(NB):
            result = jnp.where(row == b, read(b).astype(F32), result)
        return result

    lane_int = lax.broadcasted_iota(jnp.int32, (NB, LANES), 1)
    lane = lane_int.astype(F32)
    col_weights = lanczos_weights(column(lambda b: shift_ref[1, b]))
    row_weights = lanczos_weights(column(lambda b: shift_ref[0, b]))
    place = jnp.where(lane_int == 0, 0.0, float(LANES) - lane)
    row_offset = column(lambda b: off_ref[0, b])
    bells, quads = factor_rows(place - column(lambda b: off_ref[1, b]), col_weights)
    for w in range(3):
        base_ref[2 * w] = bells[w]
        base_ref[2 * w + 1] = quads[w]
    coefs = [column(lambda b, i=i: coef_ref[b, i]) for i in range(9)]
    for d, delta in enumerate((0.0, -1.0, 1.0)):
        bells, quads = factor_rows(2.0 * lane + delta - row_offset, row_weights)
        for w in range(3):
            first, second, third = coefs[3 * w : 3 * w + 3]
            base_ref[6 + 6 * d + 2 * w] = first * bells[w] + second * quads[w]
            base_ref[6 + 6 * d + 2 * w + 1] = third * bells[w]


def skew(row, count):
    return pltpu.roll(jnp.broadcast_to(row, (count, LANES)), 0, 1, stride=1, stride_axis=0)


def warp_block(k, stamps_ref, base_ref, mh, ml, lh, ll, zb, flux_ref):
    r_iota = lax.broadcasted_iota(jnp.int32, (LANES, LANES), 0)
    c_iota = lax.broadcasted_iota(jnp.int32, (LANES, LANES), 1)
    lower = r_iota >= c_iota
    for j in range(6):
        cols = slice(j * LANES, (j + 1) * LANES)
        full = skew(base_ref[j, pl.ds(k, 1), :], LANES)
        hi, lo = split(jnp.where(lower, full, 0.0))
        mh[64:192, cols] = hi
        ml[64:192, cols] = lo
        hi, lo = split(jnp.where(lower[0:64], 0.0, full[0:64]))
        mh[192:256, cols] = hi
        ml[192:256, cols] = lo
        for d, spots in enumerate((((0, 0), (1, 1)), ((1, 0),), ((0, 1),))):
            hi, lo = split(skew(base_ref[6 + 6 * d + j, pl.ds(k, 1), :], 64))
            for e, f in spots:
                at = (f * 6 + j) * LANES
                lh[e * 64 : (e + 1) * 64, at : at + LANES] = hi
                ll[e * 64 : (e + 1) * 64, at : at + LANES] = lo
    rows_a = stamps_ref[pl.ds(k, 96, 24), :]
    rows_b = stamps_ref[pl.ds(8 + k, 96, 24), :]
    rows_c = stamps_ref[pl.ds(16 + k, 96, 24), :]
    for f, (left, right, start) in enumerate(((rows_a, rows_b, 64), (rows_b, rows_c, 0))):
        xh, xl = split(jnp.concatenate([left, right], axis=1))
        z = mm(xh, mh[start : start + 256, :]) + mm(xl, mh[start : start + 256, :])
        z = z + mm(xh, ml[start : start + 256, :])
        zh, zl = split(z)
        for j in range(6):
            at = (f * 6 + j) * LANES
            zb[at : at + 96, 0:LANES] = zh[:, j * LANES : (j + 1) * LANES]
            zb[at : at + 96, LANES : 2 * LANES] = zl[:, j * LANES : (j + 1) * LANES]
    both = mm(lh[...], zb[...])
    out = both[:, 0:LANES] + both[:, LANES:] + mm(ll[...], zb[:, 0:LANES])
    flux_ref[k, 0] = out[0:64]
    flux_ref[k, 1] = out[64:128]


def filter_blocks(taps_ref, transposed):
    r_iota = lax.broadcasted_iota(jnp.int32, (LANES, LANES), 0)
    c_iota = lax.broadcasted_iota(jnp.int32, (LANES, LANES), 1)
    lag = c_iota - r_iota if transposed else r_iota - c_iota
    result = []
    for shift in (-LANES, 0, LANES):
        band = jnp.zeros((LANES, LANES), F32)
        for tap in range(2 * RF + 1):
            band = jnp.where(lag + shift == tap - RF, taps_ref[tap], band)
        result.append(band)
    return result


def kernel(
    stamps_hbm, var_ref, coef_hbm, off_hbm, shift_hbm, dest_hbm, pos_hbm, taps_hbm,
    coadd_hbm, rows_hbm,
    coef_ref, off_ref, shift_ref, dest_ref, pos_ref, taps_ref,
    stamps_ref, base_ref, mh, ml, lh, ll, zb, flux_ref,
    ids_z, zw, zf, ids_in, send_w, send_f, landed, onehot, data,
    sums, mate, half_ref, msg, ret, chunks, xbuf, ybuf, coadd_ref,
    seen, small_sem, local_sem, zw_send, zw_recv, zi_send, zi_recv, zf_send, zf_recv,
    id_send, id_recv, in_send, in_recv, mate_send, mate_recv, ret_send, ret_recv,
    ring_send, ring_recv, halo_send, halo_recv, out_sem,
):
    z = lax.axis_index("visit")
    y = lax.axis_index("prow")
    p = lax.axis_index("pcol")
    j = y * NP + p
    r = j // 2
    core = lax.rem(p, 2)
    small = [
        pltpu.make_async_copy(far, near, small_sem.at[i])
        for i, (far, near) in enumerate((
            (dest_hbm, dest_ref), (pos_hbm, pos_ref), (off_hbm, off_ref), (shift_hbm, shift_ref),
            (coef_hbm, coef_ref), (taps_hbm, taps_ref)))
    ]
    for copy in small:
        copy.start()
    fetch = pltpu.make_async_copy(stamps_hbm, stamps_ref, local_sem.at[0])
    fetch.start()

    later = []
    barrier = pltpu.get_barrier_semaphore()

    @pl.loop(1, NZ)
    def _(d):
        pl.semaphore_signal(barrier, inc=1, device_id=(lax.rem(z + d, NZ), y, p), device_id_type=MESH)

    @pl.loop(1, NY)
    def _(d):
        pl.semaphore_signal(barrier, inc=1, device_id=(z, lax.rem(y + d, NY), p), device_id_type=MESH)

    @pl.loop(1, NP)
    def _(d):
        pl.semaphore_signal(barrier, inc=1, device_id=(z, y, lax.rem(p + d, NP)), device_id_type=MESH)

    for copy in small:
        copy.wait()
    row_iota = lax.broadcasted_iota(jnp.int32, (NB, LANES), 0)
    ids = jnp.zeros((NB, LANES), F32)
    for b in range(NB):
        ids = jnp.where(row_iota == b, (dest_ref[b] * 16 + pos_ref[b]).astype(F32), ids)
    ids_z[z] = ids
    pl.semaphore_wait(barrier, NZ + NY + NP - 3)

    def z_ids(d):
        return pltpu.make_async_remote_copy(
            src_ref=ids_z.at[z], dst_ref=ids_z.at[z], send_sem=zi_send.at[d], recv_sem=zi_recv.at[z],
            device_id=(lax.rem(z + d, NZ), y, p), device_id_type=MESH)

    def z_var(d):
        to = lax.rem(z + d, NZ)
        return pltpu.make_async_remote_copy(
            src_ref=var_ref.at[:, pl.ds(pl.multiple_of(to * 16, 16), 16), :], dst_ref=zw.at[z],
            send_sem=zw_send.at[d], recv_sem=zw_recv.at[z], device_id=(to, y, p), device_id_type=MESH)

    def z_flux(e, d):
        to = lax.rem(z + d, NZ)
        return pltpu.make_async_remote_copy(
            src_ref=flux_ref.at[:, e, pl.ds(pl.multiple_of(to * 8, 8), 8), :], dst_ref=zf.at[e, z],
            send_sem=zf_send.at[e, d], recv_sem=zf_recv.at[e, z], device_id=(to, y, p), device_id_type=MESH)

    def wait_z(recv, dst):
        for d in range(1, NZ):
            source = lax.rem(z + d, NZ)
            pltpu.make_async_copy(dst.at[source], dst.at[source], recv.at[source]).wait()

    @pl.loop(1, NZ)
    def _(d):
        z_ids(d).start()

    @pl.loop(1, NZ)
    def _(d):
        z_var(d).start()

    @later.append
    def _():
        @pl.loop(1, NZ)
        def _(d):
            z_ids(d).wait_send()
            z_var(d).wait_send()

    own_var = pltpu.make_async_copy(
        var_ref.at[:, pl.ds(pl.multiple_of(z * 16, 16), 16), :], zw.at[z], local_sem.at[1])
    own_var.start()

    @pl.loop(1, NY)
    def _(d):
        pl.semaphore_signal(seen, inc=1, device_id=(z, lax.rem(y + d, NY), p), device_id_type=MESH)

    make_bases(coef_ref, off_ref, shift_ref, base_ref)
    mh[0:64, :] = jnp.zeros((64, 6 * LANES), BF)
    ml[0:64, :] = jnp.zeros((64, 6 * LANES), BF)
    mh[256:320, :] = jnp.zeros((64, 6 * LANES), BF)
    ml[256:320, :] = jnp.zeros((64, 6 * LANES), BF)
    zb[...] = jnp.zeros(zb.shape, BF)
    fetch.wait()

    @pl.loop(0, NB)
    def _(k):
        warp_block(k, stamps_ref, base_ref, mh, ml, lh, ll, zb, flux_ref)

    for e in range(2):

        @pl.loop(1, NZ)
        def _(d):
            z_flux(e, d).start()

    @later.append
    def _():
        @pl.loop(1, NZ)
        def _(d):
            for e in range(2):
                z_flux(e, d).wait_send()

    wait_z(zi_recv, ids_z)
    lane64 = lax.rem(lax.broadcasted_iota(jnp.int32, (64, LANES), 1), 64)
    row64 = lax.broadcasted_iota(jnp.int32, (64, LANES), 0)
    picked = jnp.where(lane64 == row64, ids_z[...].reshape(64, LANES), 0.0)
    ids_in[j] = jnp.broadcast_to(jnp.sum(picked, axis=0, keepdims=True), (8, LANES))

    def in_ids(d):
        other = lax.rem(j + d, NPLANE)
        return pltpu.make_async_remote_copy(
            src_ref=ids_in.at[j], dst_ref=ids_in.at[j], send_sem=id_send.at[d], recv_sem=id_recv.at[j],
            device_id=(z, other // NP, lax.rem(other, NP)), device_id_type=MESH)

    pl.semaphore_wait(seen, NY - 1)

    @pl.loop(1, NPLANE)
    def _(d):
        in_ids(d).start()

    @later.append
    def _():
        @pl.loop(1, NPLANE)
        def _(d):
            in_ids(d).wait_send()

    def in_copy(buf, kind, row):
        other = 2 * row + kind
        return pltpu.make_async_remote_copy(
            src_ref=buf.at[row], dst_ref=landed.at[j], send_sem=in_send.at[other], recv_sem=in_recv.at[j],
            device_id=(z, other // NP, lax.rem(other, NP)), device_id_type=MESH)

    def own_copy(buf):
        return pltpu.make_async_copy(buf.at[r], landed.at[j], in_recv.at[j])

    @later.append
    def _():
        @pl.loop(0, 16)
        def _(row):
            for kind, buf in ((0, send_f), (1, send_w)):

                @pl.when(2 * row + kind != j)
                def _():
                    in_copy(buf, kind, row).wait_send()

    def send_rows(buf, kind, first, step):
        @pl.loop(0, 16 // step)
        def _(d):
            row = lax.rem(r // step + d, 16 // step) * step + first
            here = 2 * row + kind == j

            @pl.when(here)
            def _():
                own_copy(buf).start()

            @pl.when(jnp.logical_not(here))
            def _():
                in_copy(buf, kind, row).start()

    wait_z(zw_recv, zw)
    own_var.wait()
    for source in range(NZ):
        weight = 1.0 / jnp.swapaxes(zw[source], 0, 1)
        send_w[:, source * NB : (source + 1) * NB, :] = weight
    send_rows(send_w, 1, 0, 1)

    @pl.loop(1, NPLANE)
    def _(d):
        other = lax.rem(j + d, NPLANE)
        pltpu.make_async_copy(ids_in.at[other], ids_in.at[other], id_recv.at[other]).wait()

    @pl.loop(0, 16)
    def _(pair):
        lane = lax.broadcasted_iota(jnp.int32, (8, LANES), 1)
        mixed = jnp.where(lane < 64, ids_in[2 * pair], ids_in[2 * pair + 1])
        tile = lax.broadcasted_iota(jnp.int32, (TILES, LANES), 0).astype(F32)
        onehot[:, pl.ds(pl.multiple_of(pair * LANES, LANES), LANES)] = jnp.where(
            tile == mixed[0:1], 1.0, 0.0).astype(BF)

    col_blocks = jnp.concatenate(filter_blocks(taps_ref, False), axis=0)
    col_hi, col_lo = split(col_blocks)
    col_both = jnp.concatenate([col_hi, col_lo], axis=1)

    for e in range(2):
        wait_z(zf_recv.at[e], zf.at[e])
        zf[e, z] = flux_ref[:, e, pl.ds(pl.multiple_of(z * 8, 8), 8), :]
        for source in range(NZ):
            cells = jnp.swapaxes(zf[e, source], 0, 1)
            for q in range(8):
                at = slice(source * NB, (source + 1) * NB)
                send_f[2 * q + e, at, :] = cells[q] * send_w[2 * q + e, at, :]
        send_rows(send_f, 0, e, 2)

    @pl.loop(0, NPLANE)
    def _(d):
        other = lax.rem(j + d, NPLANE)
        pltpu.make_async_copy(landed.at[other], landed.at[other], in_recv.at[other]).wait()

    hi, lo = split(landed[...].reshape(NPLANE * 64, LANES))
    data[:, 0:LANES] = hi
    data[:, LANES:] = lo
    total = mm(onehot[...], data[...])
    sums[...] = total[:, 0:LANES] + total[:, LANES:]

    trade = pltpu.make_async_remote_copy(
        src_ref=sums.at[pl.ds(pl.multiple_of((1 - core) * 256, 256), 256), :], dst_ref=mate,
        send_sem=mate_send, recv_sem=mate_recv, device_id=(z, y, p + 1 - 2 * core), device_id_type=MESH)
    trade.start()
    later.append(trade.wait_send)
    half_ref[0:16, :] = jnp.zeros((16, LANES), F32)
    half_ref[272:288, :] = jnp.zeros((16, LANES), F32)
    own = sums[pl.ds(pl.multiple_of(core * 256, 256), 256), :]
    trade.wait_recv()
    theirs = mate[...]
    half_ref[16:272, :] = jnp.where(core == 0, own, theirs) / (1.0 + jnp.where(core == 0, theirs, own))

    patch = lax.rem(lax.broadcasted_iota(jnp.int32, (64, LANES), 0) // 4, NP)
    lane = lax.broadcasted_iota(jnp.int32, (64, LANES), 1)
    right = half_ref[pl.ds(32, 64, 4), :]
    left = half_ref[pl.ds(3, 64, 4), :]
    beside = jnp.where((lane < RF) & (patch < NP - 1), right, 0.0)
    beside = jnp.where((lane >= LANES - RF) & (patch > 0), left, beside)
    for m in range(16):
        msg[m, 0:16, :] = half_ref[16 + 16 * m : 32 + 16 * m, :]
        msg[m, 16:20, :] = beside[4 * m : 4 * m + 4]
        msg[m, 20:24, :] = jnp.zeros((4, LANES), F32)

    def ret_copy(m):
        return pltpu.make_async_remote_copy(
            src_ref=msg.at[m], dst_ref=ret.at[r], send_sem=ret_send.at[m], recv_sem=ret_recv.at[r],
            device_id=(z, 2 * core + m // 8, lax.rem(m, 8)), device_id_type=MESH)

    def each_owner(far, near):
        @pl.loop(0, 16)
        def _(d):
            m = lax.rem(r + d, 16)
            here = jnp.logical_and(2 * core + m // 8 == y, lax.rem(m, 8) == p)

            @pl.when(here)
            def _():
                near(m)

            @pl.when(jnp.logical_not(here))
            def _():
                far(m)

    each_owner(
        lambda m: ret_copy(m).start(),
        lambda m: pltpu.make_async_copy(msg.at[m], ret.at[r], ret_recv.at[r]).start())

    later.append(lambda: each_owner(lambda m: ret_copy(m).wait_send(), lambda m: None))

    @pl.loop(0, 16)
    def _(s):
        pltpu.make_async_copy(ret.at[s], ret.at[s], ret_recv.at[s]).wait()

    got = jnp.swapaxes(ret[...], 0, 1)
    mine = chunks.at[z]
    for t in range(16):
        mine[16 * t : 16 * t + 16, :] = got[t]
    packed = jnp.zeros((8, LANES), F32)
    for g in range(8):
        packed = packed + pltpu.roll(got[16 + g // 2, 8 * (g % 2) : 8 * (g % 2) + 8, :], (8 + 16 * g) % LANES, 1)
    mine[256:264, :] = packed


    def ring(way, step, part):
        which = lax.rem(z - step + NZ, NZ) if way == 0 else lax.rem(z + step, NZ)
        to = lax.rem(z + 1, NZ) if way == 0 else lax.rem(z + NZ - 1, NZ)
        at, size = PARTS[part]
        ref = chunks.at[which, pl.ds(at, size), :]
        return pltpu.make_async_remote_copy(
            src_ref=ref, dst_ref=ref, send_sem=ring_send.at[way, step, part],
            recv_sem=ring_recv.at[way, step, part], device_id=(to, y, p), device_id_type=MESH)

    def came(way, step, part):
        which = lax.rem(z - step - 1 + NZ, NZ) if way == 0 else lax.rem(z + step + 1, NZ)
        at, size = PARTS[part]
        ref = chunks.at[which, pl.ds(at, size), :]
        pltpu.make_async_copy(ref, ref, ring_recv.at[way, step, part]).wait()

    def halo(side):
        mine, theirs = (RF, 512 + RF) if side == 0 else (512, 0)
        return pltpu.make_async_remote_copy(
            src_ref=ybuf.at[pl.ds(mine, RF), :], dst_ref=ybuf.at[pl.ds(theirs, RF), :],
            send_sem=halo_send.at[side], recv_sem=halo_recv.at[1 - side],
            device_id=(z, y - 1 + 2 * side, p), device_id_type=MESH)

    def filter_chunk(which):
        chunk = chunks[which]
        lane8 = lax.broadcasted_iota(jnp.int32, (8, LANES), 1)
        for pr in range(4):
            beside = []
            for h in range(2):
                rolled = pltpu.roll(chunk[256:264], (LANES - 8 - 16 * (2 * pr + h)) % LANES, 1)
                beside.append(jnp.where((lane8 < RF) | (lane8 >= LANES - RF), rolled, 0.0))
            beside = jnp.concatenate(beside, axis=0)
            tiles = [chunk[(4 * pr + pc) * 16 : (4 * pr + pc) * 16 + 16] for pc in range(4)]
            at = pl.ds(pl.multiple_of(pr * 128 + which * 16, 16), 16)
            for pc in range(4):
                coadd_ref[at, pc * LANES : (pc + 1) * LANES] = tiles[pc]
            around = [beside, *tiles, beside]
            for pc in range(4):
                hi, lo = split(jnp.concatenate(around[pc : pc + 3], axis=1))
                xbuf[pc * 64 + pr * 16 : pc * 64 + pr * 16 + 16, :] = hi
                xbuf[256 + pc * 64 + pr * 16 : 256 + pc * 64 + pr * 16 + 16, :] = lo
        got = mm(xbuf[0:256, :], col_both)
        got = got[:, 0:LANES] + got[:, LANES:] + mm(xbuf[256:512, :], col_hi)
        for pc in range(4):
            for pr in range(4):
                at = pl.ds(pl.multiple_of(RF + pr * 128 + which * 16, 8), 16)
                ybuf[at, pc * LANES : (pc + 1) * LANES] = got[pc * 64 + pr * 16 : pc * 64 + pr * 16 + 16]

        for pr in range(4):
            at = pl.ds(pl.multiple_of(pr * 128 + which * 16, 16), 16)
            pltpu.make_async_copy(coadd_ref.at[at, :], coadd_hbm.at[at, :], out_sem.at[0]).start()

        @pl.when(jnp.logical_and(which == 0, y > 0))
        def _():
            halo(0).start()

        @pl.when(jnp.logical_and(which == NZ - 1, y < NY - 1))
        def _():
            halo(1).start()

    def passes(way, step, part):
        return step < 3 or part // 2 == way

    @later.append
    def _():
        for way in range(2):
            for step in range(4):
                for part in range(4):
                    if passes(way, step, part):
                        ring(way, step, part).wait_send()

    def advance(step, part):
        for way in range(2):
            if passes(way, step - 1, part):
                came(way, step - 1, part)
                if step < 4 and passes(way, step, part):
                    ring(way, step, part).start()

    for part in range(4):
        ring(0, 0, part).start()
        ring(1, 0, part).start()
    filter_chunk(z)
    for step in range(1, 5):
        for part in range(4):
            advance(step, part)
            if step > 1 and part == 1:
                filter_chunk(lax.rem(z - step + 1 + NZ, NZ))
        if step > 1:
            filter_chunk(lax.rem(z + step - 1, NZ))
    filter_chunk(lax.rem(z + 4, NZ))

    for side in range(2):
        there = y > 0 if side == 0 else y < NY - 1
        at = 0 if side == 0 else 512 + RF

        @pl.when(there)
        def _():
            halo(1 - side).wait_recv()

        @pl.when(jnp.logical_not(there))
        def _():
            ybuf[at : at + RF, :] = jnp.zeros((RF, 512), F32)

    @later.append
    def _():
        for side in range(2):
            there = y > 0 if side == 0 else y < NY - 1

            @pl.when(there)
            def _():
                halo(side).wait_send()

    rows_out = pltpu.make_async_copy(ybuf, rows_hbm, out_sem.at[1])
    rows_out.start()
    for left in later:
        left()
    pltpu.make_async_copy(coadd_ref, coadd_hbm, out_sem.at[0]).wait()
    rows_out.wait()


def filter_rows(taps_hbm, cells_hbm, rows_hbm, coadd_hbm, det_hbm, taps_ref, rows_ref, cells_ref, det_ref, in_sem, out_sem):
    cells = pltpu.make_async_copy(cells_hbm, cells_ref, in_sem.at[5])
    pieces = []
    for t in range(4):
        at = pl.ds(t * 136, 136 if t < 3 else 120)
        pieces.append(pltpu.make_async_copy(rows_hbm.at[at, :], rows_ref.at[at, :], in_sem.at[t]))
    taps = pltpu.make_async_copy(taps_hbm, taps_ref, in_sem.at[4])
    for copy in (taps, *pieces, cells):
        copy.start()
    taps.wait()
    blocks = filter_blocks(taps_ref, True)
    band = jnp.concatenate([blocks[0][:, LANES - RF :], blocks[1], blocks[2][:, 0:RF]], axis=1)
    hi, lo = split(band)
    pieces[0].wait()
    results = []
    for t in range(4):
        if t < 3:
            pieces[t + 1].wait()
        yh, yl = split(rows_ref[t * 128 : t * 128 + 128 + 2 * RF, :])
        det_ref[t * 128 : (t + 1) * 128, :] = mm(hi, yh) + mm(hi, yl) + mm(lo, yh)
        at = pl.ds(t * 128, 128)
        results.append(pltpu.make_async_copy(det_ref.at[at, :], det_hbm.at[at, :], out_sem.at[t]))
        results[-1].start()
        if t == 1:
            cells.wait()
            results.append(pltpu.make_async_copy(cells_ref, coadd_hbm, out_sem.at[4]))
            results[-1].start()
    for copy in results:
        copy.wait()


def body(stamps, variance, coefficients, band_offsets, shifts, destination, position, psf_taps):
    cells = stamps.reshape(NB, S * S // LANES, LANES).transpose(1, 0, 2).reshape(NB * S * S // LANES, LANES)
    hbm = pl.BlockSpec(memory_space=pl.ANY)
    dma = pltpu.SemaphoreType.DMA
    scratch = [
        pltpu.SMEM((NB, 9), F32),
        pltpu.SMEM((2, NB), jnp.int32),
        pltpu.SMEM((2, NB), F32),
        pltpu.SMEM((NB,), jnp.int32),
        pltpu.SMEM((NB,), jnp.int32),
        pltpu.SMEM((2 * RF + 1,), F32),
        pltpu.VMEM((NB * S * S // LANES, LANES), F32),
        pltpu.VMEM((24, NB, LANES), F32),
        pltpu.VMEM((320, 768), BF),
        pltpu.VMEM((320, 768), BF),
        pltpu.VMEM((LANES, 12 * LANES), BF),
        pltpu.VMEM((LANES, 12 * LANES), BF),
        pltpu.VMEM((12 * LANES, 2 * LANES), BF),
        pltpu.VMEM((NB, 2, 64, LANES), F32),
        pltpu.VMEM((NZ, NB, LANES), F32),
        pltpu.VMEM((NZ, NB, 16, LANES), F32),
        pltpu.VMEM((2, NZ, NB, 8, LANES), F32),
        pltpu.VMEM((NPLANE, 8, LANES), F32),
        pltpu.VMEM((16, 64, LANES), F32),
        pltpu.VMEM((16, 64, LANES), F32),
        pltpu.VMEM((NPLANE, 64, LANES), F32),
        pltpu.VMEM((TILES, NPLANE * 64), BF),
        pltpu.VMEM((NPLANE * 64, 2 * LANES), BF),
        pltpu.VMEM((TILES, LANES), F32),
        pltpu.VMEM((TILES // 2, LANES), F32),
        pltpu.VMEM((288, LANES), F32),
        pltpu.VMEM((16, 24, LANES), F32),
        pltpu.VMEM((16, 24, LANES), F32),
        pltpu.VMEM((NZ, CHUNK, LANES), F32),
        pltpu.VMEM((512, 3 * LANES), BF),
        pltpu.VMEM((512 + 2 * RF, 512), F32),
        pltpu.VMEM((512, 512), F32),
        pltpu.SemaphoreType.REGULAR, dma((6,)), dma((2,)),
        dma((NZ,)), dma((NZ,)), dma((NZ,)), dma((NZ,)), dma((2, NZ)), dma((2, NZ)),
        dma((NPLANE,)), dma((NPLANE,)), dma((NPLANE,)), dma((NPLANE,)), dma, dma, dma((16,)), dma((16,)),
        dma((2, 4, 4)), dma((2, 4, 4)), dma((2,)), dma((2,)), dma((2,)),
    ]
    coadd, rows = pl.pallas_call(
        kernel,
        out_shape=(jax.ShapeDtypeStruct((512, 512), F32), jax.ShapeDtypeStruct((512 + 2 * RF, 512), F32)),
        in_specs=[hbm] * 8,
        out_specs=(hbm, hbm),
        scratch_shapes=scratch,
        compiler_params=pltpu.CompilerParams(
            collective_id=0, has_side_effects=True, vmem_limit_bytes=60 * 1024 * 1024),
    )(cells, variance, coefficients, band_offsets.T, shifts.T, destination, position, psf_taps)
    return pl.pallas_call(
        filter_rows,
        out_shape=(jax.ShapeDtypeStruct((512, 512), F32), jax.ShapeDtypeStruct((512, 512), F32)),
        in_specs=[hbm, hbm, hbm],
        out_specs=(hbm, hbm),
        scratch_shapes=[
            pltpu.SMEM((2 * RF + 1,), F32), pltpu.VMEM((512 + 2 * RF, 512), F32), pltpu.VMEM((512, 512), F32),
            pltpu.VMEM((512, 512), F32), dma((6,)), dma((5,))],
        compiler_params=pltpu.CompilerParams(vmem_limit_bytes=60 * 1024 * 1024),
    )(psf_taps, coadd, rows)


def solution(mesh):
    placed = (
        P(("visit", "prow", "pcol"), None),
        P(("visit", "prow", "pcol"), None, None),
        P(("visit", "prow", "pcol"), None),
        P(("visit", "prow", "pcol"), None),
        P(("visit", "prow", "pcol"), None),
        P(("visit", "prow", "pcol")),
        P(("visit", "prow", "pcol")),
        P(),
    )
    return jax.shard_map(
        body,
        mesh=mesh,
        in_specs=placed,
        out_specs=(P("prow", "pcol"), P("prow", "pcol")),
        check_vma=False,
    )
```

```python
import math

import jax
import jax.numpy as jnp
from jax import lax
from jax.experimental import pallas as pl
from jax.experimental.pallas import tpu as pltpu
from jax.sharding import PartitionSpec as P

MESH = pl.DeviceIdType.MESH
NB = 8
S = 192
B = 128
KR = 15
RF = 8
NZ = 8
NY = 4
NP = 8
NPLANE = NY * NP
TILES = 512
LANES = 128
WIDTHS = (1.0, 2.0, 4.0)
TAPS = (-2, -1, 0, 1, 2, 3)
CHUNK = 264
PARTS = ((0, 64), (64, 64), (128, 64), (192, 64), (256, 8))
HALF = 64
BOTH_WAYS = (1, 7, 2, 6, 3, 5, 4)
BF = jnp.bfloat16
F32 = jnp.float32


def norms(width):
    lags = range(-KR, KR + 1)
    bell = math.sqrt(sum(math.exp(-((t / width) ** 2)) for t in lags))
    quad = math.sqrt(sum((t / width) ** 4 * math.exp(-((t / width) ** 2)) for t in lags))
    return bell, quad


def split(x):
    hi = x.astype(BF)
    return hi, (x - hi.astype(F32)).astype(BF)


def mm(a, b):
    return jnp.dot(a, b, preferred_element_type=F32)


def sinc(x):
    scaled = math.pi * x
    return jnp.where(x == 0.0, 1.0, jnp.sin(scaled) / jnp.where(x == 0.0, 1.0, scaled))


def lanczos_weights(shift):
    lane = lax.broadcasted_iota(jnp.int32, (NB, LANES), 1).astype(F32)
    x = lane + float(TAPS[0]) - shift
    return jnp.where(jnp.abs(x) < 3.0, sinc(x) * sinc(x / 3.0), 0.0)


def factor_rows(place, weights):
    bells = [jnp.zeros((NB, LANES), F32) for _ in WIDTHS]
    quads = [jnp.zeros((NB, LANES), F32) for _ in WIDTHS]
    for index, tap in enumerate(TAPS):
        lag = place - float(tap + KR)
        weight = jnp.where(jnp.abs(lag) <= float(KR), weights[:, index : index + 1], 0.0)
        for w, width in enumerate(WIDTHS):
            bell_norm, quad_norm = norms(width)
            ratio = lag * (1.0 / width)
            term = weight * jnp.exp(-0.5 * ratio * ratio)
            bells[w] = bells[w] + term * (1.0 / bell_norm)
            quads[w] = quads[w] + ratio * ratio * term * (1.0 / quad_norm)
    return bells, quads


def make_bases(coef_ref, off_ref, shift_ref, base_ref):
    row = lax.broadcasted_iota(jnp.int32, (NB, LANES), 0)

    def column(read):
        result = jnp.zeros((NB, LANES), F32)
        for b in range(NB):
            result = jnp.where(row == b, read(b).astype(F32), result)
        return result

    lane_int = lax.broadcasted_iota(jnp.int32, (NB, LANES), 1)
    lane = lane_int.astype(F32)
    col_weights = lanczos_weights(column(lambda b: shift_ref[1, b]))
    row_weights = lanczos_weights(column(lambda b: shift_ref[0, b]))
    place = jnp.where(lane_int == 0, 0.0, float(LANES) - lane)
    row_offset = column(lambda b: off_ref[0, b])
    bells, quads = factor_rows(place - column(lambda b: off_ref[1, b]), col_weights)
    for w in range(3):
        base_ref[2 * w] = bells[w]
        base_ref[2 * w + 1] = quads[w]
    coefs = [column(lambda b, i=i: coef_ref[b, i]) for i in range(9)]
    for d, delta in enumerate((0.0, -1.0, 1.0)):
        bells, quads = factor_rows(2.0 * lane + delta - row_offset, row_weights)
        for w in range(3):
            first, second, third = coefs[3 * w : 3 * w + 3]
            base_ref[6 + 6 * d + 2 * w] = first * bells[w] + second * quads[w]
            base_ref[6 + 6 * d + 2 * w + 1] = third * bells[w]


def skew(row, count):
    return pltpu.roll(jnp.broadcast_to(row, (count, LANES)), 0, 1, stride=1, stride_axis=0)


def warp_block(k, stamps_ref, base_ref, mh, ml, lh, ll, zb, flux_ref):
    r_iota = lax.broadcasted_iota(jnp.int32, (LANES, LANES), 0)
    c_iota = lax.broadcasted_iota(jnp.int32, (LANES, LANES), 1)
    lower = r_iota >= c_iota
    for j in range(6):
        cols = slice(j * LANES, (j + 1) * LANES)
        full = skew(base_ref[j, pl.ds(k, 1), :], LANES)
        hi, lo = split(jnp.where(lower, full, 0.0))
        mh[64:192, cols] = hi
        ml[64:192, cols] = lo
        hi, lo = split(jnp.where(lower[0:64], 0.0, full[0:64]))
        mh[192:256, cols] = hi
        ml[192:256, cols] = lo
        for d, spots in enumerate((((0, 0), (1, 1)), ((1, 0),), ((0, 1),))):
            hi, lo = split(skew(base_ref[6 + 6 * d + j, pl.ds(k, 1), :], 64))
            for e, f in spots:
                at = (f * 6 + j) * LANES
                lh[e * 64 : (e + 1) * 64, at : at + LANES] = hi
                ll[e * 64 : (e + 1) * 64, at : at + LANES] = lo
    rows_a = stamps_ref[pl.ds(k, 96, 24), :]
    rows_b = stamps_ref[pl.ds(8 + k, 96, 24), :]
    rows_c = stamps_ref[pl.ds(16 + k, 96, 24), :]
    for f, (left, right, start) in enumerate(((rows_a, rows_b, 64), (rows_b, rows_c, 0))):
        xh, xl = split(jnp.concatenate([left, right], axis=1))
        z = mm(xh, mh[start : start + 256, :]) + mm(xl, mh[start : start + 256, :])
        z = z + mm(xh, ml[start : start + 256, :])
        zh, zl = split(z)
        for j in range(6):
            at = (f * 6 + j) * LANES
            zb[at : at + 96, 0:LANES] = zh[:, j * LANES : (j + 1) * LANES]
            zb[at : at + 96, LANES : 2 * LANES] = zl[:, j * LANES : (j + 1) * LANES]
    both = mm(lh[...], zb[...])
    out = both[:, 0:LANES] + both[:, LANES:] + mm(ll[...], zb[:, 0:LANES])
    flux_ref[pl.ds(k, 128, 8), :] = out


def filter_blocks(taps_ref, transposed):
    r_iota = lax.broadcasted_iota(jnp.int32, (LANES, LANES), 0)
    c_iota = lax.broadcasted_iota(jnp.int32, (LANES, LANES), 1)
    lag = c_iota - r_iota if transposed else r_iota - c_iota
    result = []
    for shift in (-LANES, 0, LANES):
        band = jnp.zeros((LANES, LANES), F32)
        for tap in range(2 * RF + 1):
            band = jnp.where(lag + shift == tap - RF, taps_ref[tap], band)
        result.append(band)
    return result


def kernel(
    stamps_hbm, var_ref, coef_hbm, off_hbm, shift_hbm, dest_hbm, pos_hbm, taps_hbm,
    coadd_hbm, rows_hbm,
    coef_ref, off_ref, shift_ref, dest_ref, pos_ref, taps_ref,
    stamps_ref, base_ref, mh, ml, lh, ll, zb, flux_ref,
    ids_z, zw, zf, ids_in, weights, pack_w, pack_f, landed_w, landed_f, onehot, data,
    sums, msg, side_out, side_in, chunks, xbuf, ybuf, coadd_ref,
    seen, small_sem, local_sem, zw_send, zw_recv, zi_send, zi_recv, zf_send, zf_recv,
    id_send, id_recv, in_send, in_recv, side_send, side_recv, ret_send, ret_recv,
    ring_send, ring_recv, halo_send, halo_recv, out_sem,
):
    z = lax.axis_index("visit")
    y = lax.axis_index("prow")
    p = lax.axis_index("pcol")
    j = y * NP + p
    core = lax.rem(p, 2)
    small = [
        pltpu.make_async_copy(far, near, small_sem.at[i])
        for i, (far, near) in enumerate((
            (dest_hbm, dest_ref), (pos_hbm, pos_ref), (off_hbm, off_ref), (shift_hbm, shift_ref),
            (coef_hbm, coef_ref), (taps_hbm, taps_ref)))
    ]
    for copy in small:
        copy.start()
    fetch = pltpu.make_async_copy(stamps_hbm, stamps_ref, local_sem.at[0])
    fetch.start()

    later = []
    barrier = pltpu.get_barrier_semaphore()

    @pl.loop(1, NZ)
    def _(d):
        pl.semaphore_signal(barrier, inc=1, device_id=(lax.rem(z + d, NZ), y, p), device_id_type=MESH)

    @pl.loop(1, NY)
    def _(d):
        pl.semaphore_signal(barrier, inc=1, device_id=(z, lax.rem(y + d, NY), p), device_id_type=MESH)

    @pl.loop(1, NP)
    def _(d):
        pl.semaphore_signal(barrier, inc=1, device_id=(z, y, lax.rem(p + d, NP)), device_id_type=MESH)

    for copy in small:
        copy.wait()
    row_iota = lax.broadcasted_iota(jnp.int32, (NB, LANES), 0)
    ids = jnp.zeros((NB, LANES), F32)
    for b in range(NB):
        ids = jnp.where(row_iota == b, (dest_ref[b] * 16 + pos_ref[b]).astype(F32), ids)
    ids_z[z] = ids
    pl.semaphore_wait(barrier, NZ + NY + NP - 3)

    def z_ids(d):
        return pltpu.make_async_remote_copy(
            src_ref=ids_z.at[z], dst_ref=ids_z.at[z], send_sem=zi_send.at[d], recv_sem=zi_recv.at[z],
            device_id=(lax.rem(z + d, NZ), y, p), device_id_type=MESH)

    def z_var(d):
        to = lax.rem(z + d, NZ)
        return pltpu.make_async_remote_copy(
            src_ref=var_ref.at[:, pl.ds(pl.multiple_of(to * 16, 16), 16), :], dst_ref=zw.at[z],
            send_sem=zw_send.at[d], recv_sem=zw_recv.at[z], device_id=(to, y, p), device_id_type=MESH)

    def z_flux(e, d):
        to = lax.rem(z + d, NZ)
        return pltpu.make_async_remote_copy(
            src_ref=flux_ref.at[pl.ds(pl.multiple_of(e * 512 + to * 64, 64), 64), :], dst_ref=zf.at[e, z],
            send_sem=zf_send.at[e, d], recv_sem=zf_recv.at[e, z], device_id=(to, y, p), device_id_type=MESH)

    def wait_z(recv, dst):
        for d in range(1, NZ):
            source = lax.rem(z + d, NZ)
            pltpu.make_async_copy(dst.at[source], dst.at[source], recv.at[source]).wait()

    @pl.loop(1, NZ)
    def _(d):
        z_ids(d).start()

    for d in BOTH_WAYS:
        z_var(d).start()

    @later.append
    def _():
        @pl.loop(1, NZ)
        def _(d):
            z_ids(d).wait_send()
            z_var(d).wait_send()

    own_var = pltpu.make_async_copy(
        var_ref.at[:, pl.ds(pl.multiple_of(z * 16, 16), 16), :], zw.at[z], local_sem.at[1])
    own_var.start()

    @pl.loop(1, NY)
    def _(d):
        pl.semaphore_signal(seen, inc=1, device_id=(z, lax.rem(y + d, NY), p), device_id_type=MESH)

    make_bases(coef_ref, off_ref, shift_ref, base_ref)
    mh[0:64, :] = jnp.zeros((64, 6 * LANES), BF)
    ml[0:64, :] = jnp.zeros((64, 6 * LANES), BF)
    mh[256:320, :] = jnp.zeros((64, 6 * LANES), BF)
    ml[256:320, :] = jnp.zeros((64, 6 * LANES), BF)
    zb[...] = jnp.zeros(zb.shape, BF)
    fetch.wait()

    @pl.loop(0, NB)
    def _(k):
        warp_block(k, stamps_ref, base_ref, mh, ml, lh, ll, zb, flux_ref)

    pl.semaphore_wait(seen, NY - 1)

    for e in range(2):
        for d in BOTH_WAYS:
            z_flux(e, d).start()

    @later.append
    def _():
        @pl.loop(1, NZ)
        def _(d):
            for e in range(2):
                z_flux(e, d).wait_send()

    wait_z(zi_recv, ids_z)
    lane32 = lax.rem(lax.broadcasted_iota(jnp.int32, (32, LANES), 1), 32)
    row32 = lax.broadcasted_iota(jnp.int32, (32, LANES), 0)
    column_ids = ids_z[...].reshape(64, LANES)
    low_ids = jnp.sum(jnp.where(lane32 == row32, column_ids[0:32], 0.0), axis=0, keepdims=True)
    high_ids = jnp.sum(jnp.where(lane32 == row32, column_ids[32:64], 0.0), axis=0, keepdims=True)
    ids_in[j] = jnp.where(lax.broadcasted_iota(jnp.int32, (8, LANES), 0) == 0, low_ids, high_ids)

    def in_ids(d):
        other = lax.rem(j + d, NPLANE)
        return pltpu.make_async_remote_copy(
            src_ref=ids_in.at[j], dst_ref=ids_in.at[j], send_sem=id_send.at[d], recv_sem=id_recv.at[j],
            device_id=(z, other // NP, lax.rem(other, NP)), device_id_type=MESH)

    @pl.loop(1, NPLANE)
    def _(d):
        in_ids(d).start()

    @later.append
    def _():
        @pl.loop(1, NPLANE)
        def _(d):
            in_ids(d).wait_send()

    def in_copy(kind, e, chip):
        buf, land = ((pack_f, landed_f), (pack_w, landed_w))[kind]
        other = 2 * chip + e
        return pltpu.make_async_remote_copy(
            src_ref=buf.at[e, chip], dst_ref=land.at[j], send_sem=in_send.at[kind, other],
            recv_sem=in_recv.at[kind, j], device_id=(z, other // NP, lax.rem(other, NP)), device_id_type=MESH)

    @later.append
    def _():
        @pl.loop(0, 16)
        def _(chip):
            for e in range(2):

                @pl.when(2 * chip + e != j)
                def _():
                    in_copy(0, e, chip).wait_send()
                    in_copy(1, e, chip).wait_send()

    def send_rows(kind, e):
        buf, land = ((pack_f, landed_f), (pack_w, landed_w))[kind]

        @pl.loop(0, 16)
        def _(d):
            chip = lax.rem(j // 2 + d, 16)
            here = 2 * chip + e == j

            @pl.when(here)
            def _():
                pltpu.make_async_copy(buf.at[e, chip], land.at[j], in_recv.at[kind, j]).start()

            @pl.when(jnp.logical_not(here))
            def _():
                in_copy(kind, e, chip).start()

    def wait_rows(kind):
        land = (landed_f, landed_w)[kind]

        @pl.loop(0, NPLANE)
        def _(d):
            other = lax.rem(j + d, NPLANE)
            pltpu.make_async_copy(land.at[other], land.at[other], in_recv.at[kind, other]).wait()

    first64 = lax.broadcasted_iota(jnp.int32, (8, LANES), 1) < HALF

    def swap(x):
        return pltpu.roll(x, HALF, 1)

    def pack(buf, e, q, at, low, high):
        buf[e, 2 * q, at, :] = jnp.where(first64, low, swap(high))
        buf[e, 2 * q + 1, at, :] = jnp.where(first64, swap(low), high)

    wait_z(zw_recv, zw)
    own_var.wait()
    for s in range(4):
        low = 1.0 / jnp.swapaxes(zw[s], 0, 1)
        high = 1.0 / jnp.swapaxes(zw[s + 4], 0, 1)
        for row in range(16):
            weights[row, s] = low[row]
            weights[row, s + 4] = high[row]
            pack(pack_w, row % 2, row // 2, slice(8 * s, 8 * s + 8), low[row], high[row])
    send_rows(1, 0)
    send_rows(1, 1)

    @pl.loop(1, NPLANE)
    def _(d):
        other = lax.rem(j + d, NPLANE)
        pltpu.make_async_copy(ids_in.at[other], ids_in.at[other], id_recv.at[other]).wait()

    @pl.loop(0, 8)
    def _(group):
        quarter = lax.broadcasted_iota(jnp.int32, (8, LANES), 1) // 32
        mixed = ids_in[4 * group]
        for i in range(1, 4):
            mixed = jnp.where(quarter == i, ids_in[4 * group + i], mixed)
        tile = lax.broadcasted_iota(jnp.int32, (TILES, LANES), 0).astype(F32)
        at = pl.ds(pl.multiple_of(group * LANES, LANES), LANES)
        for h in range(2):
            onehot[h, :, at] = jnp.where(tile == mixed[h : h + 1], 1.0, 0.0).astype(BF)

    def tile_sums(land):
        hi, lo = split(land[...].reshape(NPLANE * 32, LANES))
        data[:, 0:LANES] = hi
        data[:, LANES:] = lo
        low = mm(onehot[0], data[...])
        high = mm(onehot[1], data[...])
        return low[:, 0:LANES] + low[:, LANES:] + pltpu.roll(high[:, 0:LANES] + high[:, LANES:], HALF, 1)

    col_blocks = jnp.concatenate(filter_blocks(taps_ref, False), axis=0)
    col_hi, col_lo = split(col_blocks)
    col_both = jnp.concatenate([col_hi, col_lo], axis=1)

    def relay(e):
        wait_z(zf_recv.at[e], zf.at[e])
        zf[e, z] = flux_ref[pl.ds(pl.multiple_of(e * 512 + z * 64, 64), 64), :]
        for s in range(4):
            for q in range(8):
                row = 2 * q + e
                low = zf[e, s, 8 * q : 8 * q + 8, :] * weights[row, s]
                high = zf[e, s + 4, 8 * q : 8 * q + 8, :] * weights[row, s + 4]
                pack(pack_f, e, q, slice(8 * s, 8 * s + 8), low, high)
        send_rows(0, e)

    wait_rows(1)
    sums[...] = 1.0 / (1.0 + tile_sums(landed_w))
    relay(0)
    relay(1)
    wait_rows(0)
    cells = (tile_sums(landed_f) * sums[...]).reshape(NPLANE, 2, 8, LANES)
    for o in range(NPLANE):
        msg[o] = jnp.where(first64, cells[o, 0], swap(cells[o, 1]))

    def ret_copy(o):
        return pltpu.make_async_remote_copy(
            src_ref=msg.at[o], dst_ref=chunks.at[z, pl.ds(pl.multiple_of(8 * j, 8), 8), :],
            send_sem=ret_send.at[o], recv_sem=ret_recv.at[j],
            device_id=(z, o // NP, lax.rem(o, NP)), device_id_type=MESH)

    pltpu.make_async_copy(
        msg.at[j], chunks.at[z, pl.ds(pl.multiple_of(8 * j, 8), 8), :], ret_recv.at[j]).start()

    @pl.loop(1, NPLANE)
    def _(d):
        ret_copy(lax.rem(j + d, NPLANE)).start()

    @later.append
    def _():
        @pl.loop(1, NPLANE)
        def _(d):
            ret_copy(lax.rem(j + d, NPLANE)).wait_send()

    def wait_ret(first, count):
        @pl.loop(first, first + count)
        def _(s):
            ref = chunks.at[z, pl.ds(pl.multiple_of(8 * s, 8), 8), :]
            pltpu.make_async_copy(ref, ref, ret_recv.at[s]).wait()

    def assembled(which):
        cell_rows = []
        for row in range(16):
            e, q = row % 2, row // 2
            one = chunks[which, 8 * (4 * q + e) : 8 * (4 * q + e) + 8, :]
            two = chunks[which, 8 * (4 * q + 2 + e) : 8 * (4 * q + 2 + e) + 8, :]
            cell_rows.append(jnp.concatenate(
                [jnp.where(first64, one, swap(two)), jnp.where(first64, swap(one), two)], axis=0)[None])
        return jnp.swapaxes(jnp.concatenate(cell_rows, axis=0), 0, 1)

    def side_copy(side):
        return pltpu.make_async_remote_copy(
            src_ref=side_out.at[side], dst_ref=side_in.at[1 - side], send_sem=side_send.at[side],
            recv_sem=side_recv.at[1 - side], device_id=(z, y, p - 1 + 2 * side), device_id_type=MESH)

    def beside(side):
        return p > 0 if side == 0 else p < NP - 1

    def send_sides(got):
        lane8 = lax.broadcasted_iota(jnp.int32, (8, LANES), 1)
        to_left = jnp.zeros((8, LANES), F32)
        to_right = jnp.zeros((8, LANES), F32)
        for g in range(8):
            rows = slice(8 * (g % 2), 8 * (g % 2) + 8)
            at = (8 + 16 * g) % LANES
            to_left = to_left + pltpu.roll(jnp.where(lane8 < RF, got[4 * (g // 2), rows, :], 0.0), at, 1)
            to_right = to_right + pltpu.roll(
                jnp.where(lane8 >= LANES - RF, got[4 * (g // 2) + 3, rows, :], 0.0), at, 1)
        side_out[0] = to_left
        side_out[1] = to_right
        for side in range(2):

            @pl.when(beside(side))
            def _():
                side_copy(side).start()

    @later.append
    def _():
        for side in range(2):

            @pl.when(beside(side))
            def _():
                side_copy(side).wait_send()


    def ring(way, step, part):
        back, hop = (step, 1) if step < 3 else (2, 2)
        which = lax.rem(z - back + NZ, NZ) if way == 0 else lax.rem(z + back, NZ)
        to = lax.rem(z + hop, NZ) if way == 0 else lax.rem(z + NZ - hop, NZ)
        at, size = PARTS[part]
        ref = chunks.at[which, pl.ds(at, size), :]
        return pltpu.make_async_remote_copy(
            src_ref=ref, dst_ref=ref, send_sem=ring_send.at[way, step, part],
            recv_sem=ring_recv.at[way, step, part], device_id=(to, y, p), device_id_type=MESH)

    def came(way, step, part):
        which = lax.rem(z - step - 1 + NZ, NZ) if way == 0 else lax.rem(z + step + 1, NZ)
        at, size = PARTS[part]
        ref = chunks.at[which, pl.ds(at, size), :]
        pltpu.make_async_copy(ref, ref, ring_recv.at[way, step, part]).wait()

    def halo(side, far):
        mine, theirs = (RF, 512 + RF) if side == 0 else (512, 0)
        return pltpu.make_async_remote_copy(
            src_ref=ybuf.at[pl.ds(mine, RF), :], dst_ref=ybuf.at[pl.ds(theirs, RF), :],
            send_sem=halo_send.at[side, far], recv_sem=halo_recv.at[1 - side],
            device_id=(lax.rem(z + 4 * far, NZ), y - 1 + 2 * side, p), device_id_type=MESH)

    def halo_goes(side, far):
        there = y > 0 if side == 0 else y < NY - 1
        first = 0 if side == 0 else NZ - 1
        return jnp.logical_and(there, z == first if far else z != (first + 4) % NZ)

    def filter_chunk(which):
        cells = assembled(which)
        packed = chunks[which, 256:264, :]
        lane8 = lax.broadcasted_iota(jnp.int32, (8, LANES), 1)
        for pr in range(4):
            beside = []
            for h in range(2):
                rolled = pltpu.roll(packed, (LANES - 8 - 16 * (2 * pr + h)) % LANES, 1)
                beside.append(jnp.where((lane8 < RF) | (lane8 >= LANES - RF), rolled, 0.0))
            beside = jnp.concatenate(beside, axis=0)
            tiles = [cells[4 * pr + pc] for pc in range(4)]
            at = pl.ds(pl.multiple_of(pr * 128 + which * 16, 16), 16)
            for pc in range(4):
                coadd_ref[at, pc * LANES : (pc + 1) * LANES] = tiles[pc]
            around = [beside, *tiles, beside]
            for pc in range(4):
                hi, lo = split(jnp.concatenate(around[pc : pc + 3], axis=1))
                xbuf[pc * 64 + pr * 16 : pc * 64 + pr * 16 + 16, :] = hi
                xbuf[256 + pc * 64 + pr * 16 : 256 + pc * 64 + pr * 16 + 16, :] = lo
        got = mm(xbuf[0:256, :], col_both)
        got = got[:, 0:LANES] + got[:, LANES:] + mm(xbuf[256:512, :], col_hi)
        for pc in range(4):
            for pr in range(4):
                at = pl.ds(pl.multiple_of(RF + pr * 128 + which * 16, 8), 16)
                ybuf[at, pc * LANES : (pc + 1) * LANES] = got[pc * 64 + pr * 16 : pc * 64 + pr * 16 + 16]

        for pr in range(4):
            at = pl.ds(pl.multiple_of(pr * 128 + which * 16, 16), 16)
            pltpu.make_async_copy(coadd_ref.at[at, :], coadd_hbm.at[at, :], out_sem.at[0]).start()
            at = pl.ds(pl.multiple_of(RF + pr * 128 + which * 16, 8), 16)
            pltpu.make_async_copy(ybuf.at[at, :], rows_hbm.at[at, :], out_sem.at[1]).start()

        for side, number in ((0, 0), (1, NZ - 1)):
            for far in range(2):

                @pl.when(jnp.logical_and(which == number, halo_goes(side, far)))
                def _():
                    halo(side, far).start()

    def passes(way, step, part):
        return step < 3 or (part < 2) == (way == 0)

    @later.append
    def _():
        for way in range(2):
            for step in range(4):
                for part in range(5):
                    if passes(way, step, part):
                        ring(way, step, part).wait_send()

    def advance(step, part):
        for way in range(2):
            if passes(way, step - 1, part):
                came(way, step - 1, part)
                if step == 2 and passes(way, 3, part):
                    ring(way, 3, part).start()
                if step < 3:
                    ring(way, step, part).start()

    for part in range(4):
        wait_ret(8 * part, 8)
        ring(0, 0, part).start()
        ring(1, 0, part).start()
    send_sides(assembled(z))
    chunks[z, 256:264, :] = jnp.zeros((8, LANES), F32)
    for side in range(2):

        @pl.when(beside(side))
        def _():
            side_copy(1 - side).wait_recv()
            chunks[z, 256:264, :] += side_in[side]

    ring(0, 0, 4).start()
    ring(1, 0, 4).start()
    for part in range(4):
        advance(1, part)
    filter_chunk(z)
    advance(1, 4)
    for part in range(4):
        advance(2, part)
    filter_chunk(lax.rem(z - 1 + NZ, NZ))
    advance(2, 4)
    filter_chunk(lax.rem(z + 1, NZ))
    filter_chunk(lax.rem(z - 2 + NZ, NZ))
    filter_chunk(lax.rem(z + 2, NZ))
    for part in range(5):
        advance(3, part)
    filter_chunk(lax.rem(z - 3 + NZ, NZ))
    filter_chunk(lax.rem(z + 3, NZ))
    for part in range(5):
        advance(4, part)
    filter_chunk(lax.rem(z + 4, NZ))

    for side in range(2):
        there = y > 0 if side == 0 else y < NY - 1
        at = pl.ds(0 if side == 0 else 512 + RF, RF)

        @pl.when(there)
        def _():
            halo(1 - side, 0).wait_recv()

        @pl.when(jnp.logical_not(there))
        def _():
            ybuf[at, :] = jnp.zeros((RF, 512), F32)

        pltpu.make_async_copy(ybuf.at[at, :], rows_hbm.at[at, :], out_sem.at[1]).start()

    @later.append
    def _():
        for side in range(2):
            for far in range(2):

                @pl.when(halo_goes(side, far))
                def _():
                    halo(side, far).wait_send()

    for left in later:
        left()
    pltpu.make_async_copy(coadd_ref, coadd_hbm, out_sem.at[0]).wait()
    pltpu.make_async_copy(ybuf, rows_hbm, out_sem.at[1]).wait()


def filter_rows(taps_hbm, cells_hbm, rows_hbm, coadd_hbm, det_hbm, taps_ref, rows_ref, cells_ref, det_ref, in_sem, out_sem):
    cells = pltpu.make_async_copy(cells_hbm, cells_ref, in_sem.at[5])
    pieces = []
    for t in range(4):
        at = pl.ds(t * 136, 136 if t < 3 else 120)
        pieces.append(pltpu.make_async_copy(rows_hbm.at[at, :], rows_ref.at[at, :], in_sem.at[t]))
    taps = pltpu.make_async_copy(taps_hbm, taps_ref, in_sem.at[4])
    for copy in (taps, *pieces, cells):
        copy.start()
    taps.wait()
    blocks = filter_blocks(taps_ref, True)
    band = jnp.concatenate([blocks[0][:, LANES - RF :], blocks[1], blocks[2][:, 0:RF]], axis=1)
    hi, lo = split(band)
    pieces[0].wait()
    results = []
    for t in range(4):
        if t < 3:
            pieces[t + 1].wait()
        yh, yl = split(rows_ref[t * 128 : t * 128 + 128 + 2 * RF, :])
        det_ref[t * 128 : (t + 1) * 128, :] = mm(hi, yh) + mm(hi, yl) + mm(lo, yh)
        at = pl.ds(t * 128, 128)
        results.append(pltpu.make_async_copy(det_ref.at[at, :], det_hbm.at[at, :], out_sem.at[t]))
        results[-1].start()
        if t == 1:
            cells.wait()
            results.append(pltpu.make_async_copy(cells_ref, coadd_hbm, out_sem.at[4]))
            results[-1].start()
    for copy in results:
        copy.wait()


def body(stamps, variance, coefficients, band_offsets, shifts, destination, position, psf_taps):
    cells = stamps.reshape(NB, S * S // LANES, LANES).transpose(1, 0, 2).reshape(NB * S * S // LANES, LANES)
    hbm = pl.BlockSpec(memory_space=pl.ANY)
    dma = pltpu.SemaphoreType.DMA
    scratch = [
        pltpu.SMEM((NB, 9), F32),
        pltpu.SMEM((2, NB), jnp.int32),
        pltpu.SMEM((2, NB), F32),
        pltpu.SMEM((NB,), jnp.int32),
        pltpu.SMEM((NB,), jnp.int32),
        pltpu.SMEM((2 * RF + 1,), F32),
        pltpu.VMEM((NB * S * S // LANES, LANES), F32),
        pltpu.VMEM((24, NB, LANES), F32),
        pltpu.VMEM((320, 768), BF),
        pltpu.VMEM((320, 768), BF),
        pltpu.VMEM((LANES, 12 * LANES), BF),
        pltpu.VMEM((LANES, 12 * LANES), BF),
        pltpu.VMEM((12 * LANES, 2 * LANES), BF),
        pltpu.VMEM((NB * LANES, LANES), F32),
        pltpu.VMEM((NZ, NB, LANES), F32),
        pltpu.VMEM((NZ, NB, 16, LANES), F32),
        pltpu.VMEM((2, NZ, 64, LANES), F32),
        pltpu.VMEM((NPLANE, 8, LANES), F32),
        pltpu.VMEM((16, NZ, NB, LANES), F32),
        pltpu.VMEM((2, 16, 32, LANES), F32),
        pltpu.VMEM((2, 16, 32, LANES), F32),
        pltpu.VMEM((NPLANE, 32, LANES), F32),
        pltpu.VMEM((NPLANE, 32, LANES), F32),
        pltpu.VMEM((2, TILES, NPLANE * 32), BF),
        pltpu.VMEM((NPLANE * 32, 2 * LANES), BF),
        pltpu.VMEM((TILES, LANES), F32),
        pltpu.VMEM((NPLANE, 8, LANES), F32),
        pltpu.VMEM((2, 8, LANES), F32),
        pltpu.VMEM((2, 8, LANES), F32),
        pltpu.VMEM((NZ, CHUNK, LANES), F32),
        pltpu.VMEM((512, 3 * LANES), BF),
        pltpu.VMEM((512 + 2 * RF, 512), F32),
        pltpu.VMEM((512, 512), F32),
        pltpu.SemaphoreType.REGULAR, dma((6,)), dma((2,)),
        dma((NZ,)), dma((NZ,)), dma((NZ,)), dma((NZ,)), dma((2, NZ)), dma((2, NZ)),
        dma((NPLANE,)), dma((NPLANE,)), dma((2, NPLANE)), dma((2, NPLANE)), dma((2,)), dma((2,)),
        dma((NPLANE,)), dma((NPLANE,)), dma((2, 4, 5)), dma((2, 4, 5)), dma((2, 2)), dma((2,)), dma((2,)),
    ]
    coadd, rows = pl.pallas_call(
        kernel,
        out_shape=(jax.ShapeDtypeStruct((512, 512), F32), jax.ShapeDtypeStruct((512 + 2 * RF, 512), F32)),
        in_specs=[hbm] * 8,
        out_specs=(hbm, hbm),
        scratch_shapes=scratch,
        compiler_params=pltpu.CompilerParams(
            collective_id=0, has_side_effects=True, vmem_limit_bytes=60 * 1024 * 1024),
    )(cells, variance, coefficients, band_offsets.T, shifts.T, destination, position, psf_taps)
    return pl.pallas_call(
        filter_rows,
        out_shape=(jax.ShapeDtypeStruct((512, 512), F32), jax.ShapeDtypeStruct((512, 512), F32)),
        in_specs=[hbm, hbm, hbm],
        out_specs=(hbm, hbm),
        scratch_shapes=[
            pltpu.SMEM((2 * RF + 1,), F32), pltpu.VMEM((512 + 2 * RF, 512), F32), pltpu.VMEM((512, 512), F32),
            pltpu.VMEM((512, 512), F32), dma((6,)), dma((5,))],
        compiler_params=pltpu.CompilerParams(vmem_limit_bytes=60 * 1024 * 1024),
    )(psf_taps, coadd, rows)


def solution(mesh):
    placed = (
        P(("visit", "prow", "pcol"), None),
        P(("visit", "prow", "pcol"), None, None),
        P(("visit", "prow", "pcol"), None),
        P(("visit", "prow", "pcol"), None),
        P(("visit", "prow", "pcol"), None),
        P(("visit", "prow", "pcol")),
        P(("visit", "prow", "pcol")),
        P(),
    )
    return jax.shard_map(
        body,
        mesh=mesh,
        in_specs=placed,
        out_specs=(P("prow", "pcol"), P("prow", "pcol")),
        check_vma=False,
    )
```

```python
import math

import jax
import jax.numpy as jnp
from jax import lax
from jax.experimental import pallas as pl
from jax.experimental.pallas import tpu as pltpu
from jax.sharding import PartitionSpec as P

MESH = pl.DeviceIdType.MESH
NB = 8
S = 192
B = 128
KR = 15
RF = 8
NZ = 8
NY = 4
NP = 8
NPLANE = NY * NP
TILES = 512
LANES = 128
WIDTHS = (1.0, 2.0, 4.0)
TAPS = (-2, -1, 0, 1, 2, 3)
CHUNK = 264
PARTS = ((0, 64), (64, 64), (128, 64), (192, 64), (256, 8))
HALF = 64
BOTH_WAYS = (1, 7, 2, 6, 3, 5, 4)
BF = jnp.bfloat16
F32 = jnp.float32


def norms(width):
    lags = range(-KR, KR + 1)
    bell = math.sqrt(sum(math.exp(-((t / width) ** 2)) for t in lags))
    quad = math.sqrt(sum((t / width) ** 4 * math.exp(-((t / width) ** 2)) for t in lags))
    return bell, quad


def split(x):
    hi = x.astype(BF)
    return hi, (x - hi.astype(F32)).astype(BF)


def mm(a, b):
    return jnp.dot(a, b, preferred_element_type=F32)


def sinc(x):
    scaled = math.pi * x
    return jnp.where(x == 0.0, 1.0, jnp.sin(scaled) / jnp.where(x == 0.0, 1.0, scaled))


def lanczos_weights(shift):
    lane = lax.broadcasted_iota(jnp.int32, (NB, LANES), 1).astype(F32)
    x = lane + float(TAPS[0]) - shift
    return jnp.where(jnp.abs(x) < 3.0, sinc(x) * sinc(x / 3.0), 0.0)


def factor_rows(place, weights):
    bells = [jnp.zeros((NB, LANES), F32) for _ in WIDTHS]
    quads = [jnp.zeros((NB, LANES), F32) for _ in WIDTHS]
    for index, tap in enumerate(TAPS):
        lag = place - float(tap + KR)
        weight = jnp.where(jnp.abs(lag) <= float(KR), weights[:, index : index + 1], 0.0)
        for w, width in enumerate(WIDTHS):
            bell_norm, quad_norm = norms(width)
            ratio = lag * (1.0 / width)
            term = weight * jnp.exp(-0.5 * ratio * ratio)
            bells[w] = bells[w] + term * (1.0 / bell_norm)
            quads[w] = quads[w] + ratio * ratio * term * (1.0 / quad_norm)
    return bells, quads


def make_bases(coef_ref, off_ref, shift_ref, base_ref):
    row = lax.broadcasted_iota(jnp.int32, (NB, LANES), 0)

    def column(read):
        result = jnp.zeros((NB, LANES), F32)
        for b in range(NB):
            result = jnp.where(row == b, read(b).astype(F32), result)
        return result

    lane_int = lax.broadcasted_iota(jnp.int32, (NB, LANES), 1)
    lane = lane_int.astype(F32)
    col_weights = lanczos_weights(column(lambda b: shift_ref[1, b]))
    row_weights = lanczos_weights(column(lambda b: shift_ref[0, b]))
    place = jnp.where(lane_int == 0, 0.0, float(LANES) - lane)
    row_offset = column(lambda b: off_ref[0, b])
    bells, quads = factor_rows(place - column(lambda b: off_ref[1, b]), col_weights)
    for w in range(3):
        base_ref[2 * w] = bells[w]
        base_ref[2 * w + 1] = quads[w]
    coefs = [column(lambda b, i=i: coef_ref[b, i]) for i in range(9)]
    for d, delta in enumerate((0.0, -1.0, 1.0)):
        bells, quads = factor_rows(2.0 * lane + delta - row_offset, row_weights)
        for w in range(3):
            first, second, third = coefs[3 * w : 3 * w + 3]
            base_ref[6 + 6 * d + 2 * w] = first * bells[w] + second * quads[w]
            base_ref[6 + 6 * d + 2 * w + 1] = third * bells[w]


def skew(row, count):
    return pltpu.roll(jnp.broadcast_to(row, (count, LANES)), 0, 1, stride=1, stride_axis=0)


def warp_block(k, stamps_ref, base_ref, mh, ml, lh, ll, zb, flux_ref):
    r_iota = lax.broadcasted_iota(jnp.int32, (LANES, LANES), 0)
    c_iota = lax.broadcasted_iota(jnp.int32, (LANES, LANES), 1)
    lower = r_iota >= c_iota
    for j in range(6):
        cols = slice(j * LANES, (j + 1) * LANES)
        full = skew(base_ref[j, pl.ds(k, 1), :], LANES)
        hi, lo = split(jnp.where(lower, full, 0.0))
        mh[64:192, cols] = hi
        ml[64:192, cols] = lo
        hi, lo = split(jnp.where(lower[0:64], 0.0, full[0:64]))
        mh[192:256, cols] = hi
        ml[192:256, cols] = lo
        for d, spots in enumerate((((0, 0), (1, 1)), ((1, 0),), ((0, 1),))):
            hi, lo = split(skew(base_ref[6 + 6 * d + j, pl.ds(k, 1), :], 64))
            for e, f in spots:
                at = (f * 6 + j) * LANES
                lh[e * 64 : (e + 1) * 64, at : at + LANES] = hi
                ll[e * 64 : (e + 1) * 64, at : at + LANES] = lo
    rows_a = stamps_ref[pl.ds(k, 96, 24), :]
    rows_b = stamps_ref[pl.ds(8 + k, 96, 24), :]
    rows_c = stamps_ref[pl.ds(16 + k, 96, 24), :]
    for f, (left, right, start) in enumerate(((rows_a, rows_b, 64), (rows_b, rows_c, 0))):
        xh, xl = split(jnp.concatenate([left, right], axis=1))
        z = mm(xh, mh[start : start + 256, :]) + mm(xl, mh[start : start + 256, :])
        z = z + mm(xh, ml[start : start + 256, :])
        zh, zl = split(z)
        for j in range(6):
            at = (f * 6 + j) * LANES
            zb[at : at + 96, 0:LANES] = zh[:, j * LANES : (j + 1) * LANES]
            zb[at : at + 96, LANES : 2 * LANES] = zl[:, j * LANES : (j + 1) * LANES]
    both = mm(lh[...], zb[...])
    out = both[:, 0:LANES] + both[:, LANES:] + mm(ll[...], zb[:, 0:LANES])
    flux_ref[pl.ds(k, 128, 8), :] = out


def filter_blocks(taps_ref, transposed):
    r_iota = lax.broadcasted_iota(jnp.int32, (LANES, LANES), 0)
    c_iota = lax.broadcasted_iota(jnp.int32, (LANES, LANES), 1)
    lag = c_iota - r_iota if transposed else r_iota - c_iota
    result = []
    for shift in (-LANES, 0, LANES):
        band = jnp.zeros((LANES, LANES), F32)
        for tap in range(2 * RF + 1):
            band = jnp.where(lag + shift == tap - RF, taps_ref[tap], band)
        result.append(band)
    return result


def kernel(
    stamps_hbm, var_ref, coef_hbm, off_hbm, shift_hbm, dest_hbm, pos_hbm, taps_hbm,
    coadd_hbm, rows_hbm,
    coef_ref, off_ref, shift_ref, dest_ref, pos_ref, taps_ref,
    stamps_ref, base_ref, mh, ml, lh, ll, zb, flux_ref,
    ids_z, zw, zf, ids_in, weights, pack_w, pack_f, landed_w, landed_f, onehot, data,
    sums, msg, side_out, side_in, chunks, xbuf, ybuf, coadd_ref,
    seen, small_sem, local_sem, zw_send, zw_recv, zi_send, zi_recv, zf_send, zf_recv,
    id_send, id_recv, in_send, in_recv, side_send, side_recv, ret_send, ret_recv,
    ring_send, ring_recv, halo_send, halo_recv, out_sem,
):
    z = lax.axis_index("visit")
    y = lax.axis_index("prow")
    p = lax.axis_index("pcol")
    j = y * NP + p
    core = lax.rem(p, 2)
    small = [
        pltpu.make_async_copy(far, near, small_sem.at[i])
        for i, (far, near) in enumerate((
            (dest_hbm, dest_ref), (pos_hbm, pos_ref), (off_hbm, off_ref), (shift_hbm, shift_ref),
            (coef_hbm, coef_ref), (taps_hbm, taps_ref)))
    ]
    for copy in small:
        copy.start()
    fetch = pltpu.make_async_copy(stamps_hbm, stamps_ref, local_sem.at[0])
    fetch.start()

    later = []
    barrier = pltpu.get_barrier_semaphore()

    @pl.loop(1, NZ)
    def _(d):
        pl.semaphore_signal(barrier, inc=1, device_id=(lax.rem(z + d, NZ), y, p), device_id_type=MESH)

    @pl.loop(1, NY)
    def _(d):
        pl.semaphore_signal(barrier, inc=1, device_id=(z, lax.rem(y + d, NY), p), device_id_type=MESH)

    @pl.loop(1, NP)
    def _(d):
        pl.semaphore_signal(barrier, inc=1, device_id=(z, y, lax.rem(p + d, NP)), device_id_type=MESH)

    for copy in small:
        copy.wait()
    row_iota = lax.broadcasted_iota(jnp.int32, (NB, LANES), 0)
    ids = jnp.zeros((NB, LANES), F32)
    for b in range(NB):
        ids = jnp.where(row_iota == b, (dest_ref[b] * 16 + pos_ref[b]).astype(F32), ids)
    ids_z[z] = ids
    pl.semaphore_wait(barrier, NZ + NY + NP - 3)

    def z_ids(d):
        return pltpu.make_async_remote_copy(
            src_ref=ids_z.at[z], dst_ref=ids_z.at[z], send_sem=zi_send, recv_sem=zi_recv,
            device_id=(lax.rem(z + d, NZ), y, p), device_id_type=MESH)

    def z_var(d):
        to = lax.rem(z + d, NZ)
        return pltpu.make_async_remote_copy(
            src_ref=var_ref.at[:, pl.ds(pl.multiple_of(to * 16, 16), 16), :], dst_ref=zw.at[z],
            send_sem=zw_send, recv_sem=zw_recv, device_id=(to, y, p), device_id_type=MESH)

    def z_flux(e, d):
        to = lax.rem(z + d, NZ)
        return pltpu.make_async_remote_copy(
            src_ref=flux_ref.at[pl.ds(pl.multiple_of(e * 512 + to * 64, 64), 64), :], dst_ref=zf.at[e, z],
            send_sem=zf_send, recv_sem=zf_recv.at[e], device_id=(to, y, p), device_id_type=MESH)

    def wait_bytes(ref, sem):
        pltpu.make_async_copy(ref, ref, sem).wait()

    def others(buf):
        return buf.at[pl.ds(0, NZ - 1)]

    @pl.loop(1, NZ)
    def _(d):
        z_ids(d).start()

    for d in BOTH_WAYS:
        z_var(d).start()

    @later.append
    def _():
        wait_bytes(others(ids_z), zi_send)
        wait_bytes(others(zw), zw_send)

    own_var = pltpu.make_async_copy(
        var_ref.at[:, pl.ds(pl.multiple_of(z * 16, 16), 16), :], zw.at[z], local_sem.at[1])
    own_var.start()

    @pl.loop(1, NY)
    def _(d):
        pl.semaphore_signal(seen, inc=1, device_id=(z, lax.rem(y + d, NY), p), device_id_type=MESH)

    make_bases(coef_ref, off_ref, shift_ref, base_ref)
    mh[0:64, :] = jnp.zeros((64, 6 * LANES), BF)
    ml[0:64, :] = jnp.zeros((64, 6 * LANES), BF)
    mh[256:320, :] = jnp.zeros((64, 6 * LANES), BF)
    ml[256:320, :] = jnp.zeros((64, 6 * LANES), BF)
    zb[...] = jnp.zeros(zb.shape, BF)
    fetch.wait()

    @pl.loop(0, NB)
    def _(k):
        warp_block(k, stamps_ref, base_ref, mh, ml, lh, ll, zb, flux_ref)

    pl.semaphore_wait(seen, NY - 1)

    for e in range(2):
        for d in BOTH_WAYS:
            z_flux(e, d).start()

    @later.append
    def _():
        wait_bytes(flux_ref.at[pl.ds(0, 2 * (NZ - 1) * 64), :], zf_send)

    wait_bytes(others(ids_z), zi_recv)
    lane32 = lax.rem(lax.broadcasted_iota(jnp.int32, (32, LANES), 1), 32)
    row32 = lax.broadcasted_iota(jnp.int32, (32, LANES), 0)
    column_ids = ids_z[...].reshape(64, LANES)
    low_ids = jnp.sum(jnp.where(lane32 == row32, column_ids[0:32], 0.0), axis=0, keepdims=True)
    high_ids = jnp.sum(jnp.where(lane32 == row32, column_ids[32:64], 0.0), axis=0, keepdims=True)
    ids_in[j] = jnp.where(lax.broadcasted_iota(jnp.int32, (8, LANES), 0) == 0, low_ids, high_ids)

    def in_ids(d):
        other = lax.rem(j + d, NPLANE)
        return pltpu.make_async_remote_copy(
            src_ref=ids_in.at[j], dst_ref=ids_in.at[j], send_sem=id_send, recv_sem=id_recv,
            device_id=(z, other // NP, lax.rem(other, NP)), device_id_type=MESH)

    @pl.loop(1, NPLANE)
    def _(d):
        in_ids(d).start()

    @later.append
    def _():
        wait_bytes(ids_in.at[pl.ds(0, NPLANE - 1)], id_send)

    def in_copy(kind, e, chip):
        buf, land = ((pack_f, landed_f), (pack_w, landed_w))[kind]
        other = 2 * chip + e
        return pltpu.make_async_remote_copy(
            src_ref=buf.at[e, chip], dst_ref=land.at[j], send_sem=in_send.at[kind],
            recv_sem=in_recv.at[kind], device_id=(z, other // NP, lax.rem(other, NP)), device_id_type=MESH)

    @later.append
    def _():
        wait_bytes(landed_f.at[pl.ds(0, NPLANE - 1)], in_send.at[0])
        wait_bytes(landed_w.at[pl.ds(0, NPLANE - 1)], in_send.at[1])

    def send_rows(kind, e):
        buf, land = ((pack_f, landed_f), (pack_w, landed_w))[kind]

        @pl.loop(0, 16)
        def _(d):
            chip = lax.rem(j // 2 + d, 16)
            here = 2 * chip + e == j

            @pl.when(here)
            def _():
                pltpu.make_async_copy(buf.at[e, chip], land.at[j], in_recv.at[kind]).start()

            @pl.when(jnp.logical_not(here))
            def _():
                in_copy(kind, e, chip).start()

    def wait_rows(kind):
        wait_bytes((landed_f, landed_w)[kind], in_recv.at[kind])

    first64 = lax.broadcasted_iota(jnp.int32, (8, LANES), 1) < HALF

    def swap(x):
        return pltpu.roll(x, HALF, 1)

    def pack(buf, e, q, at, low, high):
        buf[e, 2 * q, at, :] = jnp.where(first64, low, swap(high))
        buf[e, 2 * q + 1, at, :] = jnp.where(first64, swap(low), high)

    wait_bytes(others(zw), zw_recv)
    own_var.wait()
    for s in range(4):
        low = 1.0 / jnp.swapaxes(zw[s], 0, 1)
        high = 1.0 / jnp.swapaxes(zw[s + 4], 0, 1)
        for row in range(16):
            weights[row, s] = low[row]
            weights[row, s + 4] = high[row]
            pack(pack_w, row % 2, row // 2, slice(8 * s, 8 * s + 8), low[row], high[row])
    send_rows(1, 0)
    send_rows(1, 1)

    wait_bytes(ids_in.at[pl.ds(0, NPLANE - 1)], id_recv)

    @pl.loop(0, 8)
    def _(group):
        quarter = lax.broadcasted_iota(jnp.int32, (8, LANES), 1) // 32
        mixed = ids_in[4 * group]
        for i in range(1, 4):
            mixed = jnp.where(quarter == i, ids_in[4 * group + i], mixed)
        tile = lax.broadcasted_iota(jnp.int32, (TILES, LANES), 0).astype(F32)
        at = pl.ds(pl.multiple_of(group * LANES, LANES), LANES)
        for h in range(2):
            onehot[h, :, at] = jnp.where(tile == mixed[h : h + 1], 1.0, 0.0).astype(BF)

    def tile_sums(land):
        hi, lo = split(land[...].reshape(NPLANE * 32, LANES))
        data[:, 0:LANES] = hi
        data[:, LANES:] = lo
        low = mm(onehot[0], data[...])
        high = mm(onehot[1], data[...])
        return low[:, 0:LANES] + low[:, LANES:] + pltpu.roll(high[:, 0:LANES] + high[:, LANES:], HALF, 1)

    col_blocks = jnp.concatenate(filter_blocks(taps_ref, False), axis=0)
    col_hi, col_lo = split(col_blocks)
    col_both = jnp.concatenate([col_hi, col_lo], axis=1)

    def relay(e):
        wait_bytes(others(zf.at[e]), zf_recv.at[e])
        zf[e, z] = flux_ref[pl.ds(pl.multiple_of(e * 512 + z * 64, 64), 64), :]
        for s in range(4):
            for q in range(8):
                row = 2 * q + e
                low = zf[e, s, 8 * q : 8 * q + 8, :] * weights[row, s]
                high = zf[e, s + 4, 8 * q : 8 * q + 8, :] * weights[row, s + 4]
                pack(pack_f, e, q, slice(8 * s, 8 * s + 8), low, high)
        send_rows(0, e)

    wait_rows(1)
    sums[...] = 1.0 / (1.0 + tile_sums(landed_w))
    relay(0)
    relay(1)
    wait_rows(0)
    cells = (tile_sums(landed_f) * sums[...]).reshape(NPLANE, 2, 8, LANES)
    for o in range(NPLANE):
        msg[o] = jnp.where(first64, cells[o, 0], swap(cells[o, 1]))

    def ret_copy(o):
        return pltpu.make_async_remote_copy(
            src_ref=msg.at[o], dst_ref=chunks.at[z, pl.ds(pl.multiple_of(8 * j, 8), 8), :],
            send_sem=ret_send, recv_sem=ret_recv.at[y],
            device_id=(z, o // NP, lax.rem(o, NP)), device_id_type=MESH)

    pltpu.make_async_copy(
        msg.at[j], chunks.at[z, pl.ds(pl.multiple_of(8 * j, 8), 8), :], ret_recv.at[y]).start()

    @pl.loop(1, NPLANE)
    def _(d):
        ret_copy(lax.rem(j + d, NPLANE)).start()

    @later.append
    def _():
        wait_bytes(msg.at[pl.ds(0, NPLANE - 1)], ret_send)

    def assembled(which):
        cell_rows = []
        for row in range(16):
            e, q = row % 2, row // 2
            one = chunks[which, 8 * (4 * q + e) : 8 * (4 * q + e) + 8, :]
            two = chunks[which, 8 * (4 * q + 2 + e) : 8 * (4 * q + 2 + e) + 8, :]
            cell_rows.append(jnp.concatenate(
                [jnp.where(first64, one, swap(two)), jnp.where(first64, swap(one), two)], axis=0)[None])
        return jnp.swapaxes(jnp.concatenate(cell_rows, axis=0), 0, 1)

    def side_copy(side):
        return pltpu.make_async_remote_copy(
            src_ref=side_out.at[side], dst_ref=side_in.at[1 - side], send_sem=side_send.at[side],
            recv_sem=side_recv.at[1 - side], device_id=(z, y, p - 1 + 2 * side), device_id_type=MESH)

    def beside(side):
        return p > 0 if side == 0 else p < NP - 1

    def send_sides(got):
        lane8 = lax.broadcasted_iota(jnp.int32, (8, LANES), 1)
        to_left = jnp.zeros((8, LANES), F32)
        to_right = jnp.zeros((8, LANES), F32)
        for g in range(8):
            rows = slice(8 * (g % 2), 8 * (g % 2) + 8)
            at = (8 + 16 * g) % LANES
            to_left = to_left + pltpu.roll(jnp.where(lane8 < RF, got[4 * (g // 2), rows, :], 0.0), at, 1)
            to_right = to_right + pltpu.roll(
                jnp.where(lane8 >= LANES - RF, got[4 * (g // 2) + 3, rows, :], 0.0), at, 1)
        side_out[0] = to_left
        side_out[1] = to_right
        for side in range(2):

            @pl.when(beside(side))
            def _():
                side_copy(side).start()

    @later.append
    def _():
        for side in range(2):

            @pl.when(beside(side))
            def _():
                side_copy(side).wait_send()


    def ring_slot(way, step, part):
        return (3 * way + step) * 5 + part if step < 3 else 30 + part

    def ring(way, step, part):
        back, hop = (step, 1) if step < 3 else (2, 2)
        which = lax.rem(z - back + NZ, NZ) if way == 0 else lax.rem(z + back, NZ)
        to = lax.rem(z + hop, NZ) if way == 0 else lax.rem(z + NZ - hop, NZ)
        at, size = PARTS[part]
        ref = chunks.at[which, pl.ds(at, size), :]
        return pltpu.make_async_remote_copy(
            src_ref=ref, dst_ref=ref, send_sem=ring_send,
            recv_sem=ring_recv.at[ring_slot(way, step, part)], device_id=(to, y, p), device_id_type=MESH)

    def came(way, step, part):
        which = lax.rem(z - step - 1 + NZ, NZ) if way == 0 else lax.rem(z + step + 1, NZ)
        at, size = PARTS[part]
        ref = chunks.at[which, pl.ds(at, size), :]
        pltpu.make_async_copy(ref, ref, ring_recv.at[ring_slot(way, step, part)]).wait()

    def halo(side, far):
        mine, theirs = (RF, 512 + RF) if side == 0 else (512, 0)
        return pltpu.make_async_remote_copy(
            src_ref=ybuf.at[pl.ds(mine, RF), :], dst_ref=ybuf.at[pl.ds(theirs, RF), :],
            send_sem=halo_send.at[side, far], recv_sem=halo_recv.at[1 - side],
            device_id=(lax.rem(z + 4 * far, NZ), y - 1 + 2 * side, p), device_id_type=MESH)

    def halo_goes(side, far):
        there = y > 0 if side == 0 else y < NY - 1
        first = 0 if side == 0 else NZ - 1
        return jnp.logical_and(there, z == first if far else z != (first + 4) % NZ)

    def filter_chunk(which):
        cells = assembled(which)
        packed = chunks[which, 256:264, :]
        lane8 = lax.broadcasted_iota(jnp.int32, (8, LANES), 1)
        for pr in range(4):
            beside = []
            for h in range(2):
                rolled = pltpu.roll(packed, (LANES - 8 - 16 * (2 * pr + h)) % LANES, 1)
                beside.append(jnp.where((lane8 < RF) | (lane8 >= LANES - RF), rolled, 0.0))
            beside = jnp.concatenate(beside, axis=0)
            tiles = [cells[4 * pr + pc] for pc in range(4)]
            at = pl.ds(pl.multiple_of(pr * 128 + which * 16, 16), 16)
            for pc in range(4):
                coadd_ref[at, pc * LANES : (pc + 1) * LANES] = tiles[pc]
            around = [beside, *tiles, beside]
            for pc in range(4):
                hi, lo = split(jnp.concatenate(around[pc : pc + 3], axis=1))
                xbuf[pc * 64 + pr * 16 : pc * 64 + pr * 16 + 16, :] = hi
                xbuf[256 + pc * 64 + pr * 16 : 256 + pc * 64 + pr * 16 + 16, :] = lo
        got = mm(xbuf[0:256, :], col_both)
        got = got[:, 0:LANES] + got[:, LANES:] + mm(xbuf[256:512, :], col_hi)
        for pc in range(4):
            for pr in range(4):
                at = pl.ds(pl.multiple_of(RF + pr * 128 + which * 16, 8), 16)
                ybuf[at, pc * LANES : (pc + 1) * LANES] = got[pc * 64 + pr * 16 : pc * 64 + pr * 16 + 16]

        for pr in range(4):
            at = pl.ds(pl.multiple_of(pr * 128 + which * 16, 16), 16)
            pltpu.make_async_copy(coadd_ref.at[at, :], coadd_hbm.at[at, :], out_sem.at[0]).start()
            at = pl.ds(pl.multiple_of(RF + pr * 128 + which * 16, 8), 16)
            pltpu.make_async_copy(ybuf.at[at, :], rows_hbm.at[at, :], out_sem.at[1]).start()

        for side, number in ((0, 0), (1, NZ - 1)):
            for far in range(2):

                @pl.when(jnp.logical_and(which == number, halo_goes(side, far)))
                def _():
                    halo(side, far).start()

    def passes(way, step, part):
        return step < 3 or (part < 2) == (way == 0)

    @later.append
    def _():
        wait_bytes(others(chunks), ring_send)

    def advance(step, part):
        for way in range(2):
            if passes(way, step - 1, part):
                came(way, step - 1, part)
                if step == 2 and passes(way, 3, part):
                    ring(way, 3, part).start()
                if step < 3:
                    ring(way, step, part).start()

    for part in range(4):
        wait_bytes(chunks.at[z, pl.ds(64 * part, 64), :], ret_recv.at[part])
        ring(0, 0, part).start()
        ring(1, 0, part).start()
    send_sides(assembled(z))
    chunks[z, 256:264, :] = jnp.zeros((8, LANES), F32)
    for side in range(2):

        @pl.when(beside(side))
        def _():
            side_copy(1 - side).wait_recv()
            chunks[z, 256:264, :] += side_in[side]

    ring(0, 0, 4).start()
    ring(1, 0, 4).start()
    for part in range(4):
        advance(1, part)
    filter_chunk(z)
    advance(1, 4)
    for part in range(4):
        advance(2, part)
    filter_chunk(lax.rem(z - 1 + NZ, NZ))
    advance(2, 4)
    filter_chunk(lax.rem(z + 1, NZ))
    filter_chunk(lax.rem(z - 2 + NZ, NZ))
    filter_chunk(lax.rem(z + 2, NZ))
    for part in range(5):
        advance(3, part)
    filter_chunk(lax.rem(z - 3 + NZ, NZ))
    filter_chunk(lax.rem(z + 3, NZ))
    for part in range(5):
        advance(4, part)
    filter_chunk(lax.rem(z + 4, NZ))

    for side in range(2):
        there = y > 0 if side == 0 else y < NY - 1
        at = pl.ds(0 if side == 0 else 512 + RF, RF)

        @pl.when(there)
        def _():
            halo(1 - side, 0).wait_recv()

        @pl.when(jnp.logical_not(there))
        def _():
            ybuf[at, :] = jnp.zeros((RF, 512), F32)

        pltpu.make_async_copy(ybuf.at[at, :], rows_hbm.at[at, :], out_sem.at[1]).start()

    @later.append
    def _():
        for side in range(2):
            for far in range(2):

                @pl.when(halo_goes(side, far))
                def _():
                    halo(side, far).wait_send()

    for left in later:
        left()
    pltpu.make_async_copy(coadd_ref, coadd_hbm, out_sem.at[0]).wait()
    pltpu.make_async_copy(ybuf, rows_hbm, out_sem.at[1]).wait()


def filter_rows(taps_hbm, cells_hbm, rows_hbm, coadd_hbm, det_hbm, taps_ref, rows_ref, cells_ref, det_ref, in_sem, out_sem):
    cells = pltpu.make_async_copy(cells_hbm, cells_ref, in_sem.at[5])
    pieces = []
    for t in range(4):
        at = pl.ds(t * 136, 136 if t < 3 else 120)
        pieces.append(pltpu.make_async_copy(rows_hbm.at[at, :], rows_ref.at[at, :], in_sem.at[t]))
    taps = pltpu.make_async_copy(taps_hbm, taps_ref, in_sem.at[4])
    for copy in (taps, *pieces, cells):
        copy.start()
    taps.wait()
    blocks = filter_blocks(taps_ref, True)
    band = jnp.concatenate([blocks[0][:, LANES - RF :], blocks[1], blocks[2][:, 0:RF]], axis=1)
    hi, lo = split(band)
    pieces[0].wait()
    results = []
    for t in range(4):
        if t < 3:
            pieces[t + 1].wait()
        yh, yl = split(rows_ref[t * 128 : t * 128 + 128 + 2 * RF, :])
        det_ref[t * 128 : (t + 1) * 128, :] = mm(hi, yh) + mm(hi, yl) + mm(lo, yh)
        at = pl.ds(t * 128, 128)
        results.append(pltpu.make_async_copy(det_ref.at[at, :], det_hbm.at[at, :], out_sem.at[t]))
        results[-1].start()
        if t == 1:
            cells.wait()
            results.append(pltpu.make_async_copy(cells_ref, coadd_hbm, out_sem.at[4]))
            results[-1].start()
    for copy in results:
        copy.wait()


def body(stamps, variance, coefficients, band_offsets, shifts, destination, position, psf_taps):
    cells = stamps.reshape(NB, S * S // LANES, LANES).transpose(1, 0, 2).reshape(NB * S * S // LANES, LANES)
    hbm = pl.BlockSpec(memory_space=pl.ANY)
    dma = pltpu.SemaphoreType.DMA
    scratch = [
        pltpu.SMEM((NB, 9), F32),
        pltpu.SMEM((2, NB), jnp.int32),
        pltpu.SMEM((2, NB), F32),
        pltpu.SMEM((NB,), jnp.int32),
        pltpu.SMEM((NB,), jnp.int32),
        pltpu.SMEM((2 * RF + 1,), F32),
        pltpu.VMEM((NB * S * S // LANES, LANES), F32),
        pltpu.VMEM((24, NB, LANES), F32),
        pltpu.VMEM((320, 768), BF),
        pltpu.VMEM((320, 768), BF),
        pltpu.VMEM((LANES, 12 * LANES), BF),
        pltpu.VMEM((LANES, 12 * LANES), BF),
        pltpu.VMEM((12 * LANES, 2 * LANES), BF),
        pltpu.VMEM((NB * LANES, LANES), F32),
        pltpu.VMEM((NZ, NB, LANES), F32),
        pltpu.VMEM((NZ, NB, 16, LANES), F32),
        pltpu.VMEM((2, NZ, 64, LANES), F32),
        pltpu.VMEM((NPLANE, 8, LANES), F32),
        pltpu.VMEM((16, NZ, NB, LANES), F32),
        pltpu.VMEM((2, 16, 32, LANES), F32),
        pltpu.VMEM((2, 16, 32, LANES), F32),
        pltpu.VMEM((NPLANE, 32, LANES), F32),
        pltpu.VMEM((NPLANE, 32, LANES), F32),
        pltpu.VMEM((2, TILES, NPLANE * 32), BF),
        pltpu.VMEM((NPLANE * 32, 2 * LANES), BF),
        pltpu.VMEM((TILES, LANES), F32),
        pltpu.VMEM((NPLANE, 8, LANES), F32),
        pltpu.VMEM((2, 8, LANES), F32),
        pltpu.VMEM((2, 8, LANES), F32),
        pltpu.VMEM((NZ, CHUNK, LANES), F32),
        pltpu.VMEM((512, 3 * LANES), BF),
        pltpu.VMEM((512 + 2 * RF, 512), F32),
        pltpu.VMEM((512, 512), F32),
        pltpu.SemaphoreType.REGULAR, dma((6,)), dma((2,)),
        dma, dma, dma, dma, dma, dma((2,)),
        dma, dma, dma((2,)), dma((2,)), dma((2,)), dma((2,)),
        dma, dma((4,)), dma, dma((35,)), dma((2, 2)), dma((2,)), dma((2,)),
    ]
    coadd, rows = pl.pallas_call(
        kernel,
        out_shape=(jax.ShapeDtypeStruct((512, 512), F32), jax.ShapeDtypeStruct((512 + 2 * RF, 512), F32)),
        in_specs=[hbm] * 8,
        out_specs=(hbm, hbm),
        scratch_shapes=scratch,
        compiler_params=pltpu.CompilerParams(
            collective_id=0, has_side_effects=True, vmem_limit_bytes=60 * 1024 * 1024),
    )(cells, variance, coefficients, band_offsets.T, shifts.T, destination, position, psf_taps)
    return pl.pallas_call(
        filter_rows,
        out_shape=(jax.ShapeDtypeStruct((512, 512), F32), jax.ShapeDtypeStruct((512, 512), F32)),
        in_specs=[hbm, hbm, hbm],
        out_specs=(hbm, hbm),
        scratch_shapes=[
            pltpu.SMEM((2 * RF + 1,), F32), pltpu.VMEM((512 + 2 * RF, 512), F32), pltpu.VMEM((512, 512), F32),
            pltpu.VMEM((512, 512), F32), dma((6,)), dma((5,))],
        compiler_params=pltpu.CompilerParams(vmem_limit_bytes=60 * 1024 * 1024),
    )(psf_taps, coadd, rows)


def solution(mesh):
    placed = (
        P(("visit", "prow", "pcol"), None),
        P(("visit", "prow", "pcol"), None, None),
        P(("visit", "prow", "pcol"), None),
        P(("visit", "prow", "pcol"), None),
        P(("visit", "prow", "pcol"), None),
        P(("visit", "prow", "pcol")),
        P(("visit", "prow", "pcol")),
        P(),
    )
    return jax.shard_map(
        body,
        mesh=mesh,
        in_specs=placed,
        out_specs=(P("prow", "pcol"), P("prow", "pcol")),
        check_vma=False,
    )
```

```python
import math

import jax
import jax.numpy as jnp
from jax import lax
from jax.experimental import pallas as pl
from jax.experimental.pallas import tpu as pltpu
from jax.sharding import PartitionSpec as P

MESH = pl.DeviceIdType.MESH
NB = 8
S = 192
B = 128
KR = 15
RF = 8
NZ = 8
NY = 4
NP = 8
NPLANE = NY * NP
TILES = 512
LANES = 128
WIDTHS = (1.0, 2.0, 4.0)
TAPS = (-2, -1, 0, 1, 2, 3)
CHUNK = 264
PARTS = ((0, 64), (64, 64), (128, 64), (192, 64), (256, 8))
HALF = 64
BOTH_WAYS = (1, 7, 2, 6, 3, 5, 4)
BF = jnp.bfloat16
F32 = jnp.float32


def norms(width):
    lags = range(-KR, KR + 1)
    bell = math.sqrt(sum(math.exp(-((t / width) ** 2)) for t in lags))
    quad = math.sqrt(sum((t / width) ** 4 * math.exp(-((t / width) ** 2)) for t in lags))
    return bell, quad


def split(x):
    hi = x.astype(BF)
    return hi, (x - hi.astype(F32)).astype(BF)


def mm(a, b):
    return jnp.dot(a, b, preferred_element_type=F32)


def sinc(x):
    scaled = math.pi * x
    return jnp.where(x == 0.0, 1.0, jnp.sin(scaled) / jnp.where(x == 0.0, 1.0, scaled))


def lanczos_weights(shift):
    lane = lax.broadcasted_iota(jnp.int32, (NB, LANES), 1).astype(F32)
    x = lane + float(TAPS[0]) - shift
    return jnp.where(jnp.abs(x) < 3.0, sinc(x) * sinc(x / 3.0), 0.0)


def factor_rows(place, weights):
    bells = [jnp.zeros((NB, LANES), F32) for _ in WIDTHS]
    quads = [jnp.zeros((NB, LANES), F32) for _ in WIDTHS]
    for index, tap in enumerate(TAPS):
        lag = place - float(tap + KR)
        weight = jnp.where(jnp.abs(lag) <= float(KR), weights[:, index : index + 1], 0.0)
        for w, width in enumerate(WIDTHS):
            bell_norm, quad_norm = norms(width)
            ratio = lag * (1.0 / width)
            term = weight * jnp.exp(-0.5 * ratio * ratio)
            bells[w] = bells[w] + term * (1.0 / bell_norm)
            quads[w] = quads[w] + ratio * ratio * term * (1.0 / quad_norm)
    return bells, quads


def make_bases(coef_ref, off_ref, shift_ref, base_ref):
    row = lax.broadcasted_iota(jnp.int32, (NB, LANES), 0)

    def column(read):
        result = jnp.zeros((NB, LANES), F32)
        for b in range(NB):
            result = jnp.where(row == b, read(b).astype(F32), result)
        return result

    lane_int = lax.broadcasted_iota(jnp.int32, (NB, LANES), 1)
    lane = lane_int.astype(F32)
    col_weights = lanczos_weights(column(lambda b: shift_ref[1, b]))
    row_weights = lanczos_weights(column(lambda b: shift_ref[0, b]))
    place = jnp.where(lane_int == 0, 0.0, float(LANES) - lane)
    row_offset = column(lambda b: off_ref[0, b])
    bells, quads = factor_rows(place - column(lambda b: off_ref[1, b]), col_weights)
    for w in range(3):
        base_ref[2 * w] = bells[w]
        base_ref[2 * w + 1] = quads[w]
    coefs = [column(lambda b, i=i: coef_ref[b, i]) for i in range(9)]
    for d, delta in enumerate((0.0, -1.0, 1.0)):
        bells, quads = factor_rows(2.0 * lane + delta - row_offset, row_weights)
        for w in range(3):
            first, second, third = coefs[3 * w : 3 * w + 3]
            base_ref[6 + 6 * d + 2 * w] = first * bells[w] + second * quads[w]
            base_ref[6 + 6 * d + 2 * w + 1] = third * bells[w]


def skew(row, count):
    return pltpu.roll(jnp.broadcast_to(row, (count, LANES)), 0, 1, stride=1, stride_axis=0)


def warp_block(k, stamps_ref, base_ref, mh, ml, lh, ll, zb, flux_ref):
    r_iota = lax.broadcasted_iota(jnp.int32, (LANES, LANES), 0)
    c_iota = lax.broadcasted_iota(jnp.int32, (LANES, LANES), 1)
    lower = r_iota >= c_iota
    for j in range(6):
        cols = slice(j * LANES, (j + 1) * LANES)
        full = skew(base_ref[j, pl.ds(k, 1), :], LANES)
        hi, lo = split(jnp.where(lower, full, 0.0))
        mh[64:192, cols] = hi
        ml[64:192, cols] = lo
        hi, lo = split(jnp.where(lower[0:64], 0.0, full[0:64]))
        mh[192:256, cols] = hi
        ml[192:256, cols] = lo
        for d, spots in enumerate((((0, 0), (1, 1)), ((1, 0),), ((0, 1),))):
            hi, lo = split(skew(base_ref[6 + 6 * d + j, pl.ds(k, 1), :], 64))
            for e, f in spots:
                at = (f * 6 + j) * LANES
                lh[e * 64 : (e + 1) * 64, at : at + LANES] = hi
                ll[e * 64 : (e + 1) * 64, at : at + LANES] = lo
    rows_a = stamps_ref[pl.ds(k, 96, 24), :]
    rows_b = stamps_ref[pl.ds(8 + k, 96, 24), :]
    rows_c = stamps_ref[pl.ds(16 + k, 96, 24), :]
    for f, (left, right, start) in enumerate(((rows_a, rows_b, 64), (rows_b, rows_c, 0))):
        xh, xl = split(jnp.concatenate([left, right], axis=1))
        z = mm(xh, mh[start : start + 256, :]) + mm(xl, mh[start : start + 256, :])
        z = z + mm(xh, ml[start : start + 256, :])
        zh, zl = split(z)
        for j in range(6):
            at = (f * 6 + j) * LANES
            zb[at : at + 96, 0:LANES] = zh[:, j * LANES : (j + 1) * LANES]
            zb[at : at + 96, LANES : 2 * LANES] = zl[:, j * LANES : (j + 1) * LANES]
    both = mm(lh[...], zb[...])
    out = both[:, 0:LANES] + both[:, LANES:] + mm(ll[...], zb[:, 0:LANES])
    flux_ref[pl.ds(k, 128, 8), :] = out


def filter_blocks(taps_ref, transposed):
    r_iota = lax.broadcasted_iota(jnp.int32, (LANES, LANES), 0)
    c_iota = lax.broadcasted_iota(jnp.int32, (LANES, LANES), 1)
    lag = c_iota - r_iota if transposed else r_iota - c_iota
    result = []
    for shift in (-LANES, 0, LANES):
        band = jnp.zeros((LANES, LANES), F32)
        for tap in range(2 * RF + 1):
            band = jnp.where(lag + shift == tap - RF, taps_ref[tap], band)
        result.append(band)
    return result


def kernel(
    stamps_hbm, var_ref, coef_hbm, off_hbm, shift_hbm, dest_hbm, pos_hbm, taps_hbm,
    coadd_hbm, rows_hbm,
    coef_ref, off_ref, shift_ref, dest_ref, pos_ref, taps_ref,
    stamps_ref, base_ref, mh, ml, lh, ll, zb, flux_ref,
    ids_z, zw, zf, ids_in, weights, pack_w, pack_f, landed_w, landed_f, onehot, data,
    sums, msg, side_out, side_in, chunks, xbuf, ybuf, coadd_ref,
    seen, small_sem, local_sem, zw_send, zw_recv, zi_send, zi_recv, zf_send, zf_recv,
    id_send, id_recv, in_send, in_recv, side_send, side_recv, ret_send, ret_recv,
    ring_send, ring_recv, halo_send, halo_recv, out_sem,
):
    z = lax.axis_index("visit")
    y = lax.axis_index("prow")
    p = lax.axis_index("pcol")
    j = y * NP + p
    core = lax.rem(p, 2)
    small = [
        pltpu.make_async_copy(far, near, small_sem.at[i])
        for i, (far, near) in enumerate((
            (dest_hbm, dest_ref), (pos_hbm, pos_ref), (off_hbm, off_ref), (shift_hbm, shift_ref),
            (coef_hbm, coef_ref), (taps_hbm, taps_ref)))
    ]
    for copy in small:
        copy.start()
    fetch = pltpu.make_async_copy(stamps_hbm, stamps_ref, local_sem.at[0])
    fetch.start()

    later = []
    barrier = pltpu.get_barrier_semaphore()

    @pl.loop(1, NZ)
    def _(d):
        pl.semaphore_signal(barrier, inc=1, device_id=(lax.rem(z + d, NZ), y, p), device_id_type=MESH)

    @pl.loop(1, NY)
    def _(d):
        pl.semaphore_signal(barrier, inc=1, device_id=(z, lax.rem(y + d, NY), p), device_id_type=MESH)

    @pl.loop(1, NP)
    def _(d):
        pl.semaphore_signal(barrier, inc=1, device_id=(z, y, lax.rem(p + d, NP)), device_id_type=MESH)

    for copy in small:
        copy.wait()
    row_iota = lax.broadcasted_iota(jnp.int32, (NB, LANES), 0)
    ids = jnp.zeros((NB, LANES), F32)
    for b in range(NB):
        ids = jnp.where(row_iota == b, (dest_ref[b] * 16 + pos_ref[b]).astype(F32), ids)
    ids_z[z] = ids
    pl.semaphore_wait(barrier, NZ + NY + NP - 3)

    def z_ids(d):
        return pltpu.make_async_remote_copy(
            src_ref=ids_z.at[z], dst_ref=ids_z.at[z], send_sem=zi_send, recv_sem=zi_recv,
            device_id=(lax.rem(z + d, NZ), y, p), device_id_type=MESH)

    def z_var(d):
        to = lax.rem(z + d, NZ)
        return pltpu.make_async_remote_copy(
            src_ref=var_ref.at[:, pl.ds(pl.multiple_of(to * 16, 16), 16), :], dst_ref=zw.at[z],
            send_sem=zw_send, recv_sem=zw_recv, device_id=(to, y, p), device_id_type=MESH)

    def z_flux(e, d):
        to = lax.rem(z + d, NZ)
        return pltpu.make_async_remote_copy(
            src_ref=flux_ref.at[pl.ds(pl.multiple_of(e * 512 + to * 64, 64), 64), :], dst_ref=zf.at[e, z],
            send_sem=zf_send, recv_sem=zf_recv.at[e], device_id=(to, y, p), device_id_type=MESH)

    def wait_bytes(ref, sem):
        pltpu.make_async_copy(ref, ref, sem).wait()

    def others(buf):
        return buf.at[pl.ds(0, NZ - 1)]

    @pl.loop(1, NZ)
    def _(d):
        z_ids(d).start()

    for d in BOTH_WAYS:
        z_var(d).start()

    @later.append
    def _():
        wait_bytes(others(ids_z), zi_send)
        wait_bytes(others(zw), zw_send)

    own_var = pltpu.make_async_copy(
        var_ref.at[:, pl.ds(pl.multiple_of(z * 16, 16), 16), :], zw.at[z], local_sem.at[1])
    own_var.start()

    @pl.loop(1, NY)
    def _(d):
        pl.semaphore_signal(seen, inc=1, device_id=(z, lax.rem(y + d, NY), p), device_id_type=MESH)

    make_bases(coef_ref, off_ref, shift_ref, base_ref)
    mh[0:64, :] = jnp.zeros((64, 6 * LANES), BF)
    ml[0:64, :] = jnp.zeros((64, 6 * LANES), BF)
    mh[256:320, :] = jnp.zeros((64, 6 * LANES), BF)
    ml[256:320, :] = jnp.zeros((64, 6 * LANES), BF)
    zb[...] = jnp.zeros(zb.shape, BF)
    fetch.wait()

    @pl.loop(0, NB)
    def _(k):
        warp_block(k, stamps_ref, base_ref, mh, ml, lh, ll, zb, flux_ref)

    pl.semaphore_wait(seen, NY - 1)

    for e in range(2):
        for d in BOTH_WAYS:
            z_flux(e, d).start()

    @later.append
    def _():
        wait_bytes(flux_ref.at[pl.ds(0, 2 * (NZ - 1) * 64), :], zf_send)

    wait_bytes(others(ids_z), zi_recv)
    lane32 = lax.rem(lax.broadcasted_iota(jnp.int32, (32, LANES), 1), 32)
    row32 = lax.broadcasted_iota(jnp.int32, (32, LANES), 0)
    column_ids = ids_z[...].reshape(64, LANES)
    low_ids = jnp.sum(jnp.where(lane32 == row32, column_ids[0:32], 0.0), axis=0, keepdims=True)
    high_ids = jnp.sum(jnp.where(lane32 == row32, column_ids[32:64], 0.0), axis=0, keepdims=True)
    ids_in[j] = jnp.where(lax.broadcasted_iota(jnp.int32, (8, LANES), 0) == 0, low_ids, high_ids)

    def in_ids(d):
        other = lax.rem(j + d, NPLANE)
        return pltpu.make_async_remote_copy(
            src_ref=ids_in.at[j], dst_ref=ids_in.at[j], send_sem=id_send, recv_sem=id_recv,
            device_id=(z, other // NP, lax.rem(other, NP)), device_id_type=MESH)

    @pl.loop(1, NPLANE)
    def _(d):
        in_ids(d).start()

    @later.append
    def _():
        wait_bytes(ids_in.at[pl.ds(0, NPLANE - 1)], id_send)

    def in_copy(kind, e, chip):
        buf, land = ((pack_f, landed_f), (pack_w, landed_w))[kind]
        other = 2 * chip + e
        return pltpu.make_async_remote_copy(
            src_ref=buf.at[e, chip], dst_ref=land.at[j], send_sem=in_send.at[kind],
            recv_sem=in_recv.at[kind], device_id=(z, other // NP, lax.rem(other, NP)), device_id_type=MESH)

    @later.append
    def _():
        wait_bytes(landed_f.at[pl.ds(0, NPLANE - 1)], in_send.at[0])
        wait_bytes(landed_w.at[pl.ds(0, NPLANE - 1)], in_send.at[1])

    def send_rows(kind, e):
        buf, land = ((pack_f, landed_f), (pack_w, landed_w))[kind]

        @pl.loop(0, 16)
        def _(d):
            chip = lax.rem(j // 2 + d, 16)
            here = 2 * chip + e == j

            @pl.when(here)
            def _():
                pltpu.make_async_copy(buf.at[e, chip], land.at[j], in_recv.at[kind]).start()

            @pl.when(jnp.logical_not(here))
            def _():
                in_copy(kind, e, chip).start()

    def wait_rows(kind):
        wait_bytes((landed_f, landed_w)[kind], in_recv.at[kind])

    first64 = lax.broadcasted_iota(jnp.int32, (8, LANES), 1) < HALF

    def swap(x):
        return pltpu.roll(x, HALF, 1)

    def pack(buf, e, q, at, low, high):
        buf[e, 2 * q, at, :] = jnp.where(first64, low, swap(high))
        buf[e, 2 * q + 1, at, :] = jnp.where(first64, swap(low), high)

    wait_bytes(others(zw), zw_recv)
    own_var.wait()
    for s in range(4):
        low = 1.0 / jnp.swapaxes(zw[s], 0, 1)
        high = 1.0 / jnp.swapaxes(zw[s + 4], 0, 1)
        for row in range(16):
            weights[row, s] = low[row]
            weights[row, s + 4] = high[row]
            pack(pack_w, row % 2, row // 2, slice(8 * s, 8 * s + 8), low[row], high[row])
    send_rows(1, 0)
    send_rows(1, 1)

    wait_bytes(ids_in.at[pl.ds(0, NPLANE - 1)], id_recv)

    @pl.loop(0, 8)
    def _(group):
        quarter = lax.broadcasted_iota(jnp.int32, (8, LANES), 1) // 32
        mixed = ids_in[4 * group]
        for i in range(1, 4):
            mixed = jnp.where(quarter == i, ids_in[4 * group + i], mixed)
        tile = lax.broadcasted_iota(jnp.int32, (TILES, LANES), 0).astype(F32)
        at = pl.ds(pl.multiple_of(group * LANES, LANES), LANES)
        for h in range(2):
            onehot[h, :, at] = jnp.where(tile == mixed[h : h + 1], 1.0, 0.0).astype(BF)

    def tile_sums(land):
        hi, lo = split(land[...].reshape(NPLANE * 32, LANES))
        data[:, 0:LANES] = hi
        data[:, LANES:] = lo
        low = mm(onehot[0], data[...])
        high = mm(onehot[1], data[...])
        return low[:, 0:LANES] + low[:, LANES:] + pltpu.roll(high[:, 0:LANES] + high[:, LANES:], HALF, 1)

    col_blocks = jnp.concatenate(filter_blocks(taps_ref, False), axis=0)
    col_hi, col_lo = split(col_blocks)
    col_both = jnp.concatenate([col_hi, col_lo], axis=1)

    def relay(e):
        wait_bytes(others(zf.at[e]), zf_recv.at[e])
        zf[e, z] = flux_ref[pl.ds(pl.multiple_of(e * 512 + z * 64, 64), 64), :]
        for s in range(4):
            for q in range(8):
                row = 2 * q + e
                low = zf[e, s, 8 * q : 8 * q + 8, :] * weights[row, s]
                high = zf[e, s + 4, 8 * q : 8 * q + 8, :] * weights[row, s + 4]
                pack(pack_f, e, q, slice(8 * s, 8 * s + 8), low, high)
        send_rows(0, e)

    relay(0)
    wait_rows(1)
    sums[...] = 1.0 / (1.0 + tile_sums(landed_w))
    relay(1)
    wait_rows(0)
    cells = (tile_sums(landed_f) * sums[...]).reshape(NPLANE, 2, 8, LANES)
    for o in range(NPLANE):
        msg[o] = jnp.where(first64, cells[o, 0], swap(cells[o, 1]))

    def ret_copy(o):
        return pltpu.make_async_remote_copy(
            src_ref=msg.at[o], dst_ref=chunks.at[z, pl.ds(pl.multiple_of(8 * j, 8), 8), :],
            send_sem=ret_send, recv_sem=ret_recv.at[y],
            device_id=(z, o // NP, lax.rem(o, NP)), device_id_type=MESH)

    pltpu.make_async_copy(
        msg.at[j], chunks.at[z, pl.ds(pl.multiple_of(8 * j, 8), 8), :], ret_recv.at[y]).start()

    @pl.loop(1, NPLANE)
    def _(d):
        ret_copy(lax.rem(j + d, NPLANE)).start()

    @later.append
    def _():
        wait_bytes(msg.at[pl.ds(0, NPLANE - 1)], ret_send)

    def assembled(which):
        cell_rows = []
        for row in range(16):
            e, q = row % 2, row // 2
            one = chunks[which, 8 * (4 * q + e) : 8 * (4 * q + e) + 8, :]
            two = chunks[which, 8 * (4 * q + 2 + e) : 8 * (4 * q + 2 + e) + 8, :]
            cell_rows.append(jnp.concatenate(
                [jnp.where(first64, one, swap(two)), jnp.where(first64, swap(one), two)], axis=0)[None])
        return jnp.swapaxes(jnp.concatenate(cell_rows, axis=0), 0, 1)

    def side_copy(side):
        return pltpu.make_async_remote_copy(
            src_ref=side_out.at[side], dst_ref=side_in.at[1 - side], send_sem=side_send.at[side],
            recv_sem=side_recv.at[1 - side], device_id=(z, y, p - 1 + 2 * side), device_id_type=MESH)

    def beside(side):
        return p > 0 if side == 0 else p < NP - 1

    def send_sides(got):
        lane8 = lax.broadcasted_iota(jnp.int32, (8, LANES), 1)
        to_left = jnp.zeros((8, LANES), F32)
        to_right = jnp.zeros((8, LANES), F32)
        for g in range(8):
            rows = slice(8 * (g % 2), 8 * (g % 2) + 8)
            at = (8 + 16 * g) % LANES
            to_left = to_left + pltpu.roll(jnp.where(lane8 < RF, got[4 * (g // 2), rows, :], 0.0), at, 1)
            to_right = to_right + pltpu.roll(
                jnp.where(lane8 >= LANES - RF, got[4 * (g // 2) + 3, rows, :], 0.0), at, 1)
        side_out[0] = to_left
        side_out[1] = to_right
        for side in range(2):

            @pl.when(beside(side))
            def _():
                side_copy(side).start()

    @later.append
    def _():
        for side in range(2):

            @pl.when(beside(side))
            def _():
                side_copy(side).wait_send()


    def ring_slot(way, step, part):
        return (3 * way + step) * 5 + part if step < 3 else 30 + part

    def ring(way, step, part):
        back, hop = (step, 1) if step < 3 else (2, 2)
        which = lax.rem(z - back + NZ, NZ) if way == 0 else lax.rem(z + back, NZ)
        to = lax.rem(z + hop, NZ) if way == 0 else lax.rem(z + NZ - hop, NZ)
        at, size = PARTS[part]
        ref = chunks.at[which, pl.ds(at, size), :]
        return pltpu.make_async_remote_copy(
            src_ref=ref, dst_ref=ref, send_sem=ring_send,
            recv_sem=ring_recv.at[ring_slot(way, step, part)], device_id=(to, y, p), device_id_type=MESH)

    def came(way, step, part):
        which = lax.rem(z - step - 1 + NZ, NZ) if way == 0 else lax.rem(z + step + 1, NZ)
        at, size = PARTS[part]
        ref = chunks.at[which, pl.ds(at, size), :]
        pltpu.make_async_copy(ref, ref, ring_recv.at[ring_slot(way, step, part)]).wait()

    def halo(side, far):
        mine, theirs = (RF, 512 + RF) if side == 0 else (512, 0)
        return pltpu.make_async_remote_copy(
            src_ref=ybuf.at[pl.ds(mine, RF), :], dst_ref=ybuf.at[pl.ds(theirs, RF), :],
            send_sem=halo_send.at[side, far], recv_sem=halo_recv.at[1 - side],
            device_id=(lax.rem(z + 4 * far, NZ), y - 1 + 2 * side, p), device_id_type=MESH)

    def halo_goes(side, far):
        there = y > 0 if side == 0 else y < NY - 1
        first = 0 if side == 0 else NZ - 1
        return jnp.logical_and(there, z == first if far else z != (first + 4) % NZ)

    def filter_chunk(which):
        cells = assembled(which)
        packed = chunks[which, 256:264, :]
        lane8 = lax.broadcasted_iota(jnp.int32, (8, LANES), 1)
        for pr in range(4):
            beside = []
            for h in range(2):
                rolled = pltpu.roll(packed, (LANES - 8 - 16 * (2 * pr + h)) % LANES, 1)
                beside.append(jnp.where((lane8 < RF) | (lane8 >= LANES - RF), rolled, 0.0))
            beside = jnp.concatenate(beside, axis=0)
            tiles = [cells[4 * pr + pc] for pc in range(4)]
            at = pl.ds(pl.multiple_of(pr * 128 + which * 16, 16), 16)
            for pc in range(4):
                coadd_ref[at, pc * LANES : (pc + 1) * LANES] = tiles[pc]
            around = [beside, *tiles, beside]
            for pc in range(4):
                hi, lo = split(jnp.concatenate(around[pc : pc + 3], axis=1))
                xbuf[pc * 64 + pr * 16 : pc * 64 + pr * 16 + 16, :] = hi
                xbuf[256 + pc * 64 + pr * 16 : 256 + pc * 64 + pr * 16 + 16, :] = lo
        got = mm(xbuf[0:256, :], col_both)
        got = got[:, 0:LANES] + got[:, LANES:] + mm(xbuf[256:512, :], col_hi)
        for pc in range(4):
            for pr in range(4):
                at = pl.ds(pl.multiple_of(RF + pr * 128 + which * 16, 8), 16)
                ybuf[at, pc * LANES : (pc + 1) * LANES] = got[pc * 64 + pr * 16 : pc * 64 + pr * 16 + 16]

        for pr in range(4):
            at = pl.ds(pl.multiple_of(pr * 128 + which * 16, 16), 16)
            pltpu.make_async_copy(coadd_ref.at[at, :], coadd_hbm.at[at, :], out_sem.at[0]).start()
            at = pl.ds(pl.multiple_of(RF + pr * 128 + which * 16, 8), 16)
            pltpu.make_async_copy(ybuf.at[at, :], rows_hbm.at[at, :], out_sem.at[1]).start()

        for side, number in ((0, 0), (1, NZ - 1)):
            for far in range(2):

                @pl.when(jnp.logical_and(which == number, halo_goes(side, far)))
                def _():
                    halo(side, far).start()

    def passes(way, step, part):
        return step < 3 or (part < 2) == (way == 0)

    @later.append
    def _():
        wait_bytes(others(chunks), ring_send)

    def advance(step, part):
        for way in range(2):
            if passes(way, step - 1, part):
                came(way, step - 1, part)
                if step == 2 and passes(way, 3, part):
                    ring(way, 3, part).start()
                if step < 3:
                    ring(way, step, part).start()

    for part in range(4):
        wait_bytes(chunks.at[z, pl.ds(64 * part, 64), :], ret_recv.at[part])
        ring(0, 0, part).start()
        ring(1, 0, part).start()
    send_sides(assembled(z))
    chunks[z, 256:264, :] = jnp.zeros((8, LANES), F32)
    for side in range(2):

        @pl.when(beside(side))
        def _():
            side_copy(1 - side).wait_recv()
            chunks[z, 256:264, :] += side_in[side]

    ring(0, 0, 4).start()
    ring(1, 0, 4).start()
    for part in range(4):
        advance(1, part)
    filter_chunk(z)
    advance(1, 4)
    for part in range(4):
        advance(2, part)
    filter_chunk(lax.rem(z - 1 + NZ, NZ))
    advance(2, 4)
    filter_chunk(lax.rem(z + 1, NZ))
    filter_chunk(lax.rem(z - 2 + NZ, NZ))
    filter_chunk(lax.rem(z + 2, NZ))
    for part in range(5):
        advance(3, part)
    filter_chunk(lax.rem(z - 3 + NZ, NZ))
    filter_chunk(lax.rem(z + 3, NZ))
    for part in range(5):
        advance(4, part)
    filter_chunk(lax.rem(z + 4, NZ))

    for side in range(2):
        there = y > 0 if side == 0 else y < NY - 1
        at = pl.ds(0 if side == 0 else 512 + RF, RF)

        @pl.when(there)
        def _():
            halo(1 - side, 0).wait_recv()

        @pl.when(jnp.logical_not(there))
        def _():
            ybuf[at, :] = jnp.zeros((RF, 512), F32)

        pltpu.make_async_copy(ybuf.at[at, :], rows_hbm.at[at, :], out_sem.at[1]).start()

    @later.append
    def _():
        for side in range(2):
            for far in range(2):

                @pl.when(halo_goes(side, far))
                def _():
                    halo(side, far).wait_send()

    for left in later:
        left()
    pltpu.make_async_copy(coadd_ref, coadd_hbm, out_sem.at[0]).wait()
    pltpu.make_async_copy(ybuf, rows_hbm, out_sem.at[1]).wait()


def filter_rows(taps_hbm, cells_hbm, rows_hbm, coadd_hbm, det_hbm, taps_ref, rows_ref, cells_ref, det_ref, in_sem, out_sem):
    cells = pltpu.make_async_copy(cells_hbm, cells_ref, in_sem.at[5])
    pieces = []
    for t in range(4):
        at = pl.ds(t * 136, 136 if t < 3 else 120)
        pieces.append(pltpu.make_async_copy(rows_hbm.at[at, :], rows_ref.at[at, :], in_sem.at[t]))
    taps = pltpu.make_async_copy(taps_hbm, taps_ref, in_sem.at[4])
    for copy in (taps, *pieces, cells):
        copy.start()
    taps.wait()
    blocks = filter_blocks(taps_ref, True)
    band = jnp.concatenate([blocks[0][:, LANES - RF :], blocks[1], blocks[2][:, 0:RF]], axis=1)
    hi, lo = split(band)
    pieces[0].wait()
    results = []
    for t in range(4):
        if t < 3:
            pieces[t + 1].wait()
        yh, yl = split(rows_ref[t * 128 : t * 128 + 128 + 2 * RF, :])
        det_ref[t * 128 : (t + 1) * 128, :] = mm(hi, yh) + mm(hi, yl) + mm(lo, yh)
        at = pl.ds(t * 128, 128)
        results.append(pltpu.make_async_copy(det_ref.at[at, :], det_hbm.at[at, :], out_sem.at[t]))
        results[-1].start()
        if t == 1:
            cells.wait()
            results.append(pltpu.make_async_copy(cells_ref, coadd_hbm, out_sem.at[4]))
            results[-1].start()
    for copy in results:
        copy.wait()


def body(stamps, variance, coefficients, band_offsets, shifts, destination, position, psf_taps):
    cells = stamps.reshape(NB, S * S // LANES, LANES).transpose(1, 0, 2).reshape(NB * S * S // LANES, LANES)
    hbm = pl.BlockSpec(memory_space=pl.ANY)
    dma = pltpu.SemaphoreType.DMA
    scratch = [
        pltpu.SMEM((NB, 9), F32),
        pltpu.SMEM((2, NB), jnp.int32),
        pltpu.SMEM((2, NB), F32),
        pltpu.SMEM((NB,), jnp.int32),
        pltpu.SMEM((NB,), jnp.int32),
        pltpu.SMEM((2 * RF + 1,), F32),
        pltpu.VMEM((NB * S * S // LANES, LANES), F32),
        pltpu.VMEM((24, NB, LANES), F32),
        pltpu.VMEM((320, 768), BF),
        pltpu.VMEM((320, 768), BF),
        pltpu.VMEM((LANES, 12 * LANES), BF),
        pltpu.VMEM((LANES, 12 * LANES), BF),
        pltpu.VMEM((12 * LANES, 2 * LANES), BF),
        pltpu.VMEM((NB * LANES, LANES), F32),
        pltpu.VMEM((NZ, NB, LANES), F32),
        pltpu.VMEM((NZ, NB, 16, LANES), F32),
        pltpu.VMEM((2, NZ, 64, LANES), F32),
        pltpu.VMEM((NPLANE, 8, LANES), F32),
        pltpu.VMEM((16, NZ, NB, LANES), F32),
        pltpu.VMEM((2, 16, 32, LANES), F32),
        pltpu.VMEM((2, 16, 32, LANES), F32),
        pltpu.VMEM((NPLANE, 32, LANES), F32),
        pltpu.VMEM((NPLANE, 32, LANES), F32),
        pltpu.VMEM((2, TILES, NPLANE * 32), BF),
        pltpu.VMEM((NPLANE * 32, 2 * LANES), BF),
        pltpu.VMEM((TILES, LANES), F32),
        pltpu.VMEM((NPLANE, 8, LANES), F32),
        pltpu.VMEM((2, 8, LANES), F32),
        pltpu.VMEM((2, 8, LANES), F32),
        pltpu.VMEM((NZ, CHUNK, LANES), F32),
        pltpu.VMEM((512, 3 * LANES), BF),
        pltpu.VMEM((512 + 2 * RF, 512), F32),
        pltpu.VMEM((512, 512), F32),
        pltpu.SemaphoreType.REGULAR, dma((6,)), dma((2,)),
        dma, dma, dma, dma, dma, dma((2,)),
        dma, dma, dma((2,)), dma((2,)), dma((2,)), dma((2,)),
        dma, dma((4,)), dma, dma((35,)), dma((2, 2)), dma((2,)), dma((2,)),
    ]
    coadd, rows = pl.pallas_call(
        kernel,
        out_shape=(jax.ShapeDtypeStruct((512, 512), F32), jax.ShapeDtypeStruct((512 + 2 * RF, 512), F32)),
        in_specs=[hbm] * 8,
        out_specs=(hbm, hbm),
        scratch_shapes=scratch,
        compiler_params=pltpu.CompilerParams(
            collective_id=0, has_side_effects=True, vmem_limit_bytes=60 * 1024 * 1024),
    )(cells, variance, coefficients, band_offsets.T, shifts.T, destination, position, psf_taps)
    return pl.pallas_call(
        filter_rows,
        out_shape=(jax.ShapeDtypeStruct((512, 512), F32), jax.ShapeDtypeStruct((512, 512), F32)),
        in_specs=[hbm, hbm, hbm],
        out_specs=(hbm, hbm),
        scratch_shapes=[
            pltpu.SMEM((2 * RF + 1,), F32), pltpu.VMEM((512 + 2 * RF, 512), F32), pltpu.VMEM((512, 512), F32),
            pltpu.VMEM((512, 512), F32), dma((6,)), dma((5,))],
        compiler_params=pltpu.CompilerParams(vmem_limit_bytes=60 * 1024 * 1024),
    )(psf_taps, coadd, rows)


def solution(mesh):
    placed = (
        P(("visit", "prow", "pcol"), None),
        P(("visit", "prow", "pcol"), None, None),
        P(("visit", "prow", "pcol"), None),
        P(("visit", "prow", "pcol"), None),
        P(("visit", "prow", "pcol"), None),
        P(("visit", "prow", "pcol")),
        P(("visit", "prow", "pcol")),
        P(),
    )
    return jax.shard_map(
        body,
        mesh=mesh,
        in_specs=placed,
        out_specs=(P("prow", "pcol"), P("prow", "pcol")),
        check_vma=False,
    )
```

```python
import math

import jax
import jax.numpy as jnp
from jax import lax
from jax.experimental import pallas as pl
from jax.experimental.pallas import tpu as pltpu
from jax.sharding import PartitionSpec as P

MESH = pl.DeviceIdType.MESH
NB = 8
S = 192
B = 128
KR = 15
RF = 8
NZ = 8
NY = 4
NP = 8
NPLANE = NY * NP
TILES = 512
LANES = 128
WIDTHS = (1.0, 2.0, 4.0)
TAPS = (-2, -1, 0, 1, 2, 3)
CHUNK = 264
PARTS = ((0, 64), (64, 64), (128, 64), (192, 64), (256, 8))
HALF = 64
BOTH_WAYS = (1, 7, 2, 6, 3, 5, 4)
BF = jnp.bfloat16
F32 = jnp.float32


def norms(width):
    lags = range(-KR, KR + 1)
    bell = math.sqrt(sum(math.exp(-((t / width) ** 2)) for t in lags))
    quad = math.sqrt(sum((t / width) ** 4 * math.exp(-((t / width) ** 2)) for t in lags))
    return bell, quad


def split(x):
    hi = x.astype(BF)
    return hi, (x - hi.astype(F32)).astype(BF)


def mm(a, b):
    return jnp.dot(a, b, preferred_element_type=F32)


def sinc(x):
    scaled = math.pi * x
    return jnp.where(x == 0.0, 1.0, jnp.sin(scaled) / jnp.where(x == 0.0, 1.0, scaled))


def lanczos_weights(shift):
    lane = lax.broadcasted_iota(jnp.int32, (NB, LANES), 1).astype(F32)
    x = lane + float(TAPS[0]) - shift
    return jnp.where(jnp.abs(x) < 3.0, sinc(x) * sinc(x / 3.0), 0.0)


def factor_rows(place, weights):
    bells = [jnp.zeros((NB, LANES), F32) for _ in WIDTHS]
    quads = [jnp.zeros((NB, LANES), F32) for _ in WIDTHS]
    for index, tap in enumerate(TAPS):
        lag = place - float(tap + KR)
        weight = jnp.where(jnp.abs(lag) <= float(KR), weights[:, index : index + 1], 0.0)
        for w, width in enumerate(WIDTHS):
            bell_norm, quad_norm = norms(width)
            ratio = lag * (1.0 / width)
            term = weight * jnp.exp(-0.5 * ratio * ratio)
            bells[w] = bells[w] + term * (1.0 / bell_norm)
            quads[w] = quads[w] + ratio * ratio * term * (1.0 / quad_norm)
    return bells, quads


def make_bases(coef_ref, off_ref, shift_ref, base_ref):
    row = lax.broadcasted_iota(jnp.int32, (NB, LANES), 0)

    def column(read):
        result = jnp.zeros((NB, LANES), F32)
        for b in range(NB):
            result = jnp.where(row == b, read(b).astype(F32), result)
        return result

    lane_int = lax.broadcasted_iota(jnp.int32, (NB, LANES), 1)
    lane = lane_int.astype(F32)
    col_weights = lanczos_weights(column(lambda b: shift_ref[1, b]))
    row_weights = lanczos_weights(column(lambda b: shift_ref[0, b]))
    place = jnp.where(lane_int == 0, 0.0, float(LANES) - lane)
    row_offset = column(lambda b: off_ref[0, b])
    bells, quads = factor_rows(place - column(lambda b: off_ref[1, b]), col_weights)
    for w in range(3):
        base_ref[2 * w] = bells[w]
        base_ref[2 * w + 1] = quads[w]
    coefs = [column(lambda b, i=i: coef_ref[b, i]) for i in range(9)]
    for d, delta in enumerate((0.0, -1.0, 1.0)):
        bells, quads = factor_rows(2.0 * lane + delta - row_offset, row_weights)
        for w in range(3):
            first, second, third = coefs[3 * w : 3 * w + 3]
            base_ref[6 + 6 * d + 2 * w] = first * bells[w] + second * quads[w]
            base_ref[6 + 6 * d + 2 * w + 1] = third * bells[w]


def skew(row, count):
    return pltpu.roll(jnp.broadcast_to(row, (count, LANES)), 0, 1, stride=1, stride_axis=0)


def warp_block(k, stamps_ref, base_ref, mh, ml, lh, ll, zb, flux_ref):
    r_iota = lax.broadcasted_iota(jnp.int32, (LANES, LANES), 0)
    c_iota = lax.broadcasted_iota(jnp.int32, (LANES, LANES), 1)
    lower = r_iota >= c_iota
    for j in range(6):
        cols = slice(j * LANES, (j + 1) * LANES)
        full = skew(base_ref[j, pl.ds(k, 1), :], LANES)
        hi, lo = split(jnp.where(lower, full, 0.0))
        mh[64:192, cols] = hi
        ml[64:192, cols] = lo
        hi, lo = split(jnp.where(lower[0:64], 0.0, full[0:64]))
        mh[192:256, cols] = hi
        ml[192:256, cols] = lo
        for d, spots in enumerate((((0, 0), (1, 1)), ((1, 0),), ((0, 1),))):
            hi, lo = split(skew(base_ref[6 + 6 * d + j, pl.ds(k, 1), :], 64))
            for e, f in spots:
                at = (f * 6 + j) * LANES
                lh[e * 64 : (e + 1) * 64, at : at + LANES] = hi
                ll[e * 64 : (e + 1) * 64, at : at + LANES] = lo
    rows_a = stamps_ref[pl.ds(k, 96, 24), :]
    rows_b = stamps_ref[pl.ds(8 + k, 96, 24), :]
    rows_c = stamps_ref[pl.ds(16 + k, 96, 24), :]
    for f, (left, right, start) in enumerate(((rows_a, rows_b, 64), (rows_b, rows_c, 0))):
        xh, xl = split(jnp.concatenate([left, right], axis=1))
        z = mm(xh, mh[start : start + 256, :]) + mm(xl, mh[start : start + 256, :])
        z = z + mm(xh, ml[start : start + 256, :])
        zh, zl = split(z)
        for j in range(6):
            at = (f * 6 + j) * LANES
            zb[at : at + 96, 0:LANES] = zh[:, j * LANES : (j + 1) * LANES]
            zb[at : at + 96, LANES : 2 * LANES] = zl[:, j * LANES : (j + 1) * LANES]
    both = mm(lh[...], zb[...])
    out = both[:, 0:LANES] + both[:, LANES:] + mm(ll[...], zb[:, 0:LANES])
    flux_ref[pl.ds(k, 128, 8), :] = out


def filter_blocks(taps_ref, transposed):
    r_iota = lax.broadcasted_iota(jnp.int32, (LANES, LANES), 0)
    c_iota = lax.broadcasted_iota(jnp.int32, (LANES, LANES), 1)
    lag = c_iota - r_iota if transposed else r_iota - c_iota
    result = []
    for shift in (-LANES, 0, LANES):
        band = jnp.zeros((LANES, LANES), F32)
        for tap in range(2 * RF + 1):
            band = jnp.where(lag + shift == tap - RF, taps_ref[tap], band)
        result.append(band)
    return result


def kernel(
    stamps_hbm, var_ref, coef_hbm, off_hbm, shift_hbm, dest_hbm, pos_hbm, taps_hbm,
    coadd_hbm, rows_hbm,
    coef_ref, off_ref, shift_ref, dest_ref, pos_ref, taps_ref,
    stamps_ref, base_ref, mh, ml, lh, ll, zb, flux_ref,
    ids_z, zw, zf, ids_in, weights, pack_w, pack_f, landed_w, landed_f, onehot, data,
    sums, msg, side_out, side_in, chunks, xbuf, ybuf, coadd_ref,
    seen, small_sem, local_sem, zw_send, zw_recv, zi_send, zi_recv, zf_send, zf_recv,
    id_send, id_recv, in_send, in_recv, side_send, side_recv, ret_send, ret_recv,
    ring_send, ring_recv, halo_send, halo_recv, out_sem,
):
    z = lax.axis_index("visit")
    y = lax.axis_index("prow")
    p = lax.axis_index("pcol")
    j = y * NP + p
    core = lax.rem(p, 2)
    small = [
        pltpu.make_async_copy(far, near, small_sem.at[i])
        for i, (far, near) in enumerate((
            (dest_hbm, dest_ref), (pos_hbm, pos_ref), (off_hbm, off_ref), (shift_hbm, shift_ref),
            (coef_hbm, coef_ref), (taps_hbm, taps_ref)))
    ]
    for copy in small:
        copy.start()
    fetch = pltpu.make_async_copy(stamps_hbm, stamps_ref, local_sem.at[0])
    fetch.start()

    later = []
    barrier = pltpu.get_barrier_semaphore()

    @pl.loop(1, NZ)
    def _(d):
        pl.semaphore_signal(barrier, inc=1, device_id=(lax.rem(z + d, NZ), y, p), device_id_type=MESH)

    @pl.loop(1, NY)
    def _(d):
        pl.semaphore_signal(barrier, inc=1, device_id=(z, lax.rem(y + d, NY), p), device_id_type=MESH)

    @pl.loop(1, NP)
    def _(d):
        pl.semaphore_signal(barrier, inc=1, device_id=(z, y, lax.rem(p + d, NP)), device_id_type=MESH)

    for copy in small:
        copy.wait()
    row_iota = lax.broadcasted_iota(jnp.int32, (NB, LANES), 0)
    ids = jnp.zeros((NB, LANES), F32)
    for b in range(NB):
        ids = jnp.where(row_iota == b, (dest_ref[b] * 16 + pos_ref[b]).astype(F32), ids)
    ids_z[z] = ids
    pl.semaphore_wait(barrier, NZ + NY + NP - 3)

    def z_ids(d):
        return pltpu.make_async_remote_copy(
            src_ref=ids_z.at[z], dst_ref=ids_z.at[z], send_sem=zi_send, recv_sem=zi_recv,
            device_id=(lax.rem(z + d, NZ), y, p), device_id_type=MESH)

    def z_var(d):
        to = lax.rem(z + d, NZ)
        return pltpu.make_async_remote_copy(
            src_ref=var_ref.at[:, pl.ds(pl.multiple_of(to * 16, 16), 16), :], dst_ref=zw.at[z],
            send_sem=zw_send, recv_sem=zw_recv, device_id=(to, y, p), device_id_type=MESH)

    def z_flux(e, d):
        to = lax.rem(z + d, NZ)
        return pltpu.make_async_remote_copy(
            src_ref=flux_ref.at[pl.ds(pl.multiple_of(e * 512 + to * 64, 64), 64), :], dst_ref=zf.at[e, z],
            send_sem=zf_send, recv_sem=zf_recv.at[e], device_id=(to, y, p), device_id_type=MESH)

    def wait_bytes(ref, sem):
        pltpu.make_async_copy(ref, ref, sem).wait()

    def others(buf):
        return buf.at[pl.ds(0, NZ - 1)]

    @pl.loop(1, NZ)
    def _(d):
        z_ids(d).start()

    for d in BOTH_WAYS:
        z_var(d).start()

    @later.append
    def _():
        wait_bytes(others(ids_z), zi_send)
        wait_bytes(others(zw), zw_send)

    own_var = pltpu.make_async_copy(
        var_ref.at[:, pl.ds(pl.multiple_of(z * 16, 16), 16), :], zw.at[z], local_sem.at[1])
    own_var.start()

    @pl.loop(1, NY)
    def _(d):
        pl.semaphore_signal(seen, inc=1, device_id=(z, lax.rem(y + d, NY), p), device_id_type=MESH)

    make_bases(coef_ref, off_ref, shift_ref, base_ref)
    mh[0:64, :] = jnp.zeros((64, 6 * LANES), BF)
    ml[0:64, :] = jnp.zeros((64, 6 * LANES), BF)
    mh[256:320, :] = jnp.zeros((64, 6 * LANES), BF)
    ml[256:320, :] = jnp.zeros((64, 6 * LANES), BF)
    zb[...] = jnp.zeros(zb.shape, BF)
    fetch.wait()

    @pl.loop(0, NB)
    def _(k):
        warp_block(k, stamps_ref, base_ref, mh, ml, lh, ll, zb, flux_ref)

    pl.semaphore_wait(seen, NY - 1)

    for e in range(2):
        for d in BOTH_WAYS:
            z_flux(e, d).start()

    @later.append
    def _():
        wait_bytes(flux_ref.at[pl.ds(0, 2 * (NZ - 1) * 64), :], zf_send)

    wait_bytes(others(ids_z), zi_recv)
    lane32 = lax.rem(lax.broadcasted_iota(jnp.int32, (32, LANES), 1), 32)
    row32 = lax.broadcasted_iota(jnp.int32, (32, LANES), 0)
    column_ids = ids_z[...].reshape(64, LANES)
    low_ids = jnp.sum(jnp.where(lane32 == row32, column_ids[0:32], 0.0), axis=0, keepdims=True)
    high_ids = jnp.sum(jnp.where(lane32 == row32, column_ids[32:64], 0.0), axis=0, keepdims=True)
    ids_in[j] = jnp.where(lax.broadcasted_iota(jnp.int32, (8, LANES), 0) == 0, low_ids, high_ids)

    def in_ids(d):
        other = lax.rem(j + d, NPLANE)
        return pltpu.make_async_remote_copy(
            src_ref=ids_in.at[j], dst_ref=ids_in.at[j], send_sem=id_send, recv_sem=id_recv,
            device_id=(z, other // NP, lax.rem(other, NP)), device_id_type=MESH)

    @pl.loop(1, NPLANE)
    def _(d):
        in_ids(d).start()

    @later.append
    def _():
        wait_bytes(ids_in.at[pl.ds(0, NPLANE - 1)], id_send)

    def in_copy(kind, e, chip):
        buf, land = ((pack_f, landed_f), (pack_w, landed_w))[kind]
        other = 2 * chip + e
        return pltpu.make_async_remote_copy(
            src_ref=buf.at[e, chip], dst_ref=land.at[j], send_sem=in_send.at[kind],
            recv_sem=in_recv.at[kind], device_id=(z, other // NP, lax.rem(other, NP)), device_id_type=MESH)

    @later.append
    def _():
        wait_bytes(landed_f.at[pl.ds(0, NPLANE - 1)], in_send.at[0])
        wait_bytes(landed_w.at[pl.ds(0, NPLANE - 1)], in_send.at[1])

    def send_rows(kind, e):
        buf, land = ((pack_f, landed_f), (pack_w, landed_w))[kind]

        @pl.loop(0, 16)
        def _(d):
            chip = lax.rem(j // 2 + d, 16)
            here = 2 * chip + e == j

            @pl.when(here)
            def _():
                pltpu.make_async_copy(buf.at[e, chip], land.at[j], in_recv.at[kind]).start()

            @pl.when(jnp.logical_not(here))
            def _():
                in_copy(kind, e, chip).start()

    def wait_rows(kind):
        wait_bytes((landed_f, landed_w)[kind], in_recv.at[kind])

    first64 = lax.broadcasted_iota(jnp.int32, (8, LANES), 1) < HALF

    def swap(x):
        return pltpu.roll(x, HALF, 1)

    def pack(buf, e, q, at, low, high):
        buf[e, 2 * q, at, :] = jnp.where(first64, low, swap(high))
        buf[e, 2 * q + 1, at, :] = jnp.where(first64, swap(low), high)

    wait_bytes(others(zw), zw_recv)
    own_var.wait()
    for s in range(4):
        low = 1.0 / jnp.swapaxes(zw[s], 0, 1)
        high = 1.0 / jnp.swapaxes(zw[s + 4], 0, 1)
        for row in range(16):
            weights[row, s] = low[row]
            weights[row, s + 4] = high[row]
            pack(pack_w, row % 2, row // 2, slice(8 * s, 8 * s + 8), low[row], high[row])
    send_rows(1, 0)
    send_rows(1, 1)

    wait_bytes(ids_in.at[pl.ds(0, NPLANE - 1)], id_recv)

    @pl.loop(0, 8)
    def _(group):
        quarter = lax.broadcasted_iota(jnp.int32, (8, LANES), 1) // 32
        mixed = ids_in[4 * group]
        for i in range(1, 4):
            mixed = jnp.where(quarter == i, ids_in[4 * group + i], mixed)
        tile = lax.broadcasted_iota(jnp.int32, (TILES, LANES), 0).astype(F32)
        at = pl.ds(pl.multiple_of(group * LANES, LANES), LANES)
        for h in range(2):
            onehot[h, :, at] = jnp.where(tile == mixed[h : h + 1], 1.0, 0.0).astype(BF)

    def tile_sums(land):
        hi, lo = split(land[...].reshape(NPLANE * 32, LANES))
        data[:, 0:LANES] = hi
        data[:, LANES:] = lo
        low = mm(onehot[0], data[...])
        high = mm(onehot[1], data[...])
        return low[:, 0:LANES] + low[:, LANES:] + pltpu.roll(high[:, 0:LANES] + high[:, LANES:], HALF, 1)

    col_blocks = jnp.concatenate(filter_blocks(taps_ref, False), axis=0)
    col_hi, col_lo = split(col_blocks)
    col_both = jnp.concatenate([col_hi, col_lo], axis=1)

    def relay(e):
        wait_bytes(others(zf.at[e]), zf_recv.at[e])
        zf[e, z] = flux_ref[pl.ds(pl.multiple_of(e * 512 + z * 64, 64), 64), :]
        for s in range(4):
            for q in range(8):
                row = 2 * q + e
                low = zf[e, s, 8 * q : 8 * q + 8, :] * weights[row, s]
                high = zf[e, s + 4, 8 * q : 8 * q + 8, :] * weights[row, s + 4]
                pack(pack_f, e, q, slice(8 * s, 8 * s + 8), low, high)
        send_rows(0, e)

    relay(0)
    relay(1)
    wait_rows(1)
    sums[...] = 1.0 / (1.0 + tile_sums(landed_w))
    wait_rows(0)
    cells = (tile_sums(landed_f) * sums[...]).reshape(NPLANE, 2, 8, LANES)
    for o in range(NPLANE):
        msg[o] = jnp.where(first64, cells[o, 0], swap(cells[o, 1]))

    def ret_copy(o):
        return pltpu.make_async_remote_copy(
            src_ref=msg.at[o], dst_ref=chunks.at[z, pl.ds(pl.multiple_of(8 * j, 8), 8), :],
            send_sem=ret_send, recv_sem=ret_recv.at[y],
            device_id=(z, o // NP, lax.rem(o, NP)), device_id_type=MESH)

    pltpu.make_async_copy(
        msg.at[j], chunks.at[z, pl.ds(pl.multiple_of(8 * j, 8), 8), :], ret_recv.at[y]).start()

    @pl.loop(1, NPLANE)
    def _(d):
        ret_copy(lax.rem(j + d, NPLANE)).start()

    @later.append
    def _():
        wait_bytes(msg.at[pl.ds(0, NPLANE - 1)], ret_send)

    def assembled(which):
        cell_rows = []
        for row in range(16):
            e, q = row % 2, row // 2
            one = chunks[which, 8 * (4 * q + e) : 8 * (4 * q + e) + 8, :]
            two = chunks[which, 8 * (4 * q + 2 + e) : 8 * (4 * q + 2 + e) + 8, :]
            cell_rows.append(jnp.concatenate(
                [jnp.where(first64, one, swap(two)), jnp.where(first64, swap(one), two)], axis=0)[None])
        return jnp.swapaxes(jnp.concatenate(cell_rows, axis=0), 0, 1)

    def side_copy(side):
        return pltpu.make_async_remote_copy(
            src_ref=side_out.at[side], dst_ref=side_in.at[1 - side], send_sem=side_send.at[side],
            recv_sem=side_recv.at[1 - side], device_id=(z, y, p - 1 + 2 * side), device_id_type=MESH)

    def beside(side):
        return p > 0 if side == 0 else p < NP - 1

    def send_sides(got):
        lane8 = lax.broadcasted_iota(jnp.int32, (8, LANES), 1)
        to_left = jnp.zeros((8, LANES), F32)
        to_right = jnp.zeros((8, LANES), F32)
        for g in range(8):
            rows = slice(8 * (g % 2), 8 * (g % 2) + 8)
            at = (8 + 16 * g) % LANES
            to_left = to_left + pltpu.roll(jnp.where(lane8 < RF, got[4 * (g // 2), rows, :], 0.0), at, 1)
            to_right = to_right + pltpu.roll(
                jnp.where(lane8 >= LANES - RF, got[4 * (g // 2) + 3, rows, :], 0.0), at, 1)
        side_out[0] = to_left
        side_out[1] = to_right
        for side in range(2):

            @pl.when(beside(side))
            def _():
                side_copy(side).start()

    @later.append
    def _():
        for side in range(2):

            @pl.when(beside(side))
            def _():
                side_copy(side).wait_send()


    def ring_slot(way, step, part):
        return (3 * way + step) * 5 + part if step < 3 else 30 + part

    def ring(way, step, part):
        back, hop = (step, 1) if step < 3 else (2, 2)
        which = lax.rem(z - back + NZ, NZ) if way == 0 else lax.rem(z + back, NZ)
        to = lax.rem(z + hop, NZ) if way == 0 else lax.rem(z + NZ - hop, NZ)
        at, size = PARTS[part]
        ref = chunks.at[which, pl.ds(at, size), :]
        return pltpu.make_async_remote_copy(
            src_ref=ref, dst_ref=ref, send_sem=ring_send,
            recv_sem=ring_recv.at[ring_slot(way, step, part)], device_id=(to, y, p), device_id_type=MESH)

    def came(way, step, part):
        which = lax.rem(z - step - 1 + NZ, NZ) if way == 0 else lax.rem(z + step + 1, NZ)
        at, size = PARTS[part]
        ref = chunks.at[which, pl.ds(at, size), :]
        pltpu.make_async_copy(ref, ref, ring_recv.at[ring_slot(way, step, part)]).wait()

    def halo(side, far):
        mine, theirs = (RF, 512 + RF) if side == 0 else (512, 0)
        return pltpu.make_async_remote_copy(
            src_ref=ybuf.at[pl.ds(mine, RF), :], dst_ref=ybuf.at[pl.ds(theirs, RF), :],
            send_sem=halo_send.at[side, far], recv_sem=halo_recv.at[1 - side],
            device_id=(lax.rem(z + 4 * far, NZ), y - 1 + 2 * side, p), device_id_type=MESH)

    def halo_goes(side, far):
        there = y > 0 if side == 0 else y < NY - 1
        first = 0 if side == 0 else NZ - 1
        return jnp.logical_and(there, z == first if far else z != (first + 4) % NZ)

    def filter_chunk(which):
        cells = assembled(which)
        packed = chunks[which, 256:264, :]
        lane8 = lax.broadcasted_iota(jnp.int32, (8, LANES), 1)
        for pr in range(4):
            beside = []
            for h in range(2):
                rolled = pltpu.roll(packed, (LANES - 8 - 16 * (2 * pr + h)) % LANES, 1)
                beside.append(jnp.where((lane8 < RF) | (lane8 >= LANES - RF), rolled, 0.0))
            beside = jnp.concatenate(beside, axis=0)
            tiles = [cells[4 * pr + pc] for pc in range(4)]
            at = pl.ds(pl.multiple_of(pr * 128 + which * 16, 16), 16)
            for pc in range(4):
                coadd_ref[at, pc * LANES : (pc + 1) * LANES] = tiles[pc]
            around = [beside, *tiles, beside]
            for pc in range(4):
                hi, lo = split(jnp.concatenate(around[pc : pc + 3], axis=1))
                xbuf[pc * 64 + pr * 16 : pc * 64 + pr * 16 + 16, :] = hi
                xbuf[256 + pc * 64 + pr * 16 : 256 + pc * 64 + pr * 16 + 16, :] = lo
        got = mm(xbuf[0:256, :], col_both)
        got = got[:, 0:LANES] + got[:, LANES:] + mm(xbuf[256:512, :], col_hi)
        for pc in range(4):
            for pr in range(4):
                at = pl.ds(pl.multiple_of(RF + pr * 128 + which * 16, 8), 16)
                ybuf[at, pc * LANES : (pc + 1) * LANES] = got[pc * 64 + pr * 16 : pc * 64 + pr * 16 + 16]

        for pr in range(4):
            at = pl.ds(pl.multiple_of(pr * 128 + which * 16, 16), 16)
            pltpu.make_async_copy(coadd_ref.at[at, :], coadd_hbm.at[at, :], out_sem.at[0]).start()
            at = pl.ds(pl.multiple_of(RF + pr * 128 + which * 16, 8), 16)
            pltpu.make_async_copy(ybuf.at[at, :], rows_hbm.at[at, :], out_sem.at[1]).start()

        for side, number in ((0, 0), (1, NZ - 1)):
            for far in range(2):

                @pl.when(jnp.logical_and(which == number, halo_goes(side, far)))
                def _():
                    halo(side, far).start()

    def passes(way, step, part):
        return step < 3 or (part < 2) == (way == 0)

    @later.append
    def _():
        wait_bytes(others(chunks), ring_send)

    def advance(step, part):
        for way in range(2):
            if passes(way, step - 1, part):
                came(way, step - 1, part)
                if step == 2 and passes(way, 3, part):
                    ring(way, 3, part).start()
                if step < 3:
                    ring(way, step, part).start()

    for part in range(4):
        wait_bytes(chunks.at[z, pl.ds(64 * part, 64), :], ret_recv.at[part])
        ring(0, 0, part).start()
        ring(1, 0, part).start()
    send_sides(assembled(z))
    chunks[z, 256:264, :] = jnp.zeros((8, LANES), F32)
    for side in range(2):

        @pl.when(beside(side))
        def _():
            side_copy(1 - side).wait_recv()
            chunks[z, 256:264, :] += side_in[side]

    ring(0, 0, 4).start()
    ring(1, 0, 4).start()
    for part in range(4):
        advance(1, part)
    filter_chunk(z)
    advance(1, 4)
    for part in range(4):
        advance(2, part)
    filter_chunk(lax.rem(z - 1 + NZ, NZ))
    advance(2, 4)
    filter_chunk(lax.rem(z + 1, NZ))
    filter_chunk(lax.rem(z - 2 + NZ, NZ))
    filter_chunk(lax.rem(z + 2, NZ))
    for part in range(5):
        advance(3, part)
    filter_chunk(lax.rem(z - 3 + NZ, NZ))
    filter_chunk(lax.rem(z + 3, NZ))
    for part in range(5):
        advance(4, part)
    filter_chunk(lax.rem(z + 4, NZ))

    for side in range(2):
        there = y > 0 if side == 0 else y < NY - 1
        at = pl.ds(0 if side == 0 else 512 + RF, RF)

        @pl.when(there)
        def _():
            halo(1 - side, 0).wait_recv()

        @pl.when(jnp.logical_not(there))
        def _():
            ybuf[at, :] = jnp.zeros((RF, 512), F32)

        pltpu.make_async_copy(ybuf.at[at, :], rows_hbm.at[at, :], out_sem.at[1]).start()

    @later.append
    def _():
        for side in range(2):
            for far in range(2):

                @pl.when(halo_goes(side, far))
                def _():
                    halo(side, far).wait_send()

    for left in later:
        left()
    pltpu.make_async_copy(coadd_ref, coadd_hbm, out_sem.at[0]).wait()
    pltpu.make_async_copy(ybuf, rows_hbm, out_sem.at[1]).wait()


def filter_rows(taps_hbm, cells_hbm, rows_hbm, coadd_hbm, det_hbm, taps_ref, rows_ref, cells_ref, det_ref, in_sem, out_sem):
    cells = pltpu.make_async_copy(cells_hbm, cells_ref, in_sem.at[5])
    pieces = []
    for t in range(4):
        at = pl.ds(t * 136, 136 if t < 3 else 120)
        pieces.append(pltpu.make_async_copy(rows_hbm.at[at, :], rows_ref.at[at, :], in_sem.at[t]))
    taps = pltpu.make_async_copy(taps_hbm, taps_ref, in_sem.at[4])
    for copy in (taps, *pieces, cells):
        copy.start()
    taps.wait()
    blocks = filter_blocks(taps_ref, True)
    band = jnp.concatenate([blocks[0][:, LANES - RF :], blocks[1], blocks[2][:, 0:RF]], axis=1)
    hi, lo = split(band)
    pieces[0].wait()
    results = []
    for t in range(4):
        if t < 3:
            pieces[t + 1].wait()
        yh, yl = split(rows_ref[t * 128 : t * 128 + 128 + 2 * RF, :])
        det_ref[t * 128 : (t + 1) * 128, :] = mm(hi, yh) + mm(hi, yl) + mm(lo, yh)
        at = pl.ds(t * 128, 128)
        results.append(pltpu.make_async_copy(det_ref.at[at, :], det_hbm.at[at, :], out_sem.at[t]))
        results[-1].start()
        if t == 1:
            cells.wait()
            results.append(pltpu.make_async_copy(cells_ref, coadd_hbm, out_sem.at[4]))
            results[-1].start()
    for copy in results:
        copy.wait()


def body(stamps, variance, coefficients, band_offsets, shifts, destination, position, psf_taps):
    cells = stamps.reshape(NB, S * S // LANES, LANES).transpose(1, 0, 2).reshape(NB * S * S // LANES, LANES)
    hbm = pl.BlockSpec(memory_space=pl.ANY)
    dma = pltpu.SemaphoreType.DMA
    scratch = [
        pltpu.SMEM((NB, 9), F32),
        pltpu.SMEM((2, NB), jnp.int32),
        pltpu.SMEM((2, NB), F32),
        pltpu.SMEM((NB,), jnp.int32),
        pltpu.SMEM((NB,), jnp.int32),
        pltpu.SMEM((2 * RF + 1,), F32),
        pltpu.VMEM((NB * S * S // LANES, LANES), F32),
        pltpu.VMEM((24, NB, LANES), F32),
        pltpu.VMEM((320, 768), BF),
        pltpu.VMEM((320, 768), BF),
        pltpu.VMEM((LANES, 12 * LANES), BF),
        pltpu.VMEM((LANES, 12 * LANES), BF),
        pltpu.VMEM((12 * LANES, 2 * LANES), BF),
        pltpu.VMEM((NB * LANES, LANES), F32),
        pltpu.VMEM((NZ, NB, LANES), F32),
        pltpu.VMEM((NZ, NB, 16, LANES), F32),
        pltpu.VMEM((2, NZ, 64, LANES), F32),
        pltpu.VMEM((NPLANE, 8, LANES), F32),
        pltpu.VMEM((16, NZ, NB, LANES), F32),
        pltpu.VMEM((2, 16, 32, LANES), F32),
        pltpu.VMEM((2, 16, 32, LANES), F32),
        pltpu.VMEM((NPLANE, 32, LANES), F32),
        pltpu.VMEM((NPLANE, 32, LANES), F32),
        pltpu.VMEM((2, TILES, NPLANE * 32), BF),
        pltpu.VMEM((NPLANE * 32, 2 * LANES), BF),
        pltpu.VMEM((TILES, LANES), F32),
        pltpu.VMEM((NPLANE, 8, LANES), F32),
        pltpu.VMEM((2, 8, LANES), F32),
        pltpu.VMEM((2, 8, LANES), F32),
        pltpu.VMEM((NZ, CHUNK, LANES), F32),
        pltpu.VMEM((512, 3 * LANES), BF),
        pltpu.VMEM((512 + 2 * RF, 512), F32),
        pltpu.VMEM((512, 512), F32),
        pltpu.SemaphoreType.REGULAR, dma((6,)), dma((2,)),
        dma, dma, dma, dma, dma, dma((2,)),
        dma, dma, dma((2,)), dma((2,)), dma((2,)), dma((2,)),
        dma, dma((4,)), dma, dma((35,)), dma((2, 2)), dma((2,)), dma((2,)),
    ]
    coadd, rows = pl.pallas_call(
        kernel,
        out_shape=(jax.ShapeDtypeStruct((512, 512), F32), jax.ShapeDtypeStruct((512 + 2 * RF, 512), F32)),
        in_specs=[hbm] * 8,
        out_specs=(hbm, hbm),
        scratch_shapes=scratch,
        compiler_params=pltpu.CompilerParams(
            collective_id=0, has_side_effects=True, vmem_limit_bytes=60 * 1024 * 1024),
    )(cells, variance, coefficients, band_offsets.T, shifts.T, destination, position, psf_taps)
    return pl.pallas_call(
        filter_rows,
        out_shape=(jax.ShapeDtypeStruct((512, 512), F32), jax.ShapeDtypeStruct((512, 512), F32)),
        in_specs=[hbm, hbm, hbm],
        out_specs=(hbm, hbm),
        scratch_shapes=[
            pltpu.SMEM((2 * RF + 1,), F32), pltpu.VMEM((512 + 2 * RF, 512), F32), pltpu.VMEM((512, 512), F32),
            pltpu.VMEM((512, 512), F32), dma((6,)), dma((5,))],
        compiler_params=pltpu.CompilerParams(vmem_limit_bytes=60 * 1024 * 1024),
    )(psf_taps, coadd, rows)


def solution(mesh):
    placed = (
        P(("visit", "prow", "pcol"), None),
        P(("visit", "prow", "pcol"), None, None),
        P(("visit", "prow", "pcol"), None),
        P(("visit", "prow", "pcol"), None),
        P(("visit", "prow", "pcol"), None),
        P(("visit", "prow", "pcol")),
        P(("visit", "prow", "pcol")),
        P(),
    )
    return jax.shard_map(
        body,
        mesh=mesh,
        in_specs=placed,
        out_specs=(P("prow", "pcol"), P("prow", "pcol")),
        check_vma=False,
    )
```
